32 devices in a mesh: dp: 2 (over x), frame: 8 (over z, core), tile: 2 (over y).
Axes of the slice: x: 2, y: 2, z: 4, core: 2. Of those that a mesh axis runs over, the one named last changes fastest.
Arguments:
- clip_input: bfloat16 [2, 8, 18, 32, 640], P('dp', 'frame', 'tile'), may hold values from -36 to 36
- cotangent: bfloat16 [2, 8, 18, 32, 640], P('dp', 'frame', 'tile'), may hold values from -6 to 6
- norm_gain: float32 [640], replicated, may hold values from 0.25 to 1.75
- conv_weight: bfloat16 [9, 640, 640], P(None, ('frame', 'tile')), may hold values from -0.078125 to 0.078125
- attn_weight: bfloat16 [640, 2560], P(('frame', 'tile')), may hold values from -0.25 to 0.25
- query_gain: float32 [64], replicated, may hold values from 0.5 to 1.5
- key_gain: float32 [64], replicated, may hold values from 0.5 to 1.5
- logit_scale: float32 [10], replicated, may hold values from 0.5 to 4
Outputs:
- mid_grad: bfloat16 [2, 8, 18, 32, 640], P('dp', 'frame', 'tile')
- value_grad: float32 [640, 640], P(('frame', 'tile'))
- out_proj_grad: float32 [640, 640], P(('frame', 'tile'))
- query_gain_grad: float32 [64], replicated
- key_gain_grad: float32 [64], replicated
- scale_grad: float32 [10], replicated
The draws below stay inside these ranges and needn't reach their ends.
All inputs are finite; a program needn't handle non-finite values.
Results may differ from the reference program's by a relative error of at most 0.013.
The reference program's roundings to bfloat16 on the way count: a program that leaves them out, or rounds other values in their place, can miss the bound.
Values may be sent and summed in bfloat16 or wider, within the bound.
No kernel may reach another device: no remote copies, remote signals or barrier semaphores. Data moves between devices by JAX's collectives and lax.ppermute only.
A program may use at most 128 MiB of HBM per device.

```python
import math
import jax
import jax.numpy as jnp
from jax import lax

C = 640
HEADS = 10
DH = 64
GROUPS = 32
H = 18
W = 32
FRAMES = 8
CLIPS = 2
TOKENS = 9216


def draw_clip_input(key, part):
    key_base, key_rows, key_chan = jax.random.split(jax.random.fold_in(key, 7), 3)
    shape = (CLIPS, FRAMES, H, W, C)
    base = jnp.clip(jax.random.normal(key_base, shape, jnp.float32), -4.0, 4.0)
    rise = jnp.exp(math.log(3.0) * jnp.arange(H, dtype=jnp.float32) / max(H - 1, 1))
    rough = jnp.exp(math.log(10.0) * jax.random.uniform(key_rows, (CLIPS, FRAMES, H, 1, 1), jnp.float32))
    chan = jnp.exp(jax.random.uniform(key_chan, (C,), jnp.float32, math.log(0.3), math.log(3.0)))
    return (base * 0.1 * rise[None, None, :, None, None] * rough * chan).astype(jnp.bfloat16)


def steps_of(key, extent, shards, least, high):
    loudness, own = 1.0, jax.random.fold_in(key, 6)
    for dim, blocks in shards:
        draws = jnp.exp(jax.random.uniform(jax.random.fold_in(own, dim), (blocks,), jnp.float32, least / len(shards), high / len(shards)))
        loudness = loudness * jnp.repeat(draws, extent[dim] // blocks).reshape([-1 if axis == dim else 1 for axis in range(len(extent))])
    return loudness


def centred(rng, dims, scale, limit, cuts=(), held_as=jnp.bfloat16):
    array = jax.random.normal(rng, dims, jnp.float32) * scale
    if len(cuts) > 0:
        array = steps_of(rng, dims, cuts, -0.22, 0.18) * array
    return jnp.clip(array, min=-limit, max=limit).astype(held_as)


def setup_inputs(seed: int = 0) -> dict:
    streams_of = jax.random.split(jax.random.key(seed), 9)
    clip_input = draw_clip_input(jax.random.fold_in(streams_of[8], 71), 0)
    cotangent = centred(streams_of[1], (CLIPS, FRAMES, H, W, C), 1.0, 6.0, ((0, 2), (1, 8), (2, 2)))
    norm_gain = jnp.clip(1.0 + 0.15 * jax.random.normal(streams_of[2], (C,), jnp.float32), 0.25, 1.75)
    conv_weight = centred(streams_of[3], (9, C, C), (9 * C) ** -0.5, 0.078125, ((1, 16),))
    attn_weight = centred(streams_of[4], (C, 4 * C), C ** -0.5, 0.25, ((0, 16),))
    query_gain = jnp.clip(1.0 + 0.1 * jax.random.normal(streams_of[5], (DH,), jnp.float32), 0.5, 1.5)
    key_gain = jnp.clip(1.0 + 0.1 * jax.random.normal(streams_of[6], (DH,), jnp.float32), 0.5, 1.5)
    logit_scale = jnp.clip(jnp.exp(jax.random.uniform(streams_of[7], (HEADS,), jnp.float32, math.log(0.5), math.log(4.0))), 0.5, 4.0)
    return dict(clip_input=clip_input, cotangent=cotangent, norm_gain=norm_gain, conv_weight=conv_weight, attn_weight=attn_weight, query_gain=query_gain, key_gain=key_gain, logit_scale=logit_scale)


def layer_stats(vec):
    mean = lax.optimization_barrier(jnp.mean(vec, axis=-1, keepdims=True))
    cent = vec - mean
    var = lax.optimization_barrier(jnp.mean(cent * cent, axis=-1, keepdims=True))
    rstd = lax.rsqrt(var + 1e-05)
    return (cent * rstd, rstd)

def layer_back(dhat, hat, rstd):
    first = lax.optimization_barrier(jnp.mean(dhat, axis=-1, keepdims=True))
    second = lax.optimization_barrier(jnp.mean(dhat * hat, axis=-1, keepdims=True))
    return rstd * (dhat - first - hat * second)

def attention_pass(mid, cot, weights, query_gain, key_gain, logit_scale):
    frames, count, width = mid.shape
    heads = logit_scale.shape[0]
    depth = width // heads
    total = frames * count
    high = lax.Precision.HIGHEST
    flat = mid.reshape(total, width)
    proj = jnp.dot(flat, weights[:, :3 * width], preferred_element_type=jnp.float32)
    query = proj[:, :width].reshape(frames, count, heads, depth)
    keyed = proj[:, width:2 * width].reshape(frames, count, heads, depth)
    value = proj[:, 2 * width:].astype(jnp.bfloat16).reshape(frames, count, heads, depth)
    q_hat, q_rstd = layer_stats(query)
    k_hat, k_rstd = layer_stats(keyed)
    q_norm = q_hat * query_gain
    k_norm = k_hat * key_gain
    root = math.sqrt(depth)
    raw = jnp.einsum('fnhd,gnhd->nhfg', q_norm, k_norm, precision=high) / root
    scale = logit_scale[None, :, None, None]
    expo = jnp.exp(raw * scale)
    probs = expo / lax.optimization_barrier(jnp.sum(expo, axis=-1, keepdims=True))
    probs_b = probs.astype(jnp.bfloat16)
    mixed = jnp.einsum('nhfg,gnhd->fnhd', probs_b.astype(jnp.float32), value.astype(jnp.float32), precision=high)
    mixed = mixed.astype(jnp.bfloat16).reshape(total, width)
    cot_flat = cot.reshape(total, width)
    w_out = weights[:, 3 * width:]
    d_mixed = jnp.dot(cot_flat, w_out.T, preferred_element_type=jnp.float32)
    d_mixed = d_mixed.astype(jnp.bfloat16).reshape(frames, count, heads, depth)
    d_probs = jnp.einsum('fnhd,gnhd->nhfg', d_mixed.astype(jnp.float32), value.astype(jnp.float32), precision=high)
    d_value = jnp.einsum('nhfg,fnhd->gnhd', probs_b.astype(jnp.float32), d_mixed.astype(jnp.float32), precision=high)
    d_value = d_value.astype(jnp.bfloat16)
    d_logits = probs * (d_probs - lax.optimization_barrier(jnp.sum(probs * d_probs, axis=-1, keepdims=True)))
    scale_term = lax.optimization_barrier(jnp.sum(d_logits * raw, axis=(0, 2, 3)))
    d_raw = d_logits * scale / root
    d_qn = jnp.einsum('nhfg,gnhd->fnhd', d_raw, k_norm, precision=high)
    d_kn = jnp.einsum('nhfg,fnhd->gnhd', d_raw, q_norm, precision=high)
    qgain_term = lax.optimization_barrier(jnp.sum(d_qn * q_hat, axis=(0, 1, 2)))
    kgain_term = lax.optimization_barrier(jnp.sum(d_kn * k_hat, axis=(0, 1, 2)))
    d_query = layer_back(d_qn * query_gain, q_hat, q_rstd).astype(jnp.bfloat16)
    d_key = layer_back(d_kn * key_gain, k_hat, k_rstd).astype(jnp.bfloat16)
    d_cat = jnp.concatenate([d_query.reshape(total, width), d_key.reshape(total, width), d_value.reshape(total, width)], axis=1)
    d_mid = jnp.dot(d_cat, weights[:, :3 * width].T, preferred_element_type=jnp.float32)
    d_mid = d_mid.astype(jnp.bfloat16).reshape(frames, count, width)
    return (d_mid, mixed, d_value.reshape(total, width), scale_term, qgain_term, kgain_term)

def reference(clip_input, cotangent, norm_gain, conv_weight, attn_weight, query_gain, key_gain, logit_scale):
    width = C
    per_group = width // GROUPS

    def one_clip(pair):
        source, cot = pair
        frames = source.shape[0]
        xf = source.astype(jnp.float32).reshape(frames, H * W, GROUPS, per_group)
        count = H * W * per_group
        mean = lax.optimization_barrier(jnp.sum(xf, axis=(1, 3))) / count
        meansq = lax.optimization_barrier(jnp.sum(xf * xf, axis=(1, 3))) / count
        rstd = lax.rsqrt(meansq - mean * mean + 1e-05)
        normed = (xf - mean[:, None, :, None]) * rstd[:, None, :, None]
        zed = normed.reshape(frames, H, W, width) * norm_gain
        act = jax.nn.silu(zed).astype(jnp.bfloat16)
        padded = jnp.pad(act, ((0, 0), (1, 1), (1, 1), (0, 0)))
        slabs = []
        for row_off in (-1, 0, 1):
            for col_off in (-1, 0, 1):
                slabs.append(padded[:, 1 + row_off:1 + row_off + H, 1 + col_off:1 + col_off + W, :])
        stacked = jnp.concatenate(slabs, axis=-1).reshape(frames * H * W, 9 * width)
        pre = jnp.dot(stacked, conv_weight.reshape(9 * width, width), preferred_element_type=jnp.float32)
        mid = (source.astype(jnp.float32) + pre.reshape(frames, H, W, width)).astype(jnp.bfloat16)
        mid_rows = mid.reshape(frames, H * W, width)
        cot_rows = cot.reshape(frames, H * W, width)
        d_mid, mixed, d_value, scale_term, qgain_term, kgain_term = attention_pass(mid_rows, cot_rows, attn_weight, query_gain, key_gain, logit_scale)
        grad_here = (cot.astype(jnp.float32) + d_mid.reshape(frames, H, W, width).astype(jnp.float32)).astype(jnp.bfloat16)
        flat_mid = mid_rows.reshape(frames * H * W, width)
        flat_cot = cot_rows.reshape(frames * H * W, width)
        vgrad = jnp.dot(flat_mid.T, d_value, preferred_element_type=jnp.float32)
        ograd = jnp.dot(mixed.T, flat_cot, preferred_element_type=jnp.float32)
        return (grad_here, vgrad, ograd, scale_term, qgain_term, kgain_term)
    outs = lax.map(one_clip, (clip_input, cotangent))
    factor = 1.0 / math.sqrt(TOKENS)
    mid_grad = outs[0]
    value_grad = lax.optimization_barrier(jnp.sum(outs[1], axis=0)) * factor
    out_proj_grad = lax.optimization_barrier(jnp.sum(outs[2], axis=0)) * factor
    scale_grad = lax.optimization_barrier(jnp.sum(outs[3], axis=0)) * factor
    query_gain_grad = lax.optimization_barrier(jnp.sum(outs[4], axis=0)) * factor
    key_gain_grad = lax.optimization_barrier(jnp.sum(outs[5], axis=0)) * factor
    return (mid_grad, value_grad, out_proj_grad, query_gain_grad, key_gain_grad, scale_grad)
```

```python
import functools
import math

import jax
import jax.numpy as jnp
from jax import lax
from jax.experimental import pallas as pl
from jax.experimental.pallas import tpu as pltpu
from jax.sharding import PartitionSpec as P

GROUPS = 32
EPS = 1e-05
SLOT = 16
BF = jnp.bfloat16
F32 = jnp.float32
VMEM_BYTES = 48 * 1024 * 1024


def swap(x, axis):
    return lax.ppermute(x, axis, [(i, i ^ 1) for i in range(lax.axis_size(axis))])


def round_up(value, unit):
    return -(-value // unit) * unit


def dot(a, b):
    return lax.dot_general(a, b, (((1,), (0,)), ((), ())), preferred_element_type=F32)


def dot_t(a, b):
    return lax.dot_general(a, b, (((1,), (1,)), ((), ())), preferred_element_type=F32)


def dot_rows(a, b):
    return lax.dot_general(a, b, (((0,), (0,)), ((), ())), preferred_element_type=F32)


def halves(x):
    high = x.astype(BF)
    return high, (x - high.astype(F32)).astype(BF)


def picker(rows, cols, depth, offset):
    row = lax.broadcasted_iota(jnp.int32, (rows, cols), 0)
    col = lax.broadcasted_iota(jnp.int32, (rows, cols), 1)
    return (col - row // depth == offset).astype(F32).astype(BF)


def spreader(rows, cols, depth, offset):
    row = lax.broadcasted_iota(jnp.int32, (rows, cols), 0)
    col = lax.broadcasted_iota(jnp.int32, (rows, cols), 1)
    return (row - col // depth == offset).astype(F32).astype(BF)


def head_sums(x, pick):
    high, low = halves(x)
    return dot(high, pick) + dot(low, pick)


def spread(x, both):
    high, low = halves(x)
    return dot(jnp.concatenate([high, low], axis=1), both)


def conv_kernel(place, mine, other, weights, out, padded, *, rows, cols, part, blocks, count):
    x, core, tile = (place[0], place[1], place[2])
    whole = 2 * rows * cols
    half = rows * cols
    col = lax.broadcasted_iota(jnp.int32, (whole, part), 0) % cols
    zero = jnp.zeros((cols, padded.shape[1]), BF)
    padded[pl.ds(0, cols), :] = zero
    padded[pl.ds(cols + whole, cols), :] = zero
    for dc, source in ((0, mine), (1, other)):
        for dx in (0, 1):
            first, second = source[dx], source[2 + dx]
            padded[pl.ds(cols, half), :] = jnp.where(tile == 0, first, second)
            padded[pl.ds(cols + half, half), :] = jnp.where(tile == 0, second, first)
            taps = dot(padded[pl.ds(0, whole), :], weights[0])
            taps += dot(padded[pl.ds(cols, whole), :], weights[1])
            taps += dot(padded[pl.ds(2 * cols, whole), :], weights[2])
            left = pltpu.roll(taps[:, :part], 1, 0)
            right = pltpu.roll(taps[:, 2 * part :], whole - 1, 0)
            pre = taps[:, part : 2 * part] + jnp.where(col > 0, left, 0.0)
            pre = (pre + jnp.where(col < cols - 1, right, 0.0)).astype(BF)
            for t in (0, 1):
                for f in range(blocks):
                    start = t * half + f * count
                    out[x ^ dx, f, t, core ^ dc] = pre[start : start + count]


def attend_kernel(
    place, pre, pair, weights, qgain, kgain, scale,
    grads, sums, d_raw, q_hat, k_hat, q_rstd, k_rstd, d_value,
    mid_s, cot_s, doubled_k, doubled_v, doubled_acc,
    *, heads, count, padded,
):
    frames = pair.shape[0]
    width = pair.shape[-1]
    depth = width // heads
    total = frames * padded
    lanes = scale.shape[-1]
    me = place[0]
    mid_s[...] = jnp.zeros_like(mid_s)
    cot_s[...] = jnp.zeros_like(cot_s)
    for z in range(frames // 2):
        for e in (0, 1):
            f = 2 * z + e
            parts = [
                pre[x, z, c, t, e].astype(F32) for x in (0, 1) for c in (0, 1) for t in (0, 1)
            ]
            whole = jnp.concatenate(parts, axis=1)
            mid_s[pl.ds(f * padded, count), :] = pair[f, 0].astype(F32) + whole
            cot_s[pl.ds(f * padded, count), :] = pair[f, 1].astype(F32)
    mid = mid_s[...].astype(BF)
    cot = cot_s[...].astype(BF)
    pick = picker(width, lanes, depth, 0)
    both = jnp.concatenate([spreader(lanes, width, depth, 0)] * 2, axis=0)

    def stats(vec):
        cent = vec - spread(head_sums(vec, pick) / depth, both)
        var = head_sums(cent * cent, pick) / depth
        rstd = lax.rsqrt(var + EPS)
        return cent * spread(rstd, both), rstd

    hat, rstd = stats(dot(mid, weights[0 ^ me]))
    q_hat[...] = hat
    q_rstd[...] = rstd
    q_norm = hat * qgain[...]
    hat, rstd = stats(dot(mid, weights[1 ^ me]))
    k_hat[...] = hat
    k_rstd[...] = rstd
    hat = hat * kgain[...]
    doubled_k[pl.ds(0, total), :] = hat
    doubled_k[pl.ds(total, total), :] = hat
    value = dot(mid, weights[2 ^ me]).astype(BF).astype(F32)
    doubled_v[pl.ds(0, total), :] = value
    doubled_v[pl.ds(total, total), :] = value
    d_mixed = dot_t(cot, weights[3 ^ me]).astype(BF).astype(F32)

    raw = jnp.zeros((total, lanes), F32)
    d_probs = jnp.zeros((total, lanes), F32)
    for s in range(frames):
        here = picker(width, lanes, depth, SLOT * s)
        raw += head_sums(q_norm * doubled_k[pl.ds(s * padded, total), :], here)
        d_probs += head_sums(d_mixed * doubled_v[pl.ds(s * padded, total), :], here)
    raw = raw / math.sqrt(depth)

    def over_frames(x):
        step = SLOT
        while step < lanes:
            x = x + pltpu.roll(x, step, 1)
            step *= 2
        return x

    expo = jnp.exp(raw * scale[...])
    probs = expo / over_frames(expo)
    probs_b = probs.astype(BF)
    d_logits = probs * (d_probs - over_frames(probs * d_probs))
    sums[...] = jnp.sum(d_logits * raw, axis=0, keepdims=True)
    d_raw[...] = d_logits * scale[...] / math.sqrt(depth)

    mixed = jnp.zeros((total, width), F32)
    doubled_acc[...] = jnp.zeros_like(doubled_acc)
    for s in range(frames):
        weight = dot(probs_b, spreader(lanes, width, depth, SLOT * s))
        mixed += weight * doubled_v[pl.ds(s * padded, total), :]
        doubled_acc[pl.ds(s * padded, total), :] += weight * d_mixed
    mixed = mixed.astype(BF)
    dv = (doubled_acc[pl.ds(0, total), :] + doubled_acc[pl.ds(total, total), :]).astype(BF)
    d_value[...] = dv
    v_term = dot_rows(mid, dv).astype(BF)
    o_term = dot_rows(mixed, cot).astype(BF)
    core = place[1]
    rows = grads.shape[2]
    for z in range(frames // 2):
        for c in (0, 1):
            start = (2 * z + c) * rows
            grads[core ^ c, z, :, pl.ds(0, width)] = v_term[start : start + rows]
            grads[core ^ c, z, :, pl.ds(width, width)] = o_term[start : start + rows]


def back_kernel(
    place, d_raw, q_hat, k_hat, q_rstd, k_rstd, d_value, weights, qgain, kgain,
    d_mid, sums, doubled_k, doubled_acc,
    *, heads, padded,
):
    total, width = q_hat.shape
    depth = width // heads
    frames = total // padded
    lanes = d_raw.shape[-1]
    me = place[0]
    pick = picker(width, lanes, depth, 0)
    both = jnp.concatenate([spreader(lanes, width, depth, 0)] * 2, axis=0)
    k_norm = k_hat[...] * kgain[...]
    doubled_k[pl.ds(0, total), :] = k_norm
    doubled_k[pl.ds(total, total), :] = k_norm
    q_norm = q_hat[...] * qgain[...]
    doubled_acc[...] = jnp.zeros_like(doubled_acc)
    high, low = halves(d_raw[...])
    pair = jnp.concatenate([high, low], axis=1)
    d_qn = jnp.zeros((total, width), F32)
    for s in range(frames):
        one = spreader(lanes, width, depth, SLOT * s)
        weight = dot(pair, jnp.concatenate([one, one], axis=0))
        d_qn += weight * doubled_k[pl.ds(s * padded, total), :]
        doubled_acc[pl.ds(s * padded, total), :] += weight * q_norm
    d_kn = doubled_acc[pl.ds(0, total), :] + doubled_acc[pl.ds(total, total), :]

    def back(dhat, hat, rstd):
        first = spread(head_sums(dhat, pick) / depth, both)
        second = spread(head_sums(dhat * hat, pick) / depth, both)
        return (spread(rstd, both) * (dhat - first - hat * second)).astype(BF)

    sums[pl.ds(0, 1), :] = jnp.sum(d_qn * q_hat[...], axis=0, keepdims=True)
    sums[pl.ds(1, 1), :] = jnp.sum(d_kn * k_hat[...], axis=0, keepdims=True)
    d_query = back(d_qn * qgain[...], q_hat[...], q_rstd[...])
    d_key = back(d_kn * kgain[...], k_hat[...], k_rstd[...])
    out = dot_t(d_query, weights[0 ^ me]) + dot_t(d_key, weights[1 ^ me])
    out += dot_t(d_value[...], weights[2 ^ me])
    for f in range(frames):
        d_mid[f] = out[f * padded : (f + 1) * padded].astype(BF)


def specs(number):
    smem = pl.BlockSpec(memory_space=pltpu.SMEM)
    return [smem] + [pl.BlockSpec(memory_space=pltpu.VMEM)] * (number - 1)


def call(kernel, outs, scratch, *args):
    return pl.pallas_call(
        kernel,
        out_shape=[jax.ShapeDtypeStruct(shape, dtype) for shape, dtype in outs],
        in_specs=specs(len(args)),
        out_specs=[pl.BlockSpec(memory_space=pltpu.VMEM)] * len(outs),
        scratch_shapes=[pltpu.VMEM(shape, dtype) for shape, dtype in scratch],
        compiler_params=pltpu.CompilerParams(vmem_limit_bytes=VMEM_BYTES),
    )(*args)


def local(
    clip_input, cotangent, norm_gain, conv_weight, attn_weight, query_gain, key_gain, logit_scale
):
    source = clip_input[0, 0]
    cot = cotangent[0, 0]
    rows, cols, width = source.shape
    heads = logit_scale.shape[0]
    depth = width // heads
    tokens = rows * cols
    clips, frames, tiles = (lax.axis_size(name) for name in ("dp", "frame", "tile"))
    square = ("frame", "tile")
    ranks = frames * tiles
    share = conv_weight.shape[1]
    count = tokens // frames
    part = width // 8
    x = lax.axis_index("dp") % 2
    core = lax.axis_index("frame") % 2
    tile = lax.axis_index("tile")

    mine = lax.dynamic_slice_in_dim(conv_weight, x * (width // 2), width // 2, axis=2)
    mine = mine.reshape(3, 3, share, 4, part).transpose(3, 0, 2, 1, 4)
    mine = mine.reshape(4, 3, share, 3 * part)
    spread_out = jnp.broadcast_to(mine[None], (frames // 2,) + mine.shape)
    conv_in = lax.all_to_all(spread_out.reshape((ranks,) + mine.shape[1:]), square, 0, 0, tiled=True)
    conv_full = conv_in.transpose(1, 0, 2, 3).reshape(3, width, 3 * part)

    flat = source.reshape(tokens, width)
    xf = flat.astype(F32)
    sums = jnp.stack([jnp.sum(xf, axis=0), jnp.sum(xf * xf, axis=0)])
    sums = (sums + swap(sums, "tile")).reshape(2, GROUPS, width // GROUPS).sum(axis=-1)
    size = tokens * tiles * (width // GROUPS)
    mean = sums[0] / size
    rstd = lax.rsqrt(sums[1] / size - mean * mean + EPS)
    mean = jnp.repeat(mean, width // GROUPS)
    rstd = jnp.repeat(rstd, width // GROUPS)
    act = jax.nn.silu((xf - mean) * rstd * norm_gain).astype(BF)

    act = jnp.stack([act, swap(act, "dp")])
    act = jnp.concatenate([act, swap(act, "tile")])
    act_other = swap(act, "frame")

    pair = jnp.stack([flat.reshape(frames, count, width), cot.reshape(frames, count, width)], axis=1)
    pair = lax.all_to_all(pair, "frame", 0, 0, tiled=True)

    kinds = attn_weight.reshape(share, 4, width).transpose(1, 0, 2)
    kinds = jnp.broadcast_to(kinds[None], (frames // 2,) + kinds.shape).reshape(ranks, share, width)
    own = lax.all_to_all(kinds, square, 0, 0, tiled=True).reshape(1, width, width)
    own = jnp.concatenate([own, swap(own, "tile")])
    attn = jnp.concatenate([own, swap(own, "frame")])

    place = jnp.stack([x, core, tile]).astype(jnp.int32)
    (pre,) = call(
        functools.partial(
            conv_kernel, rows=rows, cols=cols, part=part, blocks=frames, count=count
        ),
        [((2, frames, tiles, 2, count, part), BF)],
        [((tiles * tokens + 2 * cols, width), BF)],
        place,
        act,
        act_other,
        conv_full,
    )
    groups = None
    if clips > 2:
        groups = [[2 * ranks * g + i for i in range(2 * ranks)] for g in range(clips // 2)]
    pre = lax.all_to_all(
        pre.reshape(2 * ranks, 2, count, part),
        ("dp",) + square,
        0,
        0,
        axis_index_groups=groups,
        tiled=True,
    ).reshape(2, frames // 2, 2, tiles, 2, count, part)

    lanes = frames * SLOT
    padded = round_up(count, 8)
    total = frames * padded
    scale = jnp.tile(jnp.pad(logit_scale, (0, SLOT - heads)), frames)[None]
    qgain = jnp.tile(query_gain, heads)[None]
    kgain = jnp.tile(key_gain, heads)[None]
    place = jnp.stack([2 * core + tile, core]).astype(jnp.int32)
    plane = (total, width)
    double = (2 * total, width)
    grads, scale_sums, d_raw, q_hat, k_hat, q_rstd, k_rstd, d_value = call(
        functools.partial(attend_kernel, heads=heads, count=count, padded=padded),
        [
            ((2, frames // 2, tiles * share, 2 * width), BF),
            ((1, lanes), F32),
            ((total, lanes), F32),
            (plane, F32),
            (plane, F32),
            ((total, lanes), F32),
            ((total, lanes), F32),
            (plane, BF),
        ],
        [(plane, F32), (plane, F32), (double, F32), (double, F32), (double, F32)],
        place,
        pre,
        pair,
        attn,
        qgain,
        kgain,
        scale,
    )

    chip = (grads[0].astype(F32) + swap(grads[1], "frame").astype(F32)).astype(BF)
    same_core = [[i for i in range(ranks) if (i // tiles) % 2 == c] for c in (0, 1)]
    chip = lax.all_to_all(
        chip.reshape(ranks // 2, share, 2 * width),
        square,
        0,
        0,
        axis_index_groups=same_core,
        tiled=True,
    )
    shares = jnp.sum(chip.astype(F32), axis=0)

    d_mid, gain_sums = call(
        functools.partial(back_kernel, heads=heads, padded=padded),
        [((frames, padded, width), BF), ((2, width), F32)],
        [(double, F32), (double, F32)],
        place,
        d_raw,
        q_hat,
        k_hat,
        q_rstd,
        k_rstd,
        d_value,
        attn,
        qgain,
        kgain,
    )
    d_back = lax.all_to_all(d_mid, "frame", 0, 0, tiled=True)[:, :count].reshape(rows, cols, width)
    mid_grad = (cot.astype(F32) + d_back.astype(F32)).astype(BF)

    if clips == 2:
        shares = shares.astype(BF)
        summed = shares.astype(F32) + swap(shares, "dp").astype(F32)
    else:
        summed = lax.psum(shares.astype(BF), "dp").astype(F32)
    gains = gain_sums.reshape(2, heads, depth).sum(axis=1)
    by_head = scale_sums.reshape(frames, SLOT).sum(axis=0)[:heads]
    scale_sum, qgain_sum, kgain_sum = lax.psum(
        (by_head, gains[0], gains[1]), ("dp", "frame", "tile")
    )
    factor = 1.0 / math.sqrt(clips * frames * tiles * tokens)
    return (
        mid_grad[None, None],
        summed[:, :width] * factor,
        summed[:, width:] * factor,
        qgain_sum * factor,
        kgain_sum * factor,
        scale_sum * factor,
    )


def solution(mesh):
    in_specs = (
        P("dp", "frame", "tile", None, None),
        P("dp", "frame", "tile", None, None),
        P(),
        P(None, ("frame", "tile"), None),
        P(("frame", "tile"), None),
        P(),
        P(),
        P(),
    )
    out_specs = (
        P("dp", "frame", "tile", None, None),
        P(("frame", "tile"), None),
        P(("frame", "tile"), None),
        P(),
        P(),
        P(),
    )
    return jax.shard_map(local, mesh=mesh, in_specs=in_specs, out_specs=out_specs, check_vma=False)
```

```python
import functools
import math

import jax
import jax.numpy as jnp
from jax import lax
from jax.experimental import pallas as pl
from jax.experimental.pallas import tpu as pltpu
from jax.sharding import PartitionSpec as P

GROUPS = 32
EPS = 1e-05
SLOT = 16
BF = jnp.bfloat16
F32 = jnp.float32
VMEM_BYTES = 48 * 1024 * 1024


def swap(x, axis):
    return lax.ppermute(x, axis, [(i, i ^ 1) for i in range(lax.axis_size(axis))])


def round_up(value, unit):
    return -(-value // unit) * unit


def dot(a, b):
    return lax.dot_general(a, b, (((1,), (0,)), ((), ())), preferred_element_type=F32)


def dot_t(a, b):
    return lax.dot_general(a, b, (((1,), (1,)), ((), ())), preferred_element_type=F32)


def dot_rows(a, b):
    return lax.dot_general(a, b, (((0,), (0,)), ((), ())), preferred_element_type=F32)


def halves(x):
    high = x.astype(BF)
    return high, (x - high.astype(F32)).astype(BF)


def picker(rows, cols, depth, offset):
    row = lax.broadcasted_iota(jnp.int32, (rows, cols), 0)
    col = lax.broadcasted_iota(jnp.int32, (rows, cols), 1)
    return (col - row // depth == offset).astype(F32).astype(BF)


def spreader(rows, cols, depth, offset):
    row = lax.broadcasted_iota(jnp.int32, (rows, cols), 0)
    col = lax.broadcasted_iota(jnp.int32, (rows, cols), 1)
    return (row - col // depth == offset).astype(F32).astype(BF)


def head_sums(x, pick):
    high, low = halves(x)
    return dot(high, pick) + dot(low, pick)


def spread(x, both):
    high, low = halves(x)
    return dot(jnp.concatenate([high, low], axis=1), both)


def over_slots(x):
    step = SLOT
    while step < x.shape[1]:
        x = x + pltpu.roll(x, step, 1)
        step *= 2
    return x


def each(number, body):
    if number > 8:
        lax.fori_loop(0, number, lambda i, _: body(i), None)
    else:
        for i in range(number):
            body(i)


def act_kernel(place, gain, first, *rest, cols, part):
    second, (act, kept) = (rest[:-2], rest[-2:])
    half, width = first.shape
    tile, chosen = (place[2], place[3])
    upper = first[...]
    lower = jnp.concatenate([ref[...] for ref in second], axis=0) if len(second) > 1 else second[0][...]
    upper, lower = (jnp.where(tile == 0, upper, lower), jnp.where(tile == 0, lower, upper))
    kept[pl.ds(0, half), :] = dot(upper, picker(width, part, 1, -part * chosen)).astype(BF)
    kept[pl.ds(half, half), :] = dot(lower, picker(width, part, 1, -part * chosen)).astype(BF)
    upper, lower = (upper.astype(F32), lower.astype(F32))
    total = jnp.sum(upper, axis=0, keepdims=True) + jnp.sum(lower, axis=0, keepdims=True)
    square = jnp.sum(upper * upper, axis=0, keepdims=True)
    square = square + jnp.sum(lower * lower, axis=0, keepdims=True)
    both = jnp.concatenate([total, square, jnp.zeros((6, width), F32)], axis=0)
    high, low = halves(both)
    lowest = (both - high.astype(F32) - low.astype(F32)).astype(BF)
    per_group = width // GROUPS
    pick = picker(width, 128, per_group, 0)
    back = spreader(128, width, per_group, 0)
    both = (dot(high, pick) + dot(low, pick) + dot(lowest, pick)) / (2 * half * per_group)
    mean = both[0:1]
    rstd = lax.rsqrt(both[1:2] - mean * mean + EPS)
    both = jnp.concatenate([mean, rstd, jnp.zeros((6, 128), F32)], axis=0)
    high, low = halves(both)
    lowest = (both - high.astype(F32) - low.astype(F32)).astype(BF)
    both = dot(high, back) + dot(low, back) + dot(lowest, back)
    mean = both[0:1]
    scale = both[1:2] * gain[...]
    act[pl.ds(0, cols), :] = jnp.zeros((cols, width), BF)
    act[pl.ds(cols + 2 * half, cols), :] = jnp.zeros((cols, width), BF)
    for start, x in ((cols, upper), (cols + half, lower)):
        zed = (x - mean) * scale
        act[pl.ds(start, half), :] = (zed / (1.0 + jnp.exp(-zed))).astype(BF)


def conv_kernel(place, weights, *refs, cols, part, blocks, count):
    acts, kept, out = (refs[:4], refs[4:8], refs[8])
    x, core = (place[0], place[1])
    whole = kept[0].shape[0]
    half = whole // 2
    third = count // 3
    col = lax.broadcasted_iota(jnp.int32, (whole, part), 0) % cols
    for dc in (0, 1):
        for dx in (0, 1):
            act, plus = (acts[2 * dc + dx], kept[2 * dc + dx])
            taps = dot(act[pl.ds(0, whole), :], weights[0])
            taps += dot(act[pl.ds(cols, whole), :], weights[1])
            taps += dot(act[pl.ds(2 * cols, whole), :], weights[2])
            left = pltpu.roll(taps[:, :part], 1, 0)
            right = pltpu.roll(taps[:, 2 * part :], whole - 1, 0)
            pre = taps[:, part : 2 * part] + jnp.where(col > 0, left, 0.0)
            pre = pre + jnp.where(col < cols - 1, right, 0.0)
            mid = (plus[...].astype(F32) + pre).astype(BF)
            if blocks > 8:
                out[x ^ dx, core ^ dc] = mid
                continue
            for t in (0, 1):
                for f in range(blocks):
                    start = t * half + f * count
                    three = [mid[start + third * j : start + third * (j + 1)] for j in range(3)]
                    out[x ^ dx, f, t, core ^ dc] = jnp.concatenate(three, axis=1)


def attend_kernel(
    mid_in, weights, qgain, kgain, scale,
    mid_out, q_hat, k_hat, q_rstd, k_rstd, value_out, raw_out, probs_out, mixed_out,
    mid_s, doubled, mixed_s, raw_s,
    *, heads, count, padded, part,
):
    total, width = mid_s.shape
    frames = total // padded
    depth = width // heads
    lanes = scale.shape[-1]
    third = count // 3
    mid_s[...] = jnp.zeros_like(mid_s)

    def unpack(z):
        for e in (0, 1):
            blocks = [mid_in[x, z, c, t, e] for x in (0, 1) for c in (0, 1) for t in (0, 1)]
            for j in range(3):
                piece = [b[:, j * part : (j + 1) * part] for b in blocks]
                start = (2 * z + e) * padded + j * third
                mid_s[pl.ds(start, third), :] = jnp.concatenate(piece, axis=1).astype(F32)

    for z in range(frames // 2):
        unpack(z)
    mid = mid_s[...].astype(BF)
    mid_out[...] = mid
    pick = picker(width, lanes, depth, 0)
    both = jnp.concatenate([spreader(lanes, width, depth, 0)] * 2, axis=0)

    def stats(vec):
        cent = vec - spread(head_sums(vec, pick) / depth, both)
        var = head_sums(cent * cent, pick) / depth
        rstd = lax.rsqrt(var + EPS)
        return cent * spread(rstd, both), rstd

    hat, rstd = stats(dot(mid, weights[:, pl.ds(0, width)]))
    q_hat[...] = hat
    q_rstd[...] = rstd
    q_norm = hat * qgain[...]
    hat, rstd = stats(dot(mid, weights[:, pl.ds(width, width)]))
    k_hat[...] = hat
    k_rstd[...] = rstd
    hat = hat * kgain[...]
    doubled[pl.ds(0, total), :] = hat
    doubled[pl.ds(total, total), :] = hat
    raw_s[...] = jnp.zeros_like(raw_s)

    def logits(s):
        here = picker(width, lanes, depth, SLOT * s)
        raw_s[...] += head_sums(q_norm * doubled[pl.ds(s * padded, total), :], here)

    each(frames, logits)
    raw = raw_s[...] / math.sqrt(depth)
    raw_out[...] = raw
    expo = jnp.exp(raw * scale[...])
    probs = expo / over_slots(expo)
    probs_out[...] = probs
    probs_b = probs.astype(BF)

    value = dot(mid, weights[:, pl.ds(2 * width, width)]).astype(BF)
    value_out[...] = value
    value = value.astype(F32)
    doubled[pl.ds(0, total), :] = value
    doubled[pl.ds(total, total), :] = value
    mixed_s[...] = jnp.zeros_like(mixed_s)

    def mix(s):
        weight = dot(probs_b, spreader(lanes, width, depth, SLOT * s))
        mixed_s[...] += weight * doubled[pl.ds(s * padded, total), :]

    each(frames, mix)
    mixed_out[...] = mixed_s[...].astype(BF)


def middle_kernel(
    place, cot_in, weights, mid, mixed, value_in, raw, probs_in, scale,
    grads, sums, d_raw, d_value,
    cot_s, doubled, doubled_acc, probs_s,
    *, heads, count, padded,
):
    total, width = mid.shape
    frames = total // padded
    depth = width // heads
    lanes = scale.shape[-1]
    x, core = (place[0], place[1])
    cot_s[...] = jnp.zeros_like(cot_s)

    def unpack(f):
        cot_s[pl.ds(f * padded, count), :] = cot_in[f].astype(F32)

    each(frames, unpack)
    cot = cot_s[...].astype(BF)
    rows = grads.shape[3]

    def store(kind, term):
        for z in range(frames // 2):
            for c in (0, 1):
                start = (2 * z + c) * rows
                grads[x ^ kind, core ^ c, z] = term[start : start + rows]

    store(1, dot_rows(mixed[...], cot).astype(BF))
    d_mixed = dot_t(cot, weights[:, pl.ds(3 * width, width)]).astype(BF).astype(F32)
    value = value_in[...].astype(F32)
    doubled[pl.ds(0, total), :] = value
    doubled[pl.ds(total, total), :] = value
    doubled_acc[...] = jnp.zeros_like(doubled_acc)
    probs_s[...] = jnp.zeros_like(probs_s)
    probs = probs_in[...]
    probs_b = probs.astype(BF)

    def shift(s):
        here = picker(width, lanes, depth, SLOT * s)
        probs_s[...] += head_sums(d_mixed * doubled[pl.ds(s * padded, total), :], here)
        weight = dot(probs_b, spreader(lanes, width, depth, SLOT * s))
        doubled_acc[pl.ds(s * padded, total), :] += weight * d_mixed

    each(frames, shift)
    d_probs = probs_s[...]
    dv = (doubled_acc[pl.ds(0, total), :] + doubled_acc[pl.ds(total, total), :]).astype(BF)
    d_value[...] = dv
    store(0, dot_rows(mid[...], dv).astype(BF))
    d_logits = probs * (d_probs - over_slots(probs * d_probs))
    sums[...] = jnp.sum(d_logits * raw[...], axis=0, keepdims=True)
    d_raw[...] = d_logits * scale[...] / math.sqrt(depth)


def back_kernel(
    d_raw, q_hat, k_hat, q_rstd, k_rstd, d_value, weights, qgain, kgain, scale_sums,
    d_mid,
    doubled, doubled_acc, d_qn_s,
    *, heads, count, padded,
):
    total, width = q_hat.shape
    depth = width // heads
    frames = total // padded
    lanes = d_raw.shape[-1]
    pick = picker(width, lanes, depth, 0)
    both = jnp.concatenate([spreader(lanes, width, depth, 0)] * 2, axis=0)
    k_norm = k_hat[...] * kgain[...]
    doubled[pl.ds(0, total), :] = k_norm
    doubled[pl.ds(total, total), :] = k_norm
    q_norm = q_hat[...] * qgain[...]
    doubled_acc[...] = jnp.zeros_like(doubled_acc)
    d_qn_s[...] = jnp.zeros_like(d_qn_s)
    high, low = halves(d_raw[...])
    pair = jnp.concatenate([high, low], axis=1)

    def shift(s):
        one = spreader(lanes, width, depth, SLOT * s)
        weight = dot(pair, jnp.concatenate([one, one], axis=0))
        d_qn_s[...] += weight * doubled[pl.ds(s * padded, total), :]
        doubled_acc[pl.ds(s * padded, total), :] += weight * q_norm

    each(frames, shift)
    d_qn = d_qn_s[...]
    d_kn = doubled_acc[pl.ds(0, total), :] + doubled_acc[pl.ds(total, total), :]

    def back(dhat, hat, rstd):
        first = spread(head_sums(dhat, pick) / depth, both)
        second = spread(head_sums(dhat * hat, pick) / depth, both)
        return (spread(rstd, both) * (dhat - first - hat * second)).astype(BF)

    d_query = back(d_qn * qgain[...], q_hat[...], q_rstd[...])
    d_key = back(d_kn * kgain[...], k_hat[...], k_rstd[...])
    out = dot_t(d_query, weights[:, pl.ds(0, width)])
    out += dot_t(d_key, weights[:, pl.ds(width, width)])
    out += dot_t(d_value[...], weights[:, pl.ds(2 * width, width)])

    row = lax.broadcasted_iota(jnp.int32, (width, 128), 0)
    col = lax.broadcasted_iota(jnp.int32, (width, 128), 1)
    fold = (row % depth == col).astype(F32)

    def folded(d_norm, hat):
        sums = jnp.sum(d_norm * hat, axis=0, keepdims=True)
        sums = jnp.broadcast_to(sums, (8, width))
        return jnp.dot(sums, fold, precision=lax.Precision.HIGHEST, preferred_element_type=F32)[0:1]

    by_head = over_slots(jnp.broadcast_to(scale_sums[...], (8, lanes)))[0:1, :128]
    small = [folded(d_qn, q_hat[...]), folded(d_kn, k_hat[...]), by_head]
    small.append(jnp.zeros((1, width - 384), F32))
    small = jnp.concatenate(small, axis=1)
    high, low = halves(small)
    lowest = (small - high.astype(F32) - low.astype(F32)).astype(BF)
    spare = [high.astype(F32), low.astype(F32), lowest.astype(F32)]
    if padded - count > 3:
        spare.append(jnp.zeros((padded - count - 3, width), F32))
    spare = jnp.concatenate(spare, axis=0)
    for f in range(frames):
        tokens = out[f * padded : f * padded + count]
        d_mid[f] = jnp.concatenate([tokens, spare], axis=0).astype(BF)


def call(kernel, outs, scratch, *args):
    smem = pl.BlockSpec(memory_space=pltpu.SMEM)
    vmem = pl.BlockSpec(memory_space=pltpu.VMEM)
    return pl.pallas_call(
        kernel,
        out_shape=[jax.ShapeDtypeStruct(shape, dtype) for shape, dtype in outs],
        in_specs=[smem if arg.dtype == jnp.int32 else vmem for arg in args],
        out_specs=[vmem] * len(outs),
        scratch_shapes=[pltpu.VMEM(shape, dtype) for shape, dtype in scratch],
        compiler_params=pltpu.CompilerParams(vmem_limit_bytes=VMEM_BYTES),
    )(*args)


def local(
    clip_input, cotangent, norm_gain, conv_weight, attn_weight, query_gain, key_gain, logit_scale
):
    source = clip_input[0, 0]
    cot = cotangent[0, 0]
    rows, cols, width = source.shape
    heads = logit_scale.shape[0]
    depth = width // heads
    tokens = rows * cols
    clips, frames, tiles = (lax.axis_size(name) for name in ("dp", "frame", "tile"))
    square = ("frame", "tile")
    ranks = frames * tiles
    share = conv_weight.shape[1]
    count = tokens // frames
    third = count // 3
    part = width // 8
    x = lax.axis_index("dp") % 2
    core = lax.axis_index("frame") % 2
    tile = lax.axis_index("tile")
    place = jnp.stack([x, core, tile, 4 * x + 2 * core + tile]).astype(jnp.int32)

    mine = lax.dynamic_slice_in_dim(conv_weight, x * (width // 2), width // 2, axis=2)
    mine = mine.reshape(3, 3, share, 4, part).transpose(3, 0, 2, 1, 4)
    mine = mine.reshape(4, 3, share, 3 * part)
    spread_out = jnp.broadcast_to(mine[None], (frames // 2,) + mine.shape)
    conv_in = lax.all_to_all(spread_out.reshape((ranks,) + mine.shape[1:]), square, 0, 0, tiled=True)
    conv_full = conv_in.transpose(1, 0, 2, 3).reshape(3, width, 3 * part)
    attn_full = lax.all_gather(attn_weight, square, axis=0, tiled=True)

    flat = source.reshape(tokens, width)
    half = tokens // 2
    along_x = swap(flat, "dp")
    along_y = swap(flat, "tile")
    across = (swap(along_x[:half], "tile"), swap(along_y[half:], "dp"))
    own = ((flat, along_y), (along_x,) + across)
    gain = norm_gain[None]
    acts, kept = ([], [])
    for other in (False, True):
        for pieces in own:
            if other:
                pieces = [swap(piece, "frame") for piece in pieces]
            act, keep = call(
                functools.partial(act_kernel, cols=cols, part=part),
                [((tiles * tokens + 2 * cols, width), BF), ((tiles * tokens, part), BF)],
                [],
                place,
                gain,
                *pieces,
            )
            acts.append(act)
            kept.append(keep)

    blocked = (2, frames, tiles, 2, third, 3 * part)
    plain = (2, 2, tiles * tokens, part)
    (mid,) = call(
        functools.partial(conv_kernel, cols=cols, part=part, blocks=frames, count=count),
        [(plain if frames > 8 else blocked, BF)],
        [],
        place,
        conv_full,
        *acts,
        *kept,
    )
    if frames > 8:
        mid = mid.reshape(2, 2, tiles, frames, 3, third, part).transpose(0, 3, 2, 1, 5, 4, 6)
    groups = None
    if clips > 2:
        groups = [[2 * ranks * g + i for i in range(2 * ranks)] for g in range(clips // 2)]
    mid = lax.all_to_all(
        mid.reshape(2 * ranks, 2 * third, 3 * part),
        ("dp",) + square,
        0,
        0,
        axis_index_groups=groups,
        tiled=True,
    ).reshape(2, frames // 2, 2, tiles, 2, third, 3 * part)

    cot_blocks, mid = lax.optimization_barrier((cot.reshape(frames, count, width), mid))
    cot_blocks = lax.all_to_all(cot_blocks, "frame", 0, 0, tiled=True)

    lanes = frames * SLOT
    padded = round_up(count + 3, 8)
    total = frames * padded
    scale = jnp.tile(jnp.pad(logit_scale, (0, SLOT - heads)), frames)[None]
    qgain = jnp.tile(query_gain, heads)[None]
    kgain = jnp.tile(key_gain, heads)[None]
    plane = (total, width)
    double = (2 * total, width)
    narrow = (total, lanes)
    mid, q_hat, k_hat, q_rstd, k_rstd, value, raw, probs, mixed = call(
        functools.partial(attend_kernel, heads=heads, count=count, padded=padded, part=part),
        [
            (plane, BF), (plane, F32), (plane, F32), (narrow, F32), (narrow, F32),
            (plane, BF), (narrow, F32), (narrow, F32), (plane, BF),
        ],
        [(plane, F32), (double, F32), (plane, F32), (narrow, F32)],
        mid, attn_full, qgain, kgain, scale,
    )
    grads, scale_sums, d_raw, d_value = call(
        functools.partial(middle_kernel, heads=heads, count=count, padded=padded),
        [
            ((2, 2, frames // 2, tiles * share, width), BF),
            ((1, lanes), F32), (narrow, F32), (plane, BF),
        ],
        [(plane, F32), (double, F32), (double, F32), (narrow, F32)],
        place, cot_blocks, attn_full, mid, mixed, value, raw, probs, scale,
    )

    chip = (grads[:, 0].astype(F32) + swap(grads[:, 1], "frame").astype(F32)).astype(BF)
    shares = (chip[0].astype(F32) + swap(chip[1], "dp").astype(F32)).astype(BF)
    same_core = [[i for i in range(ranks) if (i // tiles) % 2 == c] for c in (0, 1)]
    shares = lax.all_to_all(
        shares.reshape(ranks // 2, share, width),
        square,
        0,
        0,
        axis_index_groups=same_core,
        tiled=True,
    )
    shares = jnp.sum(shares.astype(F32), axis=0)

    (d_mid,) = call(
        functools.partial(back_kernel, heads=heads, count=count, padded=padded),
        [((frames, padded, width), BF)],
        [(double, F32), (double, F32), (plane, F32)],
        d_raw, q_hat, k_hat, q_rstd, k_rstd, d_value, attn_full, qgain, kgain, scale_sums,
    )
    d_back = lax.all_to_all(d_mid, "frame", 0, 0, tiled=True)
    small = jnp.sum(d_back[:, count : count + 3].astype(F32), axis=(0, 1))
    d_back = d_back[:, :count].reshape(rows, cols, width)
    mid_grad = (cot.astype(F32) + d_back.astype(F32)).astype(BF)

    small = small + swap(small, "tile")
    if clips == 2:
        small = small + swap(small, "dp")
    else:
        small = lax.psum(small, "dp")
        same_clip = [[i for i in range(clips) if i % 2 == c] for c in (0, 1)]
        shares = lax.psum(shares, "dp", axis_index_groups=same_clip)
    theirs = swap(shares, "dp")
    factor = 1.0 / math.sqrt(clips * frames * tiles * tokens)
    value_grad = jnp.where(x == 0, shares, theirs) * factor
    out_proj_grad = jnp.where(x == 0, theirs, shares) * factor
    scale_sum = small[256 : 256 + heads]
    return (
        mid_grad[None, None],
        value_grad,
        out_proj_grad,
        small[:depth] * factor,
        small[128 : 128 + depth] * factor,
        scale_sum * factor,
    )


def solution(mesh):
    in_specs = (
        P("dp", "frame", "tile", None, None),
        P("dp", "frame", "tile", None, None),
        P(),
        P(None, ("frame", "tile"), None),
        P(("frame", "tile"), None),
        P(),
        P(),
        P(),
    )
    out_specs = (
        P("dp", "frame", "tile", None, None),
        P(("frame", "tile"), None),
        P(("frame", "tile"), None),
        P(),
        P(),
        P(),
    )
    return jax.shard_map(local, mesh=mesh, in_specs=in_specs, out_specs=out_specs, check_vma=False)
```

```python
import functools
import math

import jax
import jax.numpy as jnp
from jax import lax
from jax.experimental import pallas as pl
from jax.experimental.pallas import tpu as pltpu
from jax.sharding import PartitionSpec as P

GROUPS = 32
EPS = 1e-05
SLOT = 16
BF = jnp.bfloat16
F32 = jnp.float32


def swap(x, axis):
    return lax.ppermute(x, axis, [(i, i ^ 1) for i in range(lax.axis_size(axis))])


def round_up(value, unit):
    return -(-value // unit) * unit


def dot(a, b):
    return lax.dot_general(a, b, (((1,), (0,)), ((), ())), preferred_element_type=F32)


def dot_t(a, b):
    return lax.dot_general(a, b, (((1,), (1,)), ((), ())), preferred_element_type=F32)


def dot_rows(a, b):
    return lax.dot_general(a, b, (((0,), (0,)), ((), ())), preferred_element_type=F32)


def halves(x):
    high = x.astype(BF)
    return high, (x - high.astype(F32)).astype(BF)


def picker(rows, cols, depth, offset):
    row = lax.broadcasted_iota(jnp.int32, (rows, cols), 0)
    col = lax.broadcasted_iota(jnp.int32, (rows, cols), 1)
    return (col - row // depth == offset).astype(F32).astype(BF)


def spreader(rows, cols, depth, offset):
    row = lax.broadcasted_iota(jnp.int32, (rows, cols), 0)
    col = lax.broadcasted_iota(jnp.int32, (rows, cols), 1)
    return (row - col // depth == offset).astype(F32).astype(BF)


def head_sums(x, pick):
    high, low = halves(x)
    return dot(high, pick) + dot(low, pick)


def spread(x, both):
    high, low = halves(x)
    return dot(jnp.concatenate([high, low], axis=1), both)


def over_slots(x):
    step = SLOT
    while step < x.shape[1]:
        x = x + pltpu.roll(x, step, 1)
        step *= 2
    return x


def each(number, body):
    if number > 8:
        lax.fori_loop(0, number, lambda i, _: body(i), None)
    else:
        for i in range(number):
            body(i)


def act_kernel(place, gain, *refs, cols, part):
    blocks, (acts, kept) = (refs[:-2], refs[-2:])
    half, width = blocks[0].shape
    tile, chosen = (place[2], place[3])
    choice = picker(width, part, 1, -part * chosen)
    per_group = width // GROUPS
    pick = picker(width, 128, per_group, 0)
    back = spreader(128, width, per_group, 0)

    def thirds(x):
        high, low = halves(x)
        return high, low, (x - high.astype(F32) - low.astype(F32)).astype(BF)

    totals, squares = ([], [])
    for frame in range(4):
        total, square = (0.0, 0.0)
        for dy in (0, 1):
            x = blocks[2 * frame + dy][...]
            start = pl.multiple_of((tile ^ dy) * half, half)
            kept[frame, pl.ds(start, half), :] = dot(x, choice).astype(BF)
            x = x.astype(F32)
            total = total + jnp.sum(x, axis=0, keepdims=True)
            square = square + jnp.sum(x * x, axis=0, keepdims=True)
        totals.append(total)
        squares.append(square)
    high, low, lowest = thirds(jnp.concatenate(totals + squares, axis=0))
    both = (dot(high, pick) + dot(low, pick) + dot(lowest, pick)) / (2 * half * per_group)
    mean = both[0:4]
    rstd = lax.rsqrt(both[4:8] - mean * mean + EPS)
    high, low, lowest = thirds(jnp.concatenate([mean, rstd], axis=0))
    both = dot(high, back) + dot(low, back) + dot(lowest, back)
    scales = both[4:8] * gain[...]
    for frame in range(4):
        acts[frame, pl.ds(0, cols), :] = jnp.zeros((cols, width), BF)
        acts[frame, pl.ds(cols + 2 * half, cols), :] = jnp.zeros((cols, width), BF)
        for dy in (0, 1):
            x = blocks[2 * frame + dy][...].astype(F32)
            zed = (x - both[frame : frame + 1]) * scales[frame : frame + 1]
            start = pl.multiple_of(cols + (tile ^ dy) * half, cols)
            acts[frame, pl.ds(start, half), :] = (zed / (1.0 + jnp.exp(-zed))).astype(BF)


def conv_kernel(place, weights, acts, kept, out, *, cols, part, blocks, count):
    x, core = (place[0], place[1])
    whole = kept.shape[1]
    half = whole // 2
    third = count // 3
    col = lax.broadcasted_iota(jnp.int32, (whole, part), 0) % cols
    for dx in (0, 1):
        mids = []
        for dc in (0, 1):
            frame = 2 * dc + dx
            taps = dot(acts[frame, pl.ds(0, whole), :], weights[0])
            taps += dot(acts[frame, pl.ds(cols, whole), :], weights[1])
            taps += dot(acts[frame, pl.ds(2 * cols, whole), :], weights[2])
            left = pltpu.roll(taps[:, :part], 1, 0)
            right = pltpu.roll(taps[:, 2 * part :], whole - 1, 0)
            pre = taps[:, part : 2 * part] + jnp.where(col > 0, left, 0.0)
            pre = pre + jnp.where(col < cols - 1, right, 0.0)
            mids.append((kept[frame].astype(F32) + pre).astype(BF))
        if blocks > 8:
            for dc in (0, 1):
                out[x ^ dx, dc] = mids[dc]
            continue
        for f in range(blocks):
            for t in (0, 1):
                start = t * half + f * count
                rows = [
                    jnp.concatenate(
                        [mid[start + third * j : start + third * (j + 1)] for j in range(3)], axis=1
                    )
                    for mid in mids
                ]
                index = ((x ^ dx) * blocks + f) * 2 + t
                out[index] = jnp.concatenate(rows, axis=0)


def attend_kernel(
    mid_in, weights, qgain, kgain, scale,
    mid_out, q_hat, k_hat, q_rstd, k_rstd, value_out, raw_out, probs_out, mixed_out,
    mid_s, doubled, mixed_s, raw_s,
    *, heads, count, padded, part,
):
    total, width = mid_s.shape
    frames = total // padded
    depth = width // heads
    lanes = scale.shape[-1]
    third = count // 3
    mid_s[...] = jnp.zeros_like(mid_s)

    def unpack(z):
        for e in (0, 1):
            blocks = [
                mid_in[(x * frames + 2 * z + c) * 2 + t, pl.ds((e ^ c) * third, third), :]
                for x in (0, 1)
                for c in (0, 1)
                for t in (0, 1)
            ]
            for j in range(3):
                piece = [b[:, j * part : (j + 1) * part] for b in blocks]
                start = (2 * z + e) * padded + j * third
                mid_s[pl.ds(start, third), :] = jnp.concatenate(piece, axis=1).astype(F32)

    for z in range(frames // 2):
        unpack(z)
    mid = mid_s[...].astype(BF)
    mid_out[...] = mid
    pick = picker(width, lanes, depth, 0)
    both = jnp.concatenate([spreader(lanes, width, depth, 0)] * 2, axis=0)

    def stats(vec):
        cent = vec - spread(head_sums(vec, pick) / depth, both)
        var = head_sums(cent * cent, pick) / depth
        rstd = lax.rsqrt(var + EPS)
        return cent * spread(rstd, both), rstd

    hat, rstd = stats(dot(mid, weights[:, pl.ds(0, width)]))
    q_hat[...] = hat
    q_rstd[...] = rstd
    q_norm = hat * qgain[...]
    hat, rstd = stats(dot(mid, weights[:, pl.ds(width, width)]))
    k_hat[...] = hat
    k_rstd[...] = rstd
    hat = hat * kgain[...]
    doubled[pl.ds(0, total), :] = hat
    doubled[pl.ds(total, total), :] = hat
    raw_s[...] = jnp.zeros_like(raw_s)

    def logits(s):
        here = picker(width, lanes, depth, SLOT * s)
        raw_s[...] += head_sums(q_norm * doubled[pl.ds(s * padded, total), :], here)

    each(frames, logits)
    raw = raw_s[...] / math.sqrt(depth)
    raw_out[...] = raw
    expo = jnp.exp(raw * scale[...])
    probs = expo / over_slots(expo)
    probs_out[...] = probs
    probs_b = probs.astype(BF)

    value = dot(mid, weights[:, pl.ds(2 * width, width)]).astype(BF)
    value_out[...] = value
    value = value.astype(F32)
    doubled[pl.ds(0, total), :] = value
    doubled[pl.ds(total, total), :] = value
    mixed_s[...] = jnp.zeros_like(mixed_s)

    def mix(s):
        weight = dot(probs_b, spreader(lanes, width, depth, SLOT * s))
        mixed_s[...] += weight * doubled[pl.ds(s * padded, total), :]

    each(frames, mix)
    mixed_out[...] = mixed_s[...].astype(BF)


def middle_kernel(
    place, cot_in, weights, mid, mixed, value_in, raw, probs_in, scale,
    grads, sums, d_raw, d_value,
    cot_s, doubled, doubled_acc, probs_s,
    *, heads, count, padded,
):
    total, width = mid.shape
    frames = total // padded
    depth = width // heads
    lanes = scale.shape[-1]
    x, core, tile, plane = (place[0], place[1], place[2], place[4])
    cot_s[...] = jnp.zeros_like(cot_s)

    def unpack(f):
        cot_s[pl.ds(f * padded, count), :] = cot_in[f].astype(F32)

    each(frames, unpack)
    cot = cot_s[...].astype(BF)
    rows = grads.shape[4]

    def store(kind, term):
        for z in range(frames // 2):
            for c in (0, 1):
                for t in (0, 1):
                    start = (4 * z + 2 * c + t) * rows
                    block = term[start : start + rows]
                    grads[x ^ kind, core ^ c, tile ^ t, plane ^ z] = block

    store(1, dot_rows(mixed[...], cot).astype(BF))
    d_mixed = dot_t(cot, weights[:, pl.ds(3 * width, width)]).astype(BF).astype(F32)
    value = value_in[...].astype(F32)
    doubled[pl.ds(0, total), :] = value
    doubled[pl.ds(total, total), :] = value
    doubled_acc[...] = jnp.zeros_like(doubled_acc)
    probs_s[...] = jnp.zeros_like(probs_s)
    probs = probs_in[...]
    probs_b = probs.astype(BF)

    def shift(s):
        here = picker(width, lanes, depth, SLOT * s)
        probs_s[...] += head_sums(d_mixed * doubled[pl.ds(s * padded, total), :], here)
        weight = dot(probs_b, spreader(lanes, width, depth, SLOT * s))
        doubled_acc[pl.ds(s * padded, total), :] += weight * d_mixed

    each(frames, shift)
    d_probs = probs_s[...]
    dv = (doubled_acc[pl.ds(0, total), :] + doubled_acc[pl.ds(total, total), :]).astype(BF)
    d_value[...] = dv
    store(0, dot_rows(mid[...], dv).astype(BF))
    d_logits = probs * (d_probs - over_slots(probs * d_probs))
    sums[...] = jnp.sum(d_logits * raw[...], axis=0, keepdims=True)
    d_raw[...] = d_logits * scale[...] / math.sqrt(depth)


def back_kernel(
    d_raw, q_hat, k_hat, q_rstd, k_rstd, d_value, weights, qgain, kgain, scale_sums,
    d_mid,
    doubled, doubled_acc, d_qn_s,
    *, heads, count, padded,
):
    total, width = q_hat.shape
    depth = width // heads
    frames = total // padded
    lanes = d_raw.shape[-1]
    pick = picker(width, lanes, depth, 0)
    both = jnp.concatenate([spreader(lanes, width, depth, 0)] * 2, axis=0)
    k_norm = k_hat[...] * kgain[...]
    doubled[pl.ds(0, total), :] = k_norm
    doubled[pl.ds(total, total), :] = k_norm
    q_norm = q_hat[...] * qgain[...]
    doubled_acc[...] = jnp.zeros_like(doubled_acc)
    d_qn_s[...] = jnp.zeros_like(d_qn_s)
    high, low = halves(d_raw[...])
    pair = jnp.concatenate([high, low], axis=1)

    def shift(s):
        one = spreader(lanes, width, depth, SLOT * s)
        weight = dot(pair, jnp.concatenate([one, one], axis=0))
        d_qn_s[...] += weight * doubled[pl.ds(s * padded, total), :]
        doubled_acc[pl.ds(s * padded, total), :] += weight * q_norm

    each(frames, shift)
    d_qn = d_qn_s[...]
    d_kn = doubled_acc[pl.ds(0, total), :] + doubled_acc[pl.ds(total, total), :]

    def back(dhat, hat, rstd):
        first = spread(head_sums(dhat, pick) / depth, both)
        second = spread(head_sums(dhat * hat, pick) / depth, both)
        return (spread(rstd, both) * (dhat - first - hat * second)).astype(BF)

    d_query = back(d_qn * qgain[...], q_hat[...], q_rstd[...])
    d_key = back(d_kn * kgain[...], k_hat[...], k_rstd[...])
    out = dot_t(d_query, weights[:, pl.ds(0, width)])
    out += dot_t(d_key, weights[:, pl.ds(width, width)])
    out += dot_t(d_value[...], weights[:, pl.ds(2 * width, width)])

    row = lax.broadcasted_iota(jnp.int32, (width, 128), 0)
    col = lax.broadcasted_iota(jnp.int32, (width, 128), 1)
    fold = (row % depth == col).astype(F32)

    def folded(d_norm, hat):
        sums = jnp.sum(d_norm * hat, axis=0, keepdims=True)
        sums = jnp.broadcast_to(sums, (8, width))
        return jnp.dot(sums, fold, precision=lax.Precision.HIGHEST, preferred_element_type=F32)[0:1]

    by_head = over_slots(jnp.broadcast_to(scale_sums[...], (8, lanes)))[0:1, :128]
    small = [folded(d_qn, q_hat[...]), folded(d_kn, k_hat[...]), by_head]
    small.append(jnp.zeros((1, width - 384), F32))
    small = jnp.concatenate(small, axis=1)
    high, low = halves(small)
    lowest = (small - high.astype(F32) - low.astype(F32)).astype(BF)
    spare = [high.astype(F32), low.astype(F32), lowest.astype(F32)]
    if padded - count > 3:
        spare.append(jnp.zeros((padded - count - 3, width), F32))
    spare = jnp.concatenate(spare, axis=0)
    for f in range(frames):
        tokens = out[f * padded : f * padded + count]
        d_mid[f] = jnp.concatenate([tokens, spare], axis=0).astype(BF)


def call(kernel, mebibytes, outs, scratch, *args):
    smem = pl.BlockSpec(memory_space=pltpu.SMEM)
    vmem = pl.BlockSpec(memory_space=pltpu.VMEM)
    return pl.pallas_call(
        kernel,
        out_shape=[jax.ShapeDtypeStruct(shape, dtype) for shape, dtype in outs],
        in_specs=[smem if arg.dtype == jnp.int32 else vmem for arg in args],
        out_specs=[vmem] * len(outs),
        scratch_shapes=[pltpu.VMEM(shape, dtype) for shape, dtype in scratch],
        compiler_params=pltpu.CompilerParams(vmem_limit_bytes=mebibytes << 20),
    )(*args)


def local(
    clip_input, cotangent, norm_gain, conv_weight, attn_weight, query_gain, key_gain, logit_scale
):
    source = clip_input[0, 0]
    cot = cotangent[0, 0]
    rows, cols, width = source.shape
    heads = logit_scale.shape[0]
    depth = width // heads
    tokens = rows * cols
    clips, frames, tiles = (lax.axis_size(name) for name in ("dp", "frame", "tile"))
    square = ("frame", "tile")
    ranks = frames * tiles
    share = conv_weight.shape[1]
    count = tokens // frames
    third = count // 3
    part = width // 8
    x = lax.axis_index("dp") % 2
    core = lax.axis_index("frame") % 2
    tile = lax.axis_index("tile")
    plane = lax.axis_index("frame") // 2
    place = jnp.stack([x, core, tile, 4 * x + 2 * core + tile, plane]).astype(jnp.int32)
    flat = source.reshape(tokens, width)

    mine = lax.dynamic_slice_in_dim(conv_weight, x * (width // 2), width // 2, axis=2)
    mine = mine.reshape(3, 3, share, 4, part).transpose(3, 0, 2, 1, 4)
    mine = mine.reshape(4, 3, share, 3 * part)
    mine, _ = lax.optimization_barrier((mine, swap(flat[:8, :128], "dp")))
    spread_out = jnp.broadcast_to(mine[None], (frames // 2,) + mine.shape)
    conv_in = lax.all_to_all(spread_out.reshape((ranks,) + mine.shape[1:]), square, 0, 0, tiled=True)
    conv_full = conv_in.transpose(1, 0, 2, 3).reshape(3, width, 3 * part)
    attn_full = lax.all_gather(attn_weight, square, axis=0, tiled=True)

    half = tokens // 2
    along_x = swap(flat, "dp")
    along_y = swap(flat, "tile")
    across = jnp.concatenate([swap(along_x[:half], "tile"), swap(along_y[half:], "dp")])
    pieces = [flat, along_y, along_x, across]
    pieces += [swap(piece, "frame") for piece in pieces]
    acts, kept = call(
        functools.partial(act_kernel, cols=cols, part=part),
        20,
        [((4, tiles * tokens + 2 * cols, width), BF), ((4, tiles * tokens, part), BF)],
        [],
        place,
        norm_gain[None],
        *pieces,
    )

    blocked = (2 * ranks, 2 * third, 3 * part)
    plain = (2, 2, tiles * tokens, part)
    (mid,) = call(
        functools.partial(conv_kernel, cols=cols, part=part, blocks=frames, count=count),
        16,
        [(plain if frames > 8 else blocked, BF)],
        [],
        place,
        conv_full,
        acts,
        kept,
    )
    if frames > 8:
        mid = mid.reshape(2, 2, tiles, frames, 3, third, part).transpose(0, 3, 2, 1, 5, 4, 6)
        mid = mid.reshape(blocked)
    groups = None
    if clips > 2:
        groups = [[2 * ranks * g + i for i in range(2 * ranks)] for g in range(clips // 2)]
    mid = lax.all_to_all(mid, ("dp",) + square, 0, 0, axis_index_groups=groups, tiled=True)

    cot_blocks, mid = lax.optimization_barrier((cot.reshape(frames, count, width), mid))
    cot_blocks = lax.all_to_all(cot_blocks, "frame", 0, 0, tiled=True)

    lanes = frames * SLOT
    padded = round_up(count + 3, 8)
    total = frames * padded
    scale = jnp.tile(jnp.pad(logit_scale, (0, SLOT - heads)), frames)[None]
    qgain = jnp.tile(query_gain, heads)[None]
    kgain = jnp.tile(key_gain, heads)[None]
    full = (total, width)
    double = (2 * total, width)
    narrow = (total, lanes)
    mid, q_hat, k_hat, q_rstd, k_rstd, value, raw, probs, mixed = call(
        functools.partial(attend_kernel, heads=heads, count=count, padded=padded, part=part),
        20,
        [
            (full, BF), (full, F32), (full, F32), (narrow, F32), (narrow, F32),
            (full, BF), (narrow, F32), (narrow, F32), (full, BF),
        ],
        [(full, F32), (double, F32), (full, F32), (narrow, F32)],
        mid, attn_full, qgain, kgain, scale,
    )
    grads, scale_sums, d_raw, d_value = call(
        functools.partial(middle_kernel, heads=heads, count=count, padded=padded),
        20,
        [
            ((2, 2, 2, frames // 2, share, width), BF),
            ((1, lanes), F32), (narrow, F32), (full, BF),
        ],
        [(full, F32), (double, F32), (double, F32), (narrow, F32)],
        place, cot_blocks, attn_full, mid, mixed, value, raw, probs, scale,
    )
    (d_mid,) = call(
        functools.partial(back_kernel, heads=heads, count=count, padded=padded),
        20,
        [((frames, padded, width), BF)],
        [(double, F32), (double, F32), (full, F32)],
        d_raw, q_hat, k_hat, q_rstd, k_rstd, d_value, attn_full, qgain, kgain, scale_sums,
    )

    def add(mine, theirs):
        return (mine.astype(F32) + theirs.astype(F32)).astype(BF)

    shares = add(grads[:, 0], swap(grads[:, 1], "frame"))
    shares = add(shares[0], swap(shares[1], "dp"))
    shares = add(shares[0], swap(shares[1], "tile"))
    step = frames // 4
    while step > 0:
        pairs = [(i, i ^ (2 * step)) for i in range(frames)]
        shares = add(shares[:step], lax.ppermute(shares[step:], "frame", pairs))
        step //= 2
    shares = shares[0]
    d_back = lax.all_to_all(d_mid, "frame", 0, 0, tiled=True)
    small = jnp.sum(d_back[:, count : count + 3].astype(F32), axis=(0, 1))
    d_back = d_back[:, :count].reshape(rows, cols, width)
    mid_grad = (cot.astype(F32) + d_back.astype(F32)).astype(BF)

    small = small + swap(small, "tile")
    if clips == 2:
        small = small + swap(small, "dp")
    else:
        small = lax.psum(small, "dp")
        same_clip = [[i for i in range(clips) if i % 2 == c] for c in (0, 1)]
        shares = lax.psum(shares, "dp", axis_index_groups=same_clip)
    theirs = swap(shares, "dp").astype(F32)
    shares = shares.astype(F32)
    factor = 1.0 / math.sqrt(clips * frames * tiles * tokens)
    value_grad = jnp.where(x == 0, shares, theirs) * factor
    out_proj_grad = jnp.where(x == 0, theirs, shares) * factor
    scale_sum = small[256 : 256 + heads]
    return (
        mid_grad[None, None],
        value_grad,
        out_proj_grad,
        small[:depth] * factor,
        small[128 : 128 + depth] * factor,
        scale_sum * factor,
    )


def solution(mesh):
    in_specs = (
        P("dp", "frame", "tile", None, None),
        P("dp", "frame", "tile", None, None),
        P(),
        P(None, ("frame", "tile"), None),
        P(("frame", "tile"), None),
        P(),
        P(),
        P(),
    )
    out_specs = (
        P("dp", "frame", "tile", None, None),
        P(("frame", "tile"), None),
        P(("frame", "tile"), None),
        P(),
        P(),
        P(),
    )
    return jax.shard_map(local, mesh=mesh, in_specs=in_specs, out_specs=out_specs, check_vma=False)
```

```python
import functools
import math

import jax
import jax.numpy as jnp
from jax import lax
from jax.experimental import pallas as pl
from jax.experimental.pallas import tpu as pltpu
from jax.sharding import PartitionSpec as P

GROUPS = 32
EPS = 1e-05
SLOT = 16
BF = jnp.bfloat16
F32 = jnp.float32


def swap(x, axis):
    return lax.ppermute(x, axis, [(i, i ^ 1) for i in range(lax.axis_size(axis))])


def round_up(value, unit):
    return -(-value // unit) * unit


def dot(a, b):
    return lax.dot_general(a, b, (((1,), (0,)), ((), ())), preferred_element_type=F32)


def dot_t(a, b):
    return lax.dot_general(a, b, (((1,), (1,)), ((), ())), preferred_element_type=F32)


def dot_rows(a, b):
    return lax.dot_general(a, b, (((0,), (0,)), ((), ())), preferred_element_type=F32)


def halves(x):
    high = x.astype(BF)
    return high, (x - high.astype(F32)).astype(BF)


def picker(rows, cols, depth, offset):
    row = lax.broadcasted_iota(jnp.int32, (rows, cols), 0)
    col = lax.broadcasted_iota(jnp.int32, (rows, cols), 1)
    return (col - row // depth == offset).astype(F32).astype(BF)


def spreader(rows, cols, depth, offset):
    row = lax.broadcasted_iota(jnp.int32, (rows, cols), 0)
    col = lax.broadcasted_iota(jnp.int32, (rows, cols), 1)
    return (row - col // depth == offset).astype(F32).astype(BF)


def head_sums(x, pick):
    high, low = halves(x)
    return dot(high, pick) + dot(low, pick)


def spread(x, both):
    high, low = halves(x)
    return dot(jnp.concatenate([high, low], axis=1), both)


def over_slots(x):
    step = SLOT
    while step < x.shape[1]:
        x = x + pltpu.roll(x, step, 1)
        step *= 2
    return x


def each(number, body):
    if number > 8:
        lax.fori_loop(0, number, lambda i, _: body(i), None)
    else:
        for i in range(number):
            body(i)


def act_kernel(place, gain, *refs, cols, part):
    blocks, (acts, kept) = (refs[:-2], refs[-2:])
    half, width = blocks[0].shape
    tile, chosen = (place[2], place[3])
    choice = picker(width, part, 1, -part * chosen)
    per_group = width // GROUPS
    pick = picker(width, 128, per_group, 0)
    back = spreader(128, width, per_group, 0)

    def thirds(x):
        high, low = halves(x)
        return high, low, (x - high.astype(F32) - low.astype(F32)).astype(BF)

    totals, squares = ([], [])
    for frame in range(4):
        total, square = (0.0, 0.0)
        for dy in (0, 1):
            x = blocks[2 * frame + dy][...]
            start = pl.multiple_of((tile ^ dy) * half, half)
            kept[frame, pl.ds(start, half), :] = dot(x, choice).astype(BF)
            x = x.astype(F32)
            total = total + jnp.sum(x, axis=0, keepdims=True)
            square = square + jnp.sum(x * x, axis=0, keepdims=True)
        totals.append(total)
        squares.append(square)
    high, low, lowest = thirds(jnp.concatenate(totals + squares, axis=0))
    both = (dot(high, pick) + dot(low, pick) + dot(lowest, pick)) / (2 * half * per_group)
    mean = both[0:4]
    rstd = lax.rsqrt(both[4:8] - mean * mean + EPS)
    high, low, lowest = thirds(jnp.concatenate([mean, rstd], axis=0))
    both = dot(high, back) + dot(low, back) + dot(lowest, back)
    scales = both[4:8] * gain[...]
    for frame in range(4):
        acts[frame, pl.ds(0, cols), :] = jnp.zeros((cols, width), BF)
        acts[frame, pl.ds(cols + 2 * half, cols), :] = jnp.zeros((cols, width), BF)
        for dy in (0, 1):
            x = blocks[2 * frame + dy][...].astype(F32)
            zed = (x - both[frame : frame + 1]) * scales[frame : frame + 1]
            start = pl.multiple_of(cols + (tile ^ dy) * half, cols)
            acts[frame, pl.ds(start, half), :] = (zed / (1.0 + jnp.exp(-zed))).astype(BF)


def conv_kernel(place, weights, acts, kept, out, *, cols, part, blocks, count):
    x, core = (place[0], place[1])
    whole = kept.shape[1]
    half = whole // 2
    third = count // 3
    col = lax.broadcasted_iota(jnp.int32, (whole, part), 0) % cols
    for dx in (0, 1):
        mids = []
        for dc in (0, 1):
            frame = 2 * dc + dx
            taps = dot(acts[frame, pl.ds(0, whole), :], weights[0])
            taps += dot(acts[frame, pl.ds(cols, whole), :], weights[1])
            taps += dot(acts[frame, pl.ds(2 * cols, whole), :], weights[2])
            left = pltpu.roll(taps[:, :part], 1, 0)
            right = pltpu.roll(taps[:, 2 * part :], whole - 1, 0)
            pre = taps[:, part : 2 * part] + jnp.where(col > 0, left, 0.0)
            pre = pre + jnp.where(col < cols - 1, right, 0.0)
            mids.append((kept[frame].astype(F32) + pre).astype(BF))
        if blocks > 8:
            for dc in (0, 1):
                out[x ^ dx, dc] = mids[dc]
            continue
        for f in range(blocks):
            for t in (0, 1):
                start = t * half + f * count
                rows = [
                    jnp.concatenate(
                        [mid[start + third * j : start + third * (j + 1)] for j in range(3)], axis=1
                    )
                    for mid in mids
                ]
                index = ((x ^ dx) * blocks + f) * 2 + t
                out[index] = jnp.concatenate(rows, axis=0)


def attend_kernel(
    place, mid_in, cot_in, weights, qgain, kgain, scale,
    kept, sent, sums, d_raw, q_hat, k_hat, q_rstd, k_rstd, d_value,
    mid_s, cot_s, doubled, doubled_v, mixed_s, raw_s, probs_s,
    *, heads, count, padded, part,
):
    total, width = mid_s.shape
    frames = total // padded
    depth = width // heads
    lanes = scale.shape[-1]
    third = count // 3
    x, core, tile, plane = (place[0], place[1], place[2], place[4])
    mid_s[...] = jnp.zeros_like(mid_s)
    cot_s[...] = jnp.zeros_like(cot_s)
    for z in range(frames // 2):
        for e in (0, 1):
            f = 2 * z + e
            blocks = [
                mid_in[(x * frames + 2 * z + c) * 2 + t, pl.ds((e ^ c) * third, third), :]
                for x in (0, 1)
                for c in (0, 1)
                for t in (0, 1)
            ]
            for j in range(3):
                piece = [b[:, j * part : (j + 1) * part] for b in blocks]
                start = f * padded + j * third
                mid_s[pl.ds(start, third), :] = jnp.concatenate(piece, axis=1).astype(F32)
            cot_s[pl.ds(f * padded, count), :] = cot_in[f].astype(F32)
    mid = mid_s[...].astype(BF)
    cot = cot_s[...].astype(BF)
    pick = picker(width, lanes, depth, 0)
    both = jnp.concatenate([spreader(lanes, width, depth, 0)] * 2, axis=0)

    def stats(vec):
        cent = vec - spread(head_sums(vec, pick) / depth, both)
        var = head_sums(cent * cent, pick) / depth
        rstd = lax.rsqrt(var + EPS)
        return cent * spread(rstd, both), rstd

    hat, rstd = stats(dot(mid, weights[:, pl.ds(0, width)]))
    q_hat[...] = hat
    q_rstd[...] = rstd
    q_norm = hat * qgain[...]
    hat, rstd = stats(dot(mid, weights[:, pl.ds(width, width)]))
    k_hat[...] = hat
    k_rstd[...] = rstd
    hat = hat * kgain[...]
    doubled[pl.ds(0, total), :] = hat
    doubled[pl.ds(total, total), :] = hat
    value = dot(mid, weights[:, pl.ds(2 * width, width)]).astype(BF).astype(F32)
    doubled_v[pl.ds(0, total), :] = value
    doubled_v[pl.ds(total, total), :] = value
    d_mixed = dot_t(cot, weights[:, pl.ds(3 * width, width)]).astype(BF).astype(F32)
    raw_s[...] = jnp.zeros_like(raw_s)
    probs_s[...] = jnp.zeros_like(probs_s)

    def logits(s):
        here = picker(width, lanes, depth, SLOT * s)
        raw_s[...] += head_sums(q_norm * doubled[pl.ds(s * padded, total), :], here)
        probs_s[...] += head_sums(d_mixed * doubled_v[pl.ds(s * padded, total), :], here)

    each(frames, logits)
    raw = raw_s[...] / math.sqrt(depth)
    expo = jnp.exp(raw * scale[...])
    probs = expo / over_slots(expo)
    probs_b = probs.astype(BF)
    d_probs = probs_s[...]
    d_logits = probs * (d_probs - over_slots(probs * d_probs))
    sums[...] = jnp.sum(d_logits * raw, axis=0, keepdims=True)
    d_raw[...] = d_logits * scale[...] / math.sqrt(depth)
    mixed_s[...] = jnp.zeros_like(mixed_s)
    doubled[...] = jnp.zeros_like(doubled)

    def mix(s):
        weight = dot(probs_b, spreader(lanes, width, depth, SLOT * s))
        mixed_s[...] += weight * doubled_v[pl.ds(s * padded, total), :]
        doubled[pl.ds(s * padded, total), :] += weight * d_mixed

    each(frames, mix)
    dv = (doubled[pl.ds(0, total), :] + doubled[pl.ds(total, total), :]).astype(BF)
    d_value[...] = dv
    rows = kept.shape[3]

    def store(kind, term):
        for z in range(frames // 2):
            for t in (0, 1):
                start = (4 * z + t) * rows
                first = term[start : start + rows]
                second = term[start + 2 * rows : start + 3 * rows]
                kept[x ^ kind, tile ^ t, plane ^ z] = jnp.where(core == 0, first, second)
                sent[x ^ kind, tile ^ t, plane ^ z] = jnp.where(core == 0, second, first)

    store(1, dot_rows(mixed_s[...].astype(BF), cot).astype(BF))
    store(0, dot_rows(mid, dv).astype(BF))


def slope_kernel(
    d_raw, q_hat, k_hat, qgain, kgain,
    d_qn, d_kn,
    doubled, doubled_acc,
    *, heads, padded,
):
    total, width = q_hat.shape
    depth = width // heads
    frames = total // padded
    lanes = d_raw.shape[-1]
    k_norm = k_hat[...] * kgain[...]
    doubled[pl.ds(0, total), :] = k_norm
    doubled[pl.ds(total, total), :] = k_norm
    q_norm = q_hat[...] * qgain[...]
    doubled_acc[...] = jnp.zeros_like(doubled_acc)
    d_qn[...] = jnp.zeros_like(d_qn)
    high, low = halves(d_raw[...])
    pair = jnp.concatenate([high, low], axis=1)

    def shift(s):
        one = spreader(lanes, width, depth, SLOT * s)
        weight = dot(pair, jnp.concatenate([one, one], axis=0))
        d_qn[...] += weight * doubled[pl.ds(s * padded, total), :]
        doubled_acc[pl.ds(s * padded, total), :] += weight * q_norm

    each(frames, shift)
    d_kn[...] = doubled_acc[pl.ds(0, total), :] + doubled_acc[pl.ds(total, total), :]


def back_kernel(
    d_qn, d_kn, q_hat, k_hat, q_rstd, k_rstd, d_value, weights, qgain, kgain, scale_sums,
    d_mid,
    *, heads, count, padded,
):
    total, width = q_hat.shape
    depth = width // heads
    frames = total // padded
    lanes = scale_sums.shape[-1]
    pick = picker(width, lanes, depth, 0)
    both = jnp.concatenate([spreader(lanes, width, depth, 0)] * 2, axis=0)

    def back(dhat, hat, rstd):
        first = spread(head_sums(dhat, pick) / depth, both)
        second = spread(head_sums(dhat * hat, pick) / depth, both)
        return (spread(rstd, both) * (dhat - first - hat * second)).astype(BF)

    d_query = back(d_qn[...] * qgain[...], q_hat[...], q_rstd[...])
    d_key = back(d_kn[...] * kgain[...], k_hat[...], k_rstd[...])
    out = dot_t(d_query, weights[:, pl.ds(0, width)])
    out += dot_t(d_key, weights[:, pl.ds(width, width)])
    out += dot_t(d_value[...], weights[:, pl.ds(2 * width, width)])

    row = lax.broadcasted_iota(jnp.int32, (width, 128), 0)
    col = lax.broadcasted_iota(jnp.int32, (width, 128), 1)
    fold = (row % depth == col).astype(F32)

    def folded(d_norm, hat):
        sums = jnp.sum(d_norm * hat, axis=0, keepdims=True)
        sums = jnp.broadcast_to(sums, (8, width))
        return jnp.dot(sums, fold, precision=lax.Precision.HIGHEST, preferred_element_type=F32)[0:1]

    by_head = over_slots(jnp.broadcast_to(scale_sums[...], (8, lanes)))[0:1, :128]
    small = [folded(d_qn[...], q_hat[...]), folded(d_kn[...], k_hat[...]), by_head]
    small.append(jnp.zeros((1, width - 384), F32))
    small = jnp.concatenate(small, axis=1)
    high, low = halves(small)
    lowest = (small - high.astype(F32) - low.astype(F32)).astype(BF)
    spare = [high.astype(F32), low.astype(F32), lowest.astype(F32)]
    if padded - count > 3:
        spare.append(jnp.zeros((padded - count - 3, width), F32))
    spare = jnp.concatenate(spare, axis=0)
    for f in range(frames):
        tokens = out[f * padded : f * padded + count]
        d_mid[f] = jnp.concatenate([tokens, spare], axis=0).astype(BF)


def call(kernel, mebibytes, outs, scratch, *args):
    smem = pl.BlockSpec(memory_space=pltpu.SMEM)
    vmem = pl.BlockSpec(memory_space=pltpu.VMEM)
    return pl.pallas_call(
        kernel,
        out_shape=[jax.ShapeDtypeStruct(shape, dtype) for shape, dtype in outs],
        in_specs=[smem if arg.dtype == jnp.int32 else vmem for arg in args],
        out_specs=[vmem] * len(outs),
        scratch_shapes=[pltpu.VMEM(shape, dtype) for shape, dtype in scratch],
        compiler_params=pltpu.CompilerParams(vmem_limit_bytes=mebibytes << 20),
    )(*args)


def local(
    clip_input, cotangent, norm_gain, conv_weight, attn_weight, query_gain, key_gain, logit_scale
):
    source = clip_input[0, 0]
    cot = cotangent[0, 0]
    rows, cols, width = source.shape
    heads = logit_scale.shape[0]
    depth = width // heads
    tokens = rows * cols
    clips, frames, tiles = (lax.axis_size(name) for name in ("dp", "frame", "tile"))
    square = ("frame", "tile")
    ranks = frames * tiles
    share = conv_weight.shape[1]
    count = tokens // frames
    third = count // 3
    part = width // 8
    x = lax.axis_index("dp") % 2
    core = lax.axis_index("frame") % 2
    tile = lax.axis_index("tile")
    plane = lax.axis_index("frame") // 2
    place = jnp.stack([x, core, tile, 4 * x + 2 * core + tile, plane]).astype(jnp.int32)
    flat = source.reshape(tokens, width)

    mine = lax.dynamic_slice_in_dim(conv_weight, x * (width // 2), width // 2, axis=2)
    mine = mine.reshape(3, 3, share, 4, part).transpose(3, 0, 2, 1, 4)
    mine = mine.reshape(4, 3, share, 3 * part)
    spread_out = jnp.broadcast_to(mine[None], (frames // 2,) + mine.shape)
    conv_in = lax.all_to_all(spread_out.reshape((ranks,) + mine.shape[1:]), square, 0, 0, tiled=True)
    cot_blocks, conv_in = lax.optimization_barrier((cot.reshape(frames, count, width), conv_in))
    cot_blocks = lax.all_to_all(cot_blocks, "frame", 0, 0, tiled=True)
    conv_full = conv_in.transpose(1, 0, 2, 3).reshape(3, width, 3 * part)
    attn_full = lax.all_gather(attn_weight, square, axis=0, tiled=True)

    half = tokens // 2
    along_x = swap(flat, "dp")
    along_y = swap(flat, "tile")
    across = jnp.concatenate([swap(along_x[:half], "tile"), swap(along_y[half:], "dp")])
    pieces = [flat, along_y, along_x, across]
    pieces += [swap(piece, "frame") for piece in pieces]
    acts, kept = call(
        functools.partial(act_kernel, cols=cols, part=part),
        20,
        [((4, tiles * tokens + 2 * cols, width), BF), ((4, tiles * tokens, part), BF)],
        [],
        place,
        norm_gain[None],
        *pieces,
    )

    blocked = (2 * ranks, 2 * third, 3 * part)
    plain = (2, 2, tiles * tokens, part)
    (mid,) = call(
        functools.partial(conv_kernel, cols=cols, part=part, blocks=frames, count=count),
        16,
        [(plain if frames > 8 else blocked, BF)],
        [],
        place,
        conv_full,
        acts,
        kept,
    )
    if frames > 8:
        mid = mid.reshape(2, 2, tiles, frames, 3, third, part).transpose(0, 3, 2, 1, 5, 4, 6)
        mid = mid.reshape(blocked)
    groups = None
    if clips > 2:
        groups = [[2 * ranks * g + i for i in range(2 * ranks)] for g in range(clips // 2)]
    mid, cot_blocks = lax.optimization_barrier((mid, cot_blocks))
    mid = lax.all_to_all(mid, ("dp",) + square, 0, 0, axis_index_groups=groups, tiled=True)

    lanes = frames * SLOT
    padded = round_up(count + 3, 8)
    total = frames * padded
    scale = jnp.tile(jnp.pad(logit_scale, (0, SLOT - heads)), frames)[None]
    qgain = jnp.tile(query_gain, heads)[None]
    kgain = jnp.tile(key_gain, heads)[None]
    full = (total, width)
    double = (2 * total, width)
    narrow = (total, lanes)
    kept, sent, scale_sums, d_raw, q_hat, k_hat, q_rstd, k_rstd, d_value = call(
        functools.partial(attend_kernel, heads=heads, count=count, padded=padded, part=part),
        20,
        [
            ((2, 2, frames // 2, share, width), BF),
            ((2, 2, frames // 2, share, width), BF),
            ((1, lanes), F32), (narrow, F32),
            (full, F32), (full, F32), (narrow, F32), (narrow, F32), (full, BF),
        ],
        [
            (full, F32), (full, F32), (double, F32), (double, F32), (full, F32),
            (narrow, F32), (narrow, F32),
        ],
        place, mid, cot_blocks, attn_full, qgain, kgain, scale,
    )
    d_qn, d_kn = call(
        functools.partial(slope_kernel, heads=heads, padded=padded),
        16,
        [(full, F32), (full, F32)],
        [(double, F32), (double, F32)],
        d_raw, q_hat, k_hat, qgain, kgain,
    )

    def add(mine, theirs):
        return (mine.astype(F32) + theirs.astype(F32)).astype(BF)

    shares = add(kept, swap(sent, "frame"))
    shares, d_qn = lax.optimization_barrier((shares, d_qn))
    (d_mid,) = call(
        functools.partial(back_kernel, heads=heads, count=count, padded=padded),
        16,
        [((frames, padded, width), BF)],
        [],
        d_qn, d_kn, q_hat, k_hat, q_rstd, k_rstd, d_value, attn_full, qgain, kgain, scale_sums,
    )
    shares = add(shares[0], swap(shares[1], "dp"))
    shares = add(shares[0], swap(shares[1], "tile"))
    step = frames // 4
    while step > 0:
        pairs = [(i, i ^ (2 * step)) for i in range(frames)]
        shares = add(shares[:step], lax.ppermute(shares[step:], "frame", pairs))
        step //= 2
    shares = shares[0]
    d_back = lax.all_to_all(d_mid, "frame", 0, 0, tiled=True)
    small = jnp.sum(d_back[:, count : count + 3].astype(F32), axis=(0, 1))
    d_back = d_back[:, :count].reshape(rows, cols, width)
    mid_grad = (cot.astype(F32) + d_back.astype(F32)).astype(BF)

    small = small + swap(small, "tile")
    if clips == 2:
        small = small + swap(small, "dp")
    else:
        small = lax.psum(small, "dp")
        same_clip = [[i for i in range(clips) if i % 2 == c] for c in (0, 1)]
        shares = lax.psum(shares, "dp", axis_index_groups=same_clip)
    theirs = swap(shares, "dp").astype(F32)
    shares = shares.astype(F32)
    factor = 1.0 / math.sqrt(clips * frames * tiles * tokens)
    value_grad = jnp.where(x == 0, shares, theirs) * factor
    out_proj_grad = jnp.where(x == 0, theirs, shares) * factor
    scale_sum = small[256 : 256 + heads]
    return (
        mid_grad[None, None],
        value_grad,
        out_proj_grad,
        small[:depth] * factor,
        small[128 : 128 + depth] * factor,
        scale_sum * factor,
    )


def solution(mesh):
    in_specs = (
        P("dp", "frame", "tile", None, None),
        P("dp", "frame", "tile", None, None),
        P(),
        P(None, ("frame", "tile"), None),
        P(("frame", "tile"), None),
        P(),
        P(),
        P(),
    )
    out_specs = (
        P("dp", "frame", "tile", None, None),
        P(("frame", "tile"), None),
        P(("frame", "tile"), None),
        P(),
        P(),
        P(),
    )
    return jax.shard_map(local, mesh=mesh, in_specs=in_specs, out_specs=out_specs, check_vma=False)
```

```python
import functools
import math

import jax
import jax.numpy as jnp
from jax import lax
from jax.experimental import pallas as pl
from jax.experimental.pallas import tpu as pltpu
from jax.sharding import PartitionSpec as P

GROUPS = 32
EPS = 1e-05
SLOT = 16
BF = jnp.bfloat16
F32 = jnp.float32


def swap(x, axis):
    return lax.ppermute(x, axis, [(i, i ^ 1) for i in range(lax.axis_size(axis))])


def round_up(value, unit):
    return -(-value // unit) * unit


def dot(a, b):
    return lax.dot_general(a, b, (((1,), (0,)), ((), ())), preferred_element_type=F32)


def dot_t(a, b):
    return lax.dot_general(a, b, (((1,), (1,)), ((), ())), preferred_element_type=F32)


def dot_rows(a, b):
    return lax.dot_general(a, b, (((0,), (0,)), ((), ())), preferred_element_type=F32)


def halves(x):
    high = x.astype(BF)
    return high, (x - high.astype(F32)).astype(BF)


def picker(rows, cols, depth, offset):
    row = lax.broadcasted_iota(jnp.int32, (rows, cols), 0)
    col = lax.broadcasted_iota(jnp.int32, (rows, cols), 1)
    return (col - row // depth == offset).astype(F32).astype(BF)


def spreader(rows, cols, depth, offset):
    row = lax.broadcasted_iota(jnp.int32, (rows, cols), 0)
    col = lax.broadcasted_iota(jnp.int32, (rows, cols), 1)
    return (row - col // depth == offset).astype(F32).astype(BF)


def head_sums(x, pick):
    high, low = halves(x)
    return dot(high, pick) + dot(low, pick)


def spread(x, both):
    high, low = halves(x)
    return dot(jnp.concatenate([high, low], axis=1), both)


def over_slots(x):
    step = SLOT
    while step < x.shape[1]:
        x = x + pltpu.roll(x, step, 1)
        step *= 2
    return x


def each(number, body):
    if number > 8:
        lax.fori_loop(0, number, lambda i, _: body(i), None)
    else:
        for i in range(number):
            body(i)


def pack_kernel(place, weights, cot, out):
    share, width = (weights.shape[0], cot.shape[1])
    frames = out.shape[0]
    count = cot.shape[0] // frames
    x = place[0]
    chosen = [
        jnp.where(x == 0, weights[:, pl.ds(c * width, width)], weights[:, pl.ds((2 + c) * width, width)])
        for c in (0, 1)
    ]
    for f in range(frames):
        out[f, pl.ds(0, share), :] = chosen[f % 2]
        out[f, pl.ds(share, count), :] = cot[pl.ds(f * count, count), :]


def join_kernel(place, *refs):
    pieces, out = (refs[:-1], refs[-1])
    x, core, tile = (place[0], place[1], place[2])
    frames = out.shape[1]
    for dc in (0, 1):
        own, by_tile, by_clip, low, high = pieces[5 * dc : 5 * dc + 5]
        own_kind = 2 * x + (core ^ dc)
        other_kind = 2 * (x ^ 1) + (core ^ dc)
        for f in range(frames):
            out[own_kind, f, tile] = own[f]
            out[own_kind, f, tile ^ 1] = by_tile[f]
            out[other_kind, f, tile] = by_clip[f]
            part, index = (low, f) if f < frames // 2 else (high, f - frames // 2)
            out[other_kind, f, tile ^ 1] = part[index]


def act_kernel(place, gain, *refs, cols, part):
    blocks, (acts, kept) = (refs[:-2], refs[-2:])
    half, width = blocks[0].shape
    tile, chosen = (place[2], place[3])
    choice = picker(width, part, 1, -part * chosen)
    per_group = width // GROUPS
    pick = picker(width, 128, per_group, 0)
    back = spreader(128, width, per_group, 0)

    def thirds(x):
        high, low = halves(x)
        return high, low, (x - high.astype(F32) - low.astype(F32)).astype(BF)

    totals, squares = ([], [])
    for frame in range(4):
        total, square = (0.0, 0.0)
        for dy in (0, 1):
            x = blocks[2 * frame + dy][...]
            start = pl.multiple_of((tile ^ dy) * half, half)
            kept[frame, pl.ds(start, half), :] = dot(x, choice).astype(BF)
            x = x.astype(F32)
            total = total + jnp.sum(x, axis=0, keepdims=True)
            square = square + jnp.sum(x * x, axis=0, keepdims=True)
        totals.append(total)
        squares.append(square)
    high, low, lowest = thirds(jnp.concatenate(totals + squares, axis=0))
    both = (dot(high, pick) + dot(low, pick) + dot(lowest, pick)) / (2 * half * per_group)
    mean = both[0:4]
    rstd = lax.rsqrt(both[4:8] - mean * mean + EPS)
    high, low, lowest = thirds(jnp.concatenate([mean, rstd], axis=0))
    both = dot(high, back) + dot(low, back) + dot(lowest, back)
    scales = both[4:8] * gain[...]
    for frame in range(4):
        acts[frame, pl.ds(0, cols), :] = jnp.zeros((cols, width), BF)
        acts[frame, pl.ds(cols + 2 * half, cols), :] = jnp.zeros((cols, width), BF)
        for dy in (0, 1):
            x = blocks[2 * frame + dy][...].astype(F32)
            zed = (x - both[frame : frame + 1]) * scales[frame : frame + 1]
            start = pl.multiple_of(cols + (tile ^ dy) * half, cols)
            acts[frame, pl.ds(start, half), :] = (zed / (1.0 + jnp.exp(-zed))).astype(BF)


def conv_kernel(place, weights, acts, kept, out, *, cols, part, blocks, count):
    x, core = (place[0], place[1])
    whole = kept.shape[1]
    half = whole // 2
    third = count // 3
    col = lax.broadcasted_iota(jnp.int32, (whole, part), 0) % cols
    for dx in (0, 1):
        mids = []
        for dc in (0, 1):
            frame = 2 * dc + dx
            taps = dot(acts[frame, pl.ds(0, whole), :], weights[0])
            taps += dot(acts[frame, pl.ds(cols, whole), :], weights[1])
            taps += dot(acts[frame, pl.ds(2 * cols, whole), :], weights[2])
            left = pltpu.roll(taps[:, :part], 1, 0)
            right = pltpu.roll(taps[:, 2 * part :], whole - 1, 0)
            pre = taps[:, part : 2 * part] + jnp.where(col > 0, left, 0.0)
            pre = pre + jnp.where(col < cols - 1, right, 0.0)
            mids.append((kept[frame].astype(F32) + pre).astype(BF))
        if blocks > 8:
            for dc in (0, 1):
                out[x ^ dx, dc] = mids[dc]
            continue
        for f in range(blocks):
            for t in (0, 1):
                start = t * half + f * count
                rows = [
                    jnp.concatenate(
                        [mid[start + third * j : start + third * (j + 1)] for j in range(3)], axis=1
                    )
                    for mid in mids
                ]
                index = ((x ^ dx) * blocks + f) * 2 + t
                out[index] = jnp.concatenate(rows, axis=0)


def attend_kernel(
    place, mid_in, cot_in, weights, qgain, kgain, scale,
    kept, sent, sums, d_raw, q_hat, k_hat, q_rstd, k_rstd, d_value,
    mid_s, cot_s, doubled, doubled_v, mixed_s, raw_s, probs_s,
    *, heads, count, padded, part,
):
    total, width = mid_s.shape
    frames = total // padded
    depth = width // heads
    lanes = scale.shape[-1]
    third = count // 3
    share = kept.shape[3]
    x, core, tile, plane = (place[0], place[1], place[2], place[4])
    mid_s[...] = jnp.zeros_like(mid_s)
    cot_s[...] = jnp.zeros_like(cot_s)
    for z in range(frames // 2):
        for e in (0, 1):
            f = 2 * z + e
            blocks = [
                mid_in[(x * frames + 2 * z + c) * 2 + t, pl.ds((e ^ c) * third, third), :]
                for x in (0, 1)
                for c in (0, 1)
                for t in (0, 1)
            ]
            for j in range(3):
                piece = [b[:, j * part : (j + 1) * part] for b in blocks]
                start = f * padded + j * third
                mid_s[pl.ds(start, third), :] = jnp.concatenate(piece, axis=1).astype(F32)
            cot_s[pl.ds(f * padded, count), :] = cot_in[f, pl.ds(share, count), :].astype(F32)
    mid = mid_s[...].astype(BF)
    cot = cot_s[...].astype(BF)
    pick = picker(width, lanes, depth, 0)
    both = jnp.concatenate([spreader(lanes, width, depth, 0)] * 2, axis=0)

    def stats(vec):
        cent = vec - spread(head_sums(vec, pick) / depth, both)
        var = head_sums(cent * cent, pick) / depth
        rstd = lax.rsqrt(var + EPS)
        return cent * spread(rstd, both), rstd

    hat, rstd = stats(dot(mid, weights[0]))
    q_hat[...] = hat
    q_rstd[...] = rstd
    q_norm = hat * qgain[...]
    hat, rstd = stats(dot(mid, weights[1]))
    k_hat[...] = hat
    k_rstd[...] = rstd
    hat = hat * kgain[...]
    doubled[pl.ds(0, total), :] = hat
    doubled[pl.ds(total, total), :] = hat
    value = dot(mid, weights[2]).astype(BF).astype(F32)
    doubled_v[pl.ds(0, total), :] = value
    doubled_v[pl.ds(total, total), :] = value
    d_mixed = dot_t(cot, weights[3]).astype(BF).astype(F32)
    raw_s[...] = jnp.zeros_like(raw_s)
    probs_s[...] = jnp.zeros_like(probs_s)

    def logits(s):
        here = picker(width, lanes, depth, SLOT * s)
        raw_s[...] += head_sums(q_norm * doubled[pl.ds(s * padded, total), :], here)
        probs_s[...] += head_sums(d_mixed * doubled_v[pl.ds(s * padded, total), :], here)

    each(frames, logits)
    raw = raw_s[...] / math.sqrt(depth)
    expo = jnp.exp(raw * scale[...])
    probs = expo / over_slots(expo)
    probs_b = probs.astype(BF)
    d_probs = probs_s[...]
    d_logits = probs * (d_probs - over_slots(probs * d_probs))
    sums[...] = jnp.sum(d_logits * raw, axis=0, keepdims=True)
    d_raw[...] = d_logits * scale[...] / math.sqrt(depth)
    mixed_s[...] = jnp.zeros_like(mixed_s)
    doubled[...] = jnp.zeros_like(doubled)

    def mix(s):
        weight = dot(probs_b, spreader(lanes, width, depth, SLOT * s))
        mixed_s[...] += weight * doubled_v[pl.ds(s * padded, total), :]
        doubled[pl.ds(s * padded, total), :] += weight * d_mixed

    each(frames, mix)
    dv = (doubled[pl.ds(0, total), :] + doubled[pl.ds(total, total), :]).astype(BF)
    d_value[...] = dv
    rows = kept.shape[3]

    def store(kind, term):
        for z in range(frames // 2):
            for t in (0, 1):
                start = (4 * z + t) * rows
                first = term[start : start + rows]
                second = term[start + 2 * rows : start + 3 * rows]
                kept[x ^ kind, tile ^ t, plane ^ z] = jnp.where(core == 0, first, second)
                sent[x ^ kind, tile ^ t, plane ^ z] = jnp.where(core == 0, second, first)

    store(1, dot_rows(mixed_s[...].astype(BF), cot).astype(BF))
    store(0, dot_rows(mid, dv).astype(BF))


def slope_kernel(
    d_raw, q_hat, k_hat, qgain, kgain,
    d_qn, d_kn,
    doubled, doubled_acc,
    *, heads, padded,
):
    total, width = q_hat.shape
    depth = width // heads
    frames = total // padded
    lanes = d_raw.shape[-1]
    k_norm = k_hat[...] * kgain[...]
    doubled[pl.ds(0, total), :] = k_norm
    doubled[pl.ds(total, total), :] = k_norm
    q_norm = q_hat[...] * qgain[...]
    doubled_acc[...] = jnp.zeros_like(doubled_acc)
    d_qn[...] = jnp.zeros_like(d_qn)
    high, low = halves(d_raw[...])
    pair = jnp.concatenate([high, low], axis=1)

    def shift(s):
        one = spreader(lanes, width, depth, SLOT * s)
        weight = dot(pair, jnp.concatenate([one, one], axis=0))
        d_qn[...] += weight * doubled[pl.ds(s * padded, total), :]
        doubled_acc[pl.ds(s * padded, total), :] += weight * q_norm

    each(frames, shift)
    d_kn[...] = doubled_acc[pl.ds(0, total), :] + doubled_acc[pl.ds(total, total), :]


def back_kernel(
    d_qn, d_kn, q_hat, k_hat, q_rstd, k_rstd, d_value, weights, qgain, kgain, scale_sums,
    d_mid,
    *, heads, count, padded,
):
    total, width = q_hat.shape
    depth = width // heads
    frames = total // padded
    lanes = scale_sums.shape[-1]
    pick = picker(width, lanes, depth, 0)
    both = jnp.concatenate([spreader(lanes, width, depth, 0)] * 2, axis=0)

    def back(dhat, hat, rstd):
        first = spread(head_sums(dhat, pick) / depth, both)
        second = spread(head_sums(dhat * hat, pick) / depth, both)
        return (spread(rstd, both) * (dhat - first - hat * second)).astype(BF)

    d_query = back(d_qn[...] * qgain[...], q_hat[...], q_rstd[...])
    d_key = back(d_kn[...] * kgain[...], k_hat[...], k_rstd[...])
    out = dot_t(d_query, weights[0])
    out += dot_t(d_key, weights[1])
    out += dot_t(d_value[...], weights[2])

    row = lax.broadcasted_iota(jnp.int32, (width, 128), 0)
    col = lax.broadcasted_iota(jnp.int32, (width, 128), 1)
    fold = (row % depth == col).astype(F32)

    def folded(d_norm, hat):
        sums = jnp.sum(d_norm * hat, axis=0, keepdims=True)
        sums = jnp.broadcast_to(sums, (8, width))
        return jnp.dot(sums, fold, precision=lax.Precision.HIGHEST, preferred_element_type=F32)[0:1]

    by_head = over_slots(jnp.broadcast_to(scale_sums[...], (8, lanes)))[0:1, :128]
    small = [folded(d_qn[...], q_hat[...]), folded(d_kn[...], k_hat[...]), by_head]
    small.append(jnp.zeros((1, width - 384), F32))
    small = jnp.concatenate(small, axis=1)
    high, low = halves(small)
    lowest = (small - high.astype(F32) - low.astype(F32)).astype(BF)
    spare = [high.astype(F32), low.astype(F32), lowest.astype(F32)]
    if padded - count > 3:
        spare.append(jnp.zeros((padded - count - 3, width), F32))
    spare = jnp.concatenate(spare, axis=0)
    for f in range(frames):
        tokens = out[f * padded : f * padded + count]
        d_mid[f] = jnp.concatenate([tokens, spare], axis=0).astype(BF)


def call(kernel, mebibytes, outs, scratch, *args):
    smem = pl.BlockSpec(memory_space=pltpu.SMEM)
    vmem = pl.BlockSpec(memory_space=pltpu.VMEM)
    return pl.pallas_call(
        kernel,
        out_shape=[jax.ShapeDtypeStruct(shape, dtype) for shape, dtype in outs],
        in_specs=[smem if arg.dtype == jnp.int32 else vmem for arg in args],
        out_specs=[vmem] * len(outs),
        scratch_shapes=[pltpu.VMEM(shape, dtype) for shape, dtype in scratch],
        compiler_params=pltpu.CompilerParams(vmem_limit_bytes=mebibytes << 20),
    )(*args)


def local(
    clip_input, cotangent, norm_gain, conv_weight, attn_weight, query_gain, key_gain, logit_scale
):
    source = clip_input[0, 0]
    cot = cotangent[0, 0]
    rows, cols, width = source.shape
    heads = logit_scale.shape[0]
    depth = width // heads
    tokens = rows * cols
    clips, frames, tiles = (lax.axis_size(name) for name in ("dp", "frame", "tile"))
    square = ("frame", "tile")
    ranks = frames * tiles
    share = conv_weight.shape[1]
    count = tokens // frames
    third = count // 3
    part = width // 8
    x = lax.axis_index("dp") % 2
    core = lax.axis_index("frame") % 2
    tile = lax.axis_index("tile")
    plane = lax.axis_index("frame") // 2
    place = jnp.stack([x, core, tile, 4 * x + 2 * core + tile, plane]).astype(jnp.int32)
    flat = source.reshape(tokens, width)

    (packed,) = call(
        pack_kernel,
        12,
        [((frames, share + count, width), BF)],
        [],
        place,
        attn_weight,
        cot.reshape(tokens, width),
    )
    packed = lax.all_to_all(packed, "frame", 0, 0, tiled=True)
    own = packed[:, :share]
    by_tile = swap(own, "tile")
    by_clip = swap(own, "dp")
    middle = frames // 2
    parts = [own, by_tile, by_clip, swap(by_clip[:middle], "tile"), swap(by_tile[middle:], "dp")]
    parts += [swap(piece, "frame") for piece in parts]
    (attn_full,) = call(
        join_kernel, 16, [((4, frames, tiles, share, width), BF)], [], place, *parts
    )
    attn_full = attn_full.reshape(4, width, width)

    mine = lax.dynamic_slice_in_dim(conv_weight, x * (width // 2), width // 2, axis=2)
    mine = mine.reshape(3, 3, share, 4, part).transpose(3, 0, 2, 1, 4)
    mine = mine.reshape(4, 3, share, 3 * part)
    spread_out = jnp.broadcast_to(mine[None], (frames // 2,) + mine.shape)
    spread_out = spread_out.reshape((ranks,) + mine.shape[1:])
    spread_out, packed = lax.optimization_barrier((spread_out, packed))
    conv_in = lax.all_to_all(spread_out, square, 0, 0, tiled=True)
    conv_full = conv_in.transpose(1, 0, 2, 3).reshape(3, width, 3 * part)

    half = tokens // 2
    along_x = swap(flat, "dp")
    along_y = swap(flat, "tile")
    across = jnp.concatenate([swap(along_x[:half], "tile"), swap(along_y[half:], "dp")])
    pieces = [flat, along_y, along_x, across]
    pieces += [swap(piece, "frame") for piece in pieces]
    acts, kept = call(
        functools.partial(act_kernel, cols=cols, part=part),
        20,
        [((4, tiles * tokens + 2 * cols, width), BF), ((4, tiles * tokens, part), BF)],
        [],
        place,
        norm_gain[None],
        *pieces,
    )

    blocked = (2 * ranks, 2 * third, 3 * part)
    plain = (2, 2, tiles * tokens, part)
    (mid,) = call(
        functools.partial(conv_kernel, cols=cols, part=part, blocks=frames, count=count),
        16,
        [(plain if frames > 8 else blocked, BF)],
        [],
        place,
        conv_full,
        acts,
        kept,
    )
    if frames > 8:
        mid = mid.reshape(2, 2, tiles, frames, 3, third, part).transpose(0, 3, 2, 1, 5, 4, 6)
        mid = mid.reshape(blocked)
    groups = None
    if clips > 2:
        groups = [[2 * ranks * g + i for i in range(2 * ranks)] for g in range(clips // 2)]
    mid = lax.all_to_all(mid, ("dp",) + square, 0, 0, axis_index_groups=groups, tiled=True)

    lanes = frames * SLOT
    padded = round_up(count + 3, 8)
    total = frames * padded
    scale = jnp.tile(jnp.pad(logit_scale, (0, SLOT - heads)), frames)[None]
    qgain = jnp.tile(query_gain, heads)[None]
    kgain = jnp.tile(key_gain, heads)[None]
    full = (total, width)
    double = (2 * total, width)
    narrow = (total, lanes)
    kept, sent, scale_sums, d_raw, q_hat, k_hat, q_rstd, k_rstd, d_value = call(
        functools.partial(attend_kernel, heads=heads, count=count, padded=padded, part=part),
        20,
        [
            ((2, 2, frames // 2, share, width), BF),
            ((2, 2, frames // 2, share, width), BF),
            ((1, lanes), F32), (narrow, F32),
            (full, F32), (full, F32), (narrow, F32), (narrow, F32), (full, BF),
        ],
        [
            (full, F32), (full, F32), (double, F32), (double, F32), (full, F32),
            (narrow, F32), (narrow, F32),
        ],
        place, mid, packed, attn_full, qgain, kgain, scale,
    )
    d_qn, d_kn = call(
        functools.partial(slope_kernel, heads=heads, padded=padded),
        16,
        [(full, F32), (full, F32)],
        [(double, F32), (double, F32)],
        d_raw, q_hat, k_hat, qgain, kgain,
    )

    def add(mine, theirs):
        return (mine.astype(F32) + theirs.astype(F32)).astype(BF)

    shares = add(kept, swap(sent, "frame"))
    shares, d_qn = lax.optimization_barrier((shares, d_qn))
    (d_mid,) = call(
        functools.partial(back_kernel, heads=heads, count=count, padded=padded),
        16,
        [((frames, padded, width), BF)],
        [],
        d_qn, d_kn, q_hat, k_hat, q_rstd, k_rstd, d_value, attn_full, qgain, kgain, scale_sums,
    )
    shares = add(shares[0], swap(shares[1], "dp"))
    shares = add(shares[0], swap(shares[1], "tile"))
    step = frames // 4
    while step > 0:
        pairs = [(i, i ^ (2 * step)) for i in range(frames)]
        shares = add(shares[:step], lax.ppermute(shares[step:], "frame", pairs))
        step //= 2
    shares = shares[0]
    d_back = lax.all_to_all(d_mid, "frame", 0, 0, tiled=True)
    small = jnp.sum(d_back[:, count : count + 3].astype(F32), axis=(0, 1))
    d_back = d_back[:, :count].reshape(rows, cols, width)
    mid_grad = (cot.astype(F32) + d_back.astype(F32)).astype(BF)

    small = small + swap(small, "tile")
    if clips == 2:
        small = small + swap(small, "dp")
    else:
        small = lax.psum(small, "dp")
        same_clip = [[i for i in range(clips) if i % 2 == c] for c in (0, 1)]
        shares = lax.psum(shares, "dp", axis_index_groups=same_clip)
    theirs = swap(shares, "dp").astype(F32)
    shares = shares.astype(F32)
    factor = 1.0 / math.sqrt(clips * frames * tiles * tokens)
    value_grad = jnp.where(x == 0, shares, theirs) * factor
    out_proj_grad = jnp.where(x == 0, theirs, shares) * factor
    scale_sum = small[256 : 256 + heads]
    return (
        mid_grad[None, None],
        value_grad,
        out_proj_grad,
        small[:depth] * factor,
        small[128 : 128 + depth] * factor,
        scale_sum * factor,
    )


def solution(mesh):
    in_specs = (
        P("dp", "frame", "tile", None, None),
        P("dp", "frame", "tile", None, None),
        P(),
        P(None, ("frame", "tile"), None),
        P(("frame", "tile"), None),
        P(),
        P(),
        P(),
    )
    out_specs = (
        P("dp", "frame", "tile", None, None),
        P(("frame", "tile"), None),
        P(("frame", "tile"), None),
        P(),
        P(),
        P(),
    )
    return jax.shard_map(local, mesh=mesh, in_specs=in_specs, out_specs=out_specs, check_vma=False)
```

```python
import functools
import math

import jax
import jax.numpy as jnp
from jax import lax
from jax.experimental import pallas as pl
from jax.experimental.pallas import tpu as pltpu
from jax.sharding import PartitionSpec as P

GROUPS = 32
EPS = 1e-05
SLOT = 16
BF = jnp.bfloat16
F32 = jnp.float32


def swap(x, axis):
    return lax.ppermute(x, axis, [(i, i ^ 1) for i in range(lax.axis_size(axis))])


def round_up(value, unit):
    return -(-value // unit) * unit


def dot(a, b):
    return lax.dot_general(a, b, (((1,), (0,)), ((), ())), preferred_element_type=F32)


def dot_t(a, b):
    return lax.dot_general(a, b, (((1,), (1,)), ((), ())), preferred_element_type=F32)


def dot_rows(a, b):
    return lax.dot_general(a, b, (((0,), (0,)), ((), ())), preferred_element_type=F32)


def halves(x):
    high = x.astype(BF)
    return high, (x - high.astype(F32)).astype(BF)


def picker(rows, cols, depth, offset):
    row = lax.broadcasted_iota(jnp.int32, (rows, cols), 0)
    col = lax.broadcasted_iota(jnp.int32, (rows, cols), 1)
    return (col - row // depth == offset).astype(F32).astype(BF)


def spreader(rows, cols, depth, offset):
    row = lax.broadcasted_iota(jnp.int32, (rows, cols), 0)
    col = lax.broadcasted_iota(jnp.int32, (rows, cols), 1)
    return (row - col // depth == offset).astype(F32).astype(BF)


def head_sums(x, pick):
    high, low = halves(x)
    return dot(high, pick) + dot(low, pick)


def spread(x, both):
    high, low = halves(x)
    return dot(jnp.concatenate([high, low], axis=1), both)


def over_slots(x):
    step = SLOT
    while step < x.shape[1]:
        x = x + pltpu.roll(x, step, 1)
        step *= 2
    return x


def each(number, body):
    if number > 8:
        lax.fori_loop(0, number, lambda i, _: body(i), None)
    else:
        for i in range(number):
            body(i)


def taps_kernel(place, mine, theirs, out):
    odd = place[4] % 2
    share = out.shape[2]
    for owner in range(mine.shape[0]):
        first = jnp.where(odd == 0, mine[owner], theirs[owner])
        second = jnp.where(odd == 0, theirs[owner], mine[owner])
        block = jnp.concatenate([first, second], axis=0)
        for row in range(3):
            out[row, owner] = block[row * share : (row + 1) * share]


def join_kernel(place, *refs):
    pieces, out = (refs[:-1], refs[-1])
    x, core, tile = (place[0], place[1], place[2])
    frames = out.shape[1]
    for dc in (0, 1):
        own, by_tile, by_clip, low, high = pieces[5 * dc : 5 * dc + 5]
        own_kind = 2 * x + (core ^ dc)
        other_kind = 2 * (x ^ 1) + (core ^ dc)
        for f in range(frames):
            out[own_kind, f, tile] = own[f]
            out[own_kind, f, tile ^ 1] = by_tile[f]
            out[other_kind, f, tile] = by_clip[f]
            part, index = (low, f) if f < frames // 2 else (high, f - frames // 2)
            out[other_kind, f, tile ^ 1] = part[index]


def act_kernel(place, gain, *refs, cols, part):
    blocks, (acts, kept) = (refs[:-2], refs[-2:])
    half, width = blocks[0].shape
    tile, chosen = (place[2], place[3])
    choice = picker(width, part, 1, -part * chosen)
    per_group = width // GROUPS
    pick = picker(width, 128, per_group, 0)
    back = spreader(128, width, per_group, 0)

    def thirds(x):
        high, low = halves(x)
        return high, low, (x - high.astype(F32) - low.astype(F32)).astype(BF)

    totals, squares = ([], [])
    for frame in range(4):
        total, square = (0.0, 0.0)
        for dy in (0, 1):
            x = blocks[2 * frame + dy][...]
            start = pl.multiple_of((tile ^ dy) * half, half)
            kept[frame, pl.ds(start, half), :] = dot(x, choice).astype(BF)
            x = x.astype(F32)
            total = total + jnp.sum(x, axis=0, keepdims=True)
            square = square + jnp.sum(x * x, axis=0, keepdims=True)
        totals.append(total)
        squares.append(square)
    high, low, lowest = thirds(jnp.concatenate(totals + squares, axis=0))
    both = (dot(high, pick) + dot(low, pick) + dot(lowest, pick)) / (2 * half * per_group)
    mean = both[0:4]
    rstd = lax.rsqrt(both[4:8] - mean * mean + EPS)
    high, low, lowest = thirds(jnp.concatenate([mean, rstd], axis=0))
    both = dot(high, back) + dot(low, back) + dot(lowest, back)
    scales = both[4:8] * gain[...]
    for frame in range(4):
        acts[frame, pl.ds(0, cols), :] = jnp.zeros((cols, width), BF)
        acts[frame, pl.ds(cols + 2 * half, cols), :] = jnp.zeros((cols, width), BF)
        for dy in (0, 1):
            x = blocks[2 * frame + dy][...].astype(F32)
            zed = (x - both[frame : frame + 1]) * scales[frame : frame + 1]
            start = pl.multiple_of(cols + (tile ^ dy) * half, cols)
            acts[frame, pl.ds(start, half), :] = (zed / (1.0 + jnp.exp(-zed))).astype(BF)


def conv_kernel(place, weights, acts, kept, out, *, cols, part, blocks, count):
    x, core = (place[0], place[1])
    whole = kept.shape[1]
    half = whole // 2
    third = count // 3
    col = lax.broadcasted_iota(jnp.int32, (whole, part), 0) % cols
    for dx in (0, 1):
        mids = []
        for dc in (0, 1):
            frame = 2 * dc + dx
            taps = dot(acts[frame, pl.ds(0, whole), :], weights[0])
            taps += dot(acts[frame, pl.ds(cols, whole), :], weights[1])
            taps += dot(acts[frame, pl.ds(2 * cols, whole), :], weights[2])
            left = pltpu.roll(taps[:, :part], 1, 0)
            right = pltpu.roll(taps[:, 2 * part :], whole - 1, 0)
            pre = taps[:, part : 2 * part] + jnp.where(col > 0, left, 0.0)
            pre = pre + jnp.where(col < cols - 1, right, 0.0)
            mids.append((kept[frame].astype(F32) + pre).astype(BF))
        if blocks > 8:
            for dc in (0, 1):
                out[x ^ dx, dc] = mids[dc]
            continue
        for f in range(blocks):
            for t in (0, 1):
                start = t * half + f * count
                rows = [
                    jnp.concatenate(
                        [mid[start + third * j : start + third * (j + 1)] for j in range(3)], axis=1
                    )
                    for mid in mids
                ]
                index = ((x ^ dx) * blocks + f) * 2 + t
                out[index] = jnp.concatenate(rows, axis=0)


def attend_kernel(
    place, mid_in, cot_in, weights, qgain, kgain, scale,
    kept, sent, sums, d_raw, q_hat, k_hat, q_rstd, k_rstd, d_value,
    mid_s, cot_s, doubled, doubled_v, mixed_s, raw_s, probs_s,
    *, heads, count, padded, part,
):
    total, width = mid_s.shape
    frames = total // padded
    depth = width // heads
    lanes = scale.shape[-1]
    third = count // 3
    x, core, tile, plane = (place[0], place[1], place[2], place[4])
    mid_s[...] = jnp.zeros_like(mid_s)
    cot_s[...] = jnp.zeros_like(cot_s)
    for z in range(frames // 2):
        for e in (0, 1):
            f = 2 * z + e
            blocks = [
                mid_in[(x * frames + 2 * z + c) * 2 + t, pl.ds((e ^ c) * third, third), :]
                for x in (0, 1)
                for c in (0, 1)
                for t in (0, 1)
            ]
            for j in range(3):
                piece = [b[:, j * part : (j + 1) * part] for b in blocks]
                start = f * padded + j * third
                mid_s[pl.ds(start, third), :] = jnp.concatenate(piece, axis=1).astype(F32)
            cot_s[pl.ds(f * padded, count), :] = cot_in[f].astype(F32)
    mid = mid_s[...].astype(BF)
    cot = cot_s[...].astype(BF)
    pick = picker(width, lanes, depth, 0)
    both = jnp.concatenate([spreader(lanes, width, depth, 0)] * 2, axis=0)

    def stats(vec):
        cent = vec - spread(head_sums(vec, pick) / depth, both)
        var = head_sums(cent * cent, pick) / depth
        rstd = lax.rsqrt(var + EPS)
        return cent * spread(rstd, both), rstd

    hat, rstd = stats(dot(mid, weights[0]))
    q_hat[...] = hat
    q_rstd[...] = rstd
    q_norm = hat * qgain[...]
    hat, rstd = stats(dot(mid, weights[1]))
    k_hat[...] = hat
    k_rstd[...] = rstd
    hat = hat * kgain[...]
    doubled[pl.ds(0, total), :] = hat
    doubled[pl.ds(total, total), :] = hat
    value = dot(mid, weights[2]).astype(BF).astype(F32)
    doubled_v[pl.ds(0, total), :] = value
    doubled_v[pl.ds(total, total), :] = value
    d_mixed = dot_t(cot, weights[3]).astype(BF).astype(F32)
    raw_s[...] = jnp.zeros_like(raw_s)
    probs_s[...] = jnp.zeros_like(probs_s)

    def logits(s):
        here = picker(width, lanes, depth, SLOT * s)
        raw_s[...] += head_sums(q_norm * doubled[pl.ds(s * padded, total), :], here)
        probs_s[...] += head_sums(d_mixed * doubled_v[pl.ds(s * padded, total), :], here)

    each(frames, logits)
    raw = raw_s[...] / math.sqrt(depth)
    expo = jnp.exp(raw * scale[...])
    probs = expo / over_slots(expo)
    probs_b = probs.astype(BF)
    d_probs = probs_s[...]
    d_logits = probs * (d_probs - over_slots(probs * d_probs))
    sums[...] = jnp.sum(d_logits * raw, axis=0, keepdims=True)
    d_raw[...] = d_logits * scale[...] / math.sqrt(depth)
    mixed_s[...] = jnp.zeros_like(mixed_s)
    doubled[...] = jnp.zeros_like(doubled)

    def mix(s):
        weight = dot(probs_b, spreader(lanes, width, depth, SLOT * s))
        mixed_s[...] += weight * doubled_v[pl.ds(s * padded, total), :]
        doubled[pl.ds(s * padded, total), :] += weight * d_mixed

    each(frames, mix)
    dv = (doubled[pl.ds(0, total), :] + doubled[pl.ds(total, total), :]).astype(BF)
    d_value[...] = dv
    rows = kept.shape[3]

    def store(kind, term):
        for z in range(frames // 2):
            for t in (0, 1):
                start = (4 * z + t) * rows
                first = term[start : start + rows]
                second = term[start + 2 * rows : start + 3 * rows]
                kept[x ^ kind, tile ^ t, plane ^ z] = jnp.where(core == 0, first, second)
                sent[x ^ kind, tile ^ t, plane ^ z] = jnp.where(core == 0, second, first)

    store(1, dot_rows(mixed_s[...].astype(BF), cot).astype(BF))
    store(0, dot_rows(mid, dv).astype(BF))


def slope_kernel(
    d_raw, q_hat, k_hat, qgain, kgain,
    d_qn, d_kn,
    doubled, doubled_acc,
    *, heads, padded,
):
    total, width = q_hat.shape
    depth = width // heads
    frames = total // padded
    lanes = d_raw.shape[-1]
    k_norm = k_hat[...] * kgain[...]
    doubled[pl.ds(0, total), :] = k_norm
    doubled[pl.ds(total, total), :] = k_norm
    q_norm = q_hat[...] * qgain[...]
    doubled_acc[...] = jnp.zeros_like(doubled_acc)
    d_qn[...] = jnp.zeros_like(d_qn)
    high, low = halves(d_raw[...])
    pair = jnp.concatenate([high, low], axis=1)

    def shift(s):
        one = spreader(lanes, width, depth, SLOT * s)
        weight = dot(pair, jnp.concatenate([one, one], axis=0))
        d_qn[...] += weight * doubled[pl.ds(s * padded, total), :]
        doubled_acc[pl.ds(s * padded, total), :] += weight * q_norm

    each(frames, shift)
    d_kn[...] = doubled_acc[pl.ds(0, total), :] + doubled_acc[pl.ds(total, total), :]


def back_kernel(
    d_qn, d_kn, q_hat, k_hat, q_rstd, k_rstd, d_value, weights, qgain, kgain, scale_sums,
    d_mid,
    *, heads, count, padded,
):
    total, width = q_hat.shape
    depth = width // heads
    frames = total // padded
    lanes = scale_sums.shape[-1]
    pick = picker(width, lanes, depth, 0)
    both = jnp.concatenate([spreader(lanes, width, depth, 0)] * 2, axis=0)

    def back(dhat, hat, rstd):
        first = spread(head_sums(dhat, pick) / depth, both)
        second = spread(head_sums(dhat * hat, pick) / depth, both)
        return (spread(rstd, both) * (dhat - first - hat * second)).astype(BF)

    d_query = back(d_qn[...] * qgain[...], q_hat[...], q_rstd[...])
    d_key = back(d_kn[...] * kgain[...], k_hat[...], k_rstd[...])
    out = dot_t(d_query, weights[0])
    out += dot_t(d_key, weights[1])
    out += dot_t(d_value[...], weights[2])

    row = lax.broadcasted_iota(jnp.int32, (width, 128), 0)
    col = lax.broadcasted_iota(jnp.int32, (width, 128), 1)
    fold = (row % depth == col).astype(F32)

    def folded(d_norm, hat):
        sums = jnp.sum(d_norm * hat, axis=0, keepdims=True)
        sums = jnp.broadcast_to(sums, (8, width))
        return jnp.dot(sums, fold, precision=lax.Precision.HIGHEST, preferred_element_type=F32)[0:1]

    by_head = over_slots(jnp.broadcast_to(scale_sums[...], (8, lanes)))[0:1, :128]
    small = [folded(d_qn[...], q_hat[...]), folded(d_kn[...], k_hat[...]), by_head]
    small.append(jnp.zeros((1, width - 384), F32))
    small = jnp.concatenate(small, axis=1)
    high, low = halves(small)
    lowest = (small - high.astype(F32) - low.astype(F32)).astype(BF)
    spare = [high.astype(F32), low.astype(F32), lowest.astype(F32)]
    if padded - count > 3:
        spare.append(jnp.zeros((padded - count - 3, width), F32))
    spare = jnp.concatenate(spare, axis=0)
    for f in range(frames):
        tokens = out[f * padded : f * padded + count]
        d_mid[f] = jnp.concatenate([tokens, spare], axis=0).astype(BF)


def call(kernel, mebibytes, outs, scratch, *args):
    smem = pl.BlockSpec(memory_space=pltpu.SMEM)
    vmem = pl.BlockSpec(memory_space=pltpu.VMEM)
    return pl.pallas_call(
        kernel,
        out_shape=[jax.ShapeDtypeStruct(shape, dtype) for shape, dtype in outs],
        in_specs=[smem if arg.dtype == jnp.int32 else vmem for arg in args],
        out_specs=[vmem] * len(outs),
        scratch_shapes=[pltpu.VMEM(shape, dtype) for shape, dtype in scratch],
        compiler_params=pltpu.CompilerParams(vmem_limit_bytes=mebibytes << 20),
    )(*args)


def local(
    clip_input, cotangent, norm_gain, conv_weight, attn_weight, query_gain, key_gain, logit_scale
):
    source = clip_input[0, 0]
    cot = cotangent[0, 0]
    rows, cols, width = source.shape
    heads = logit_scale.shape[0]
    depth = width // heads
    tokens = rows * cols
    clips, frames, tiles = (lax.axis_size(name) for name in ("dp", "frame", "tile"))
    square = ("frame", "tile")
    ranks = frames * tiles
    share = conv_weight.shape[1]
    count = tokens // frames
    third = count // 3
    part = width // 8
    x = lax.axis_index("dp") % 2
    core = lax.axis_index("frame") % 2
    tile = lax.axis_index("tile")
    plane = lax.axis_index("frame") // 2
    place = jnp.stack([x, core, tile, 4 * x + 2 * core + tile, plane]).astype(jnp.int32)
    flat = source.reshape(tokens, width)

    lines = 3 * share // 2
    mine = lax.dynamic_slice_in_dim(conv_weight, x * (width // 2), width // 2, axis=2)
    mine = mine.reshape(3, 3, share, 4, part).transpose(3, 0, 2, 1, 4)
    mine = mine.reshape(4, 2, lines, 3 * part).transpose(1, 0, 2, 3)
    mine = jnp.broadcast_to(mine[None], (frames // 4,) + mine.shape)
    mine = mine.reshape(ranks, lines, 3 * part)
    conv_half = lax.all_to_all(mine, square, 0, 0, tiled=True)

    along_x = swap(flat, "dp")
    along_y = swap(flat, "tile")

    kinds = lax.dynamic_slice_in_dim(attn_weight, x * 2 * width, 2 * width, axis=1)
    kinds = kinds.reshape(share, 2, width).transpose(1, 0, 2)
    kinds = jnp.broadcast_to(kinds[None], (frames // 2,) + kinds.shape).reshape(frames, share, width)
    kinds, conv_half, along_x, along_y = lax.optimization_barrier(
        (kinds, conv_half, along_x, along_y)
    )
    own = lax.all_to_all(kinds, "frame", 0, 0, tiled=True)
    conv_other = lax.ppermute(conv_half, "frame", [(i, i ^ 2) for i in range(frames)])

    half = tokens // 2
    across = jnp.concatenate([swap(along_x[:half], "tile"), swap(along_y[half:], "dp")])
    pieces = [flat, along_y, along_x, across]
    pieces += [swap(piece, "frame") for piece in pieces]
    acts, kept = call(
        functools.partial(act_kernel, cols=cols, part=part),
        20,
        [((4, tiles * tokens + 2 * cols, width), BF), ((4, tiles * tokens, part), BF)],
        [],
        place,
        norm_gain[None],
        *pieces,
    )

    cot_blocks = cot.reshape(frames, count, width)
    cot_blocks, own, acts, kept, conv_half, conv_other = lax.optimization_barrier(
        (cot_blocks, own, acts, kept, conv_half, conv_other)
    )
    cot_blocks = lax.all_to_all(cot_blocks, "frame", 0, 0, tiled=True)
    by_tile = swap(own, "tile")
    by_clip = swap(own, "dp")

    (conv_full,) = call(
        taps_kernel, 12, [((3, ranks, share, 3 * part), BF)], [], place, conv_half, conv_other
    )
    conv_full = conv_full.reshape(3, width, 3 * part)
    blocked = (2 * ranks, 2 * third, 3 * part)
    plain = (2, 2, tiles * tokens, part)
    (mid,) = call(
        functools.partial(conv_kernel, cols=cols, part=part, blocks=frames, count=count),
        16,
        [(plain if frames > 8 else blocked, BF)],
        [],
        place,
        conv_full,
        acts,
        kept,
    )
    if frames > 8:
        mid = mid.reshape(2, 2, tiles, frames, 3, third, part).transpose(0, 3, 2, 1, 5, 4, 6)
        mid = mid.reshape(blocked)
    mid, cot_blocks, by_tile, by_clip = lax.optimization_barrier(
        (mid, cot_blocks, by_tile, by_clip)
    )
    groups = None
    if clips > 2:
        groups = [[2 * ranks * g + i for i in range(2 * ranks)] for g in range(clips // 2)]
    mid = lax.all_to_all(mid, ("dp",) + square, 0, 0, axis_index_groups=groups, tiled=True)

    middle = frames // 2
    parts = [own, by_tile, by_clip, swap(by_clip[:middle], "tile"), swap(by_tile[middle:], "dp")]
    parts += [swap(piece, "frame") for piece in parts]
    (attn_full,) = call(
        join_kernel, 16, [((4, frames, tiles, share, width), BF)], [], place, *parts
    )
    attn_full = attn_full.reshape(4, width, width)

    lanes = frames * SLOT
    padded = round_up(count + 3, 8)
    total = frames * padded
    scale = jnp.tile(jnp.pad(logit_scale, (0, SLOT - heads)), frames)[None]
    qgain = jnp.tile(query_gain, heads)[None]
    kgain = jnp.tile(key_gain, heads)[None]
    full = (total, width)
    double = (2 * total, width)
    narrow = (total, lanes)
    kept, sent, scale_sums, d_raw, q_hat, k_hat, q_rstd, k_rstd, d_value = call(
        functools.partial(attend_kernel, heads=heads, count=count, padded=padded, part=part),
        20,
        [
            ((2, 2, frames // 2, share, width), BF),
            ((2, 2, frames // 2, share, width), BF),
            ((1, lanes), F32), (narrow, F32),
            (full, F32), (full, F32), (narrow, F32), (narrow, F32), (full, BF),
        ],
        [
            (full, F32), (full, F32), (double, F32), (double, F32), (full, F32),
            (narrow, F32), (narrow, F32),
        ],
        place, mid, cot_blocks, attn_full, qgain, kgain, scale,
    )
    d_qn, d_kn = call(
        functools.partial(slope_kernel, heads=heads, padded=padded),
        16,
        [(full, F32), (full, F32)],
        [(double, F32), (double, F32)],
        d_raw, q_hat, k_hat, qgain, kgain,
    )

    def add(mine, theirs):
        return (mine.astype(F32) + theirs.astype(F32)).astype(BF)

    shares = add(kept, swap(sent, "frame"))
    shares, d_qn = lax.optimization_barrier((shares, d_qn))
    (d_mid,) = call(
        functools.partial(back_kernel, heads=heads, count=count, padded=padded),
        16,
        [((frames, padded, width), BF)],
        [],
        d_qn, d_kn, q_hat, k_hat, q_rstd, k_rstd, d_value, attn_full, qgain, kgain, scale_sums,
    )
    shares = add(shares[0], swap(shares[1], "dp"))
    shares = add(shares[0], swap(shares[1], "tile"))
    step = frames // 4
    while step > 0:
        pairs = [(i, i ^ (2 * step)) for i in range(frames)]
        shares = add(shares[:step], lax.ppermute(shares[step:], "frame", pairs))
        step //= 2
    shares = shares[0]
    d_back = lax.all_to_all(d_mid, "frame", 0, 0, tiled=True)
    small = jnp.sum(d_back[:, count : count + 3].astype(F32), axis=(0, 1))
    d_back = d_back[:, :count].reshape(rows, cols, width)
    mid_grad = (cot.astype(F32) + d_back.astype(F32)).astype(BF)

    small = small + swap(small, "tile")
    if clips == 2:
        small = small + swap(small, "dp")
    else:
        small = lax.psum(small, "dp")
        same_clip = [[i for i in range(clips) if i % 2 == c] for c in (0, 1)]
        shares = lax.psum(shares, "dp", axis_index_groups=same_clip)
    theirs = swap(shares, "dp").astype(F32)
    shares = shares.astype(F32)
    factor = 1.0 / math.sqrt(clips * frames * tiles * tokens)
    value_grad = jnp.where(x == 0, shares, theirs) * factor
    out_proj_grad = jnp.where(x == 0, theirs, shares) * factor
    scale_sum = small[256 : 256 + heads]
    return (
        mid_grad[None, None],
        value_grad,
        out_proj_grad,
        small[:depth] * factor,
        small[128 : 128 + depth] * factor,
        scale_sum * factor,
    )


def solution(mesh):
    in_specs = (
        P("dp", "frame", "tile", None, None),
        P("dp", "frame", "tile", None, None),
        P(),
        P(None, ("frame", "tile"), None),
        P(("frame", "tile"), None),
        P(),
        P(),
        P(),
    )
    out_specs = (
        P("dp", "frame", "tile", None, None),
        P(("frame", "tile"), None),
        P(("frame", "tile"), None),
        P(),
        P(),
        P(),
    )
    return jax.shard_map(local, mesh=mesh, in_specs=in_specs, out_specs=out_specs, check_vma=False)
```

```python
import functools
import math

import jax
import jax.numpy as jnp
from jax import lax
from jax.experimental import pallas as pl
from jax.experimental.pallas import tpu as pltpu
from jax.sharding import PartitionSpec as P

GROUPS = 32
EPS = 1e-05
SLOT = 16
BF = jnp.bfloat16
F32 = jnp.float32


def swap(x, axis):
    return lax.ppermute(x, axis, [(i, i ^ 1) for i in range(lax.axis_size(axis))])


def round_up(value, unit):
    return -(-value // unit) * unit


def dot(a, b):
    return lax.dot_general(a, b, (((1,), (0,)), ((), ())), preferred_element_type=F32)


def dot_t(a, b):
    return lax.dot_general(a, b, (((1,), (1,)), ((), ())), preferred_element_type=F32)


def dot_rows(a, b):
    return lax.dot_general(a, b, (((0,), (0,)), ((), ())), preferred_element_type=F32)


def halves(x):
    high = x.astype(BF)
    return high, (x - high.astype(F32)).astype(BF)


def picker(rows, cols, depth, offset):
    row = lax.broadcasted_iota(jnp.int32, (rows, cols), 0)
    col = lax.broadcasted_iota(jnp.int32, (rows, cols), 1)
    return (col - row // depth == offset).astype(F32).astype(BF)


def spreader(rows, cols, depth, offset):
    row = lax.broadcasted_iota(jnp.int32, (rows, cols), 0)
    col = lax.broadcasted_iota(jnp.int32, (rows, cols), 1)
    return (row - col // depth == offset).astype(F32).astype(BF)


def head_sums(x, pick):
    high, low = halves(x)
    return dot(high, pick) + dot(low, pick)


def spread(x, both):
    high, low = halves(x)
    return dot(jnp.concatenate([high, low], axis=1), both)


def over_slots(x):
    step = SLOT
    while step < x.shape[1]:
        x = x + pltpu.roll(x, step, 1)
        step *= 2
    return x


def each(number, body):
    if number > 8:
        lax.fori_loop(0, number, lambda i, _: body(i), None)
    else:
        for i in range(number):
            body(i)


def taps_kernel(place, mine, theirs, out):
    odd = place[4] % 2
    share = out.shape[2]
    for owner in range(mine.shape[0]):
        first = jnp.where(odd == 0, mine[owner], theirs[owner])
        second = jnp.where(odd == 0, theirs[owner], mine[owner])
        block = jnp.concatenate([first, second], axis=0)
        for row in range(3):
            out[row, owner] = block[row * share : (row + 1) * share]


def join_kernel(place, *refs):
    pieces, out = (refs[:-1], refs[-1])
    x, core, tile = (place[0], place[1], place[2])
    frames = out.shape[1]
    for dc in (0, 1):
        own, by_tile, by_clip, low, high = pieces[5 * dc : 5 * dc + 5]
        own_kind = 2 * x + (core ^ dc)
        other_kind = 2 * (x ^ 1) + (core ^ dc)
        for f in range(frames):
            out[own_kind, f, tile] = own[f]
            out[own_kind, f, tile ^ 1] = by_tile[f]
            out[other_kind, f, tile] = by_clip[f]
            part, index = (low, f) if f < frames // 2 else (high, f - frames // 2)
            out[other_kind, f, tile ^ 1] = part[index]


def act_kernel(place, gain, *refs, cols, part):
    blocks, (acts, kept) = (refs[:-2], refs[-2:])
    half, width = blocks[0].shape
    tile, chosen = (place[2], place[3])
    choice = picker(width, part, 1, -part * chosen)
    per_group = width // GROUPS
    pick = picker(width, 128, per_group, 0)
    back = spreader(128, width, per_group, 0)

    def thirds(x):
        high, low = halves(x)
        return high, low, (x - high.astype(F32) - low.astype(F32)).astype(BF)

    totals, squares = ([], [])
    for frame in range(4):
        total, square = (0.0, 0.0)
        for dy in (0, 1):
            x = blocks[2 * frame + dy][...]
            start = pl.multiple_of((tile ^ dy) * half, half)
            kept[frame, pl.ds(start, half), :] = dot(x, choice).astype(BF)
            x = x.astype(F32)
            total = total + jnp.sum(x, axis=0, keepdims=True)
            square = square + jnp.sum(x * x, axis=0, keepdims=True)
        totals.append(total)
        squares.append(square)
    high, low, lowest = thirds(jnp.concatenate(totals + squares, axis=0))
    both = (dot(high, pick) + dot(low, pick) + dot(lowest, pick)) / (2 * half * per_group)
    mean = both[0:4]
    rstd = lax.rsqrt(both[4:8] - mean * mean + EPS)
    high, low, lowest = thirds(jnp.concatenate([mean, rstd], axis=0))
    both = dot(high, back) + dot(low, back) + dot(lowest, back)
    scales = both[4:8] * gain[...]
    for frame in range(4):
        acts[frame, pl.ds(0, cols), :] = jnp.zeros((cols, width), BF)
        acts[frame, pl.ds(cols + 2 * half, cols), :] = jnp.zeros((cols, width), BF)
        for dy in (0, 1):
            x = blocks[2 * frame + dy][...].astype(F32)
            zed = (x - both[frame : frame + 1]) * scales[frame : frame + 1]
            start = pl.multiple_of(cols + (tile ^ dy) * half, cols)
            acts[frame, pl.ds(start, half), :] = (zed / (1.0 + jnp.exp(-zed))).astype(BF)


def conv_kernel(place, weights, acts, kept, out, *, cols, part, blocks, count):
    x, core = (place[0], place[1])
    whole = kept.shape[1]
    half = whole // 2
    third = count // 3
    col = lax.broadcasted_iota(jnp.int32, (whole, part), 0) % cols
    for dx in (0, 1):
        mids = []
        for dc in (0, 1):
            frame = 2 * dc + dx
            taps = dot(acts[frame, pl.ds(0, whole), :], weights[0])
            taps += dot(acts[frame, pl.ds(cols, whole), :], weights[1])
            taps += dot(acts[frame, pl.ds(2 * cols, whole), :], weights[2])
            left = pltpu.roll(taps[:, :part], 1, 0)
            right = pltpu.roll(taps[:, 2 * part :], whole - 1, 0)
            pre = taps[:, part : 2 * part] + jnp.where(col > 0, left, 0.0)
            pre = pre + jnp.where(col < cols - 1, right, 0.0)
            mids.append((kept[frame].astype(F32) + pre).astype(BF))
        if blocks > 8:
            for dc in (0, 1):
                out[x ^ dx, dc] = mids[dc]
            continue
        for f in range(blocks):
            for t in (0, 1):
                start = t * half + f * count
                rows = [
                    jnp.concatenate(
                        [mid[start + third * j : start + third * (j + 1)] for j in range(3)], axis=1
                    )
                    for mid in mids
                ]
                index = ((x ^ dx) * blocks + f) * 2 + t
                out[index] = jnp.concatenate(rows, axis=0)


def attend_kernel(
    place, mid_in, cot_in, weights, qgain, kgain, scale,
    kept, sent, sums, d_raw, q_hat, k_hat, q_rstd, k_rstd, d_value,
    mid_s, cot_s, doubled, doubled_v, mixed_s, raw_s, probs_s,
    *, heads, count, padded, part,
):
    total, width = mid_s.shape
    frames = total // padded
    depth = width // heads
    lanes = scale.shape[-1]
    third = count // 3
    x, core, tile, plane = (place[0], place[1], place[2], place[4])
    mid_s[...] = jnp.zeros_like(mid_s)
    cot_s[...] = jnp.zeros_like(cot_s)
    for z in range(frames // 2):
        for e in (0, 1):
            f = 2 * z + e
            blocks = [
                mid_in[(x * frames + 2 * z + c) * 2 + t, pl.ds((e ^ c) * third, third), :]
                for x in (0, 1)
                for c in (0, 1)
                for t in (0, 1)
            ]
            for j in range(3):
                piece = [b[:, j * part : (j + 1) * part] for b in blocks]
                start = f * padded + j * third
                mid_s[pl.ds(start, third), :] = jnp.concatenate(piece, axis=1).astype(F32)
            cot_s[pl.ds(f * padded, count), :] = cot_in[f].astype(F32)
    mid = mid_s[...].astype(BF)
    cot = cot_s[...].astype(BF)
    pick = picker(width, lanes, depth, 0)
    both = jnp.concatenate([spreader(lanes, width, depth, 0)] * 2, axis=0)

    def stats(vec):
        cent = vec - spread(head_sums(vec, pick) / depth, both)
        var = head_sums(cent * cent, pick) / depth
        rstd = lax.rsqrt(var + EPS)
        return cent * spread(rstd, both), rstd

    hat, rstd = stats(dot(mid, weights[0]))
    q_hat[...] = hat
    q_rstd[...] = rstd
    q_norm = hat * qgain[...]
    hat, rstd = stats(dot(mid, weights[1]))
    k_hat[...] = hat
    k_rstd[...] = rstd
    hat = hat * kgain[...]
    doubled[pl.ds(0, total), :] = hat
    doubled[pl.ds(total, total), :] = hat
    value = dot(mid, weights[2]).astype(BF).astype(F32)
    doubled_v[pl.ds(0, total), :] = value
    doubled_v[pl.ds(total, total), :] = value
    d_mixed = dot_t(cot, weights[3]).astype(BF).astype(F32)
    raw_s[...] = jnp.zeros_like(raw_s)
    probs_s[...] = jnp.zeros_like(probs_s)

    def logits(s):
        here = picker(width, lanes, depth, SLOT * s)
        raw_s[...] += head_sums(q_norm * doubled[pl.ds(s * padded, total), :], here)
        probs_s[...] += head_sums(d_mixed * doubled_v[pl.ds(s * padded, total), :], here)

    each(frames, logits)
    raw = raw_s[...] / math.sqrt(depth)
    expo = jnp.exp(raw * scale[...])
    probs = expo / over_slots(expo)
    probs_b = probs.astype(BF)
    d_probs = probs_s[...]
    d_logits = probs * (d_probs - over_slots(probs * d_probs))
    sums[...] = jnp.sum(d_logits * raw, axis=0, keepdims=True)
    d_raw[...] = d_logits * scale[...] / math.sqrt(depth)
    mixed_s[...] = jnp.zeros_like(mixed_s)
    doubled[...] = jnp.zeros_like(doubled)

    def mix(s):
        weight = dot(probs_b, spreader(lanes, width, depth, SLOT * s))
        mixed_s[...] += weight * doubled_v[pl.ds(s * padded, total), :]
        doubled[pl.ds(s * padded, total), :] += weight * d_mixed

    each(frames, mix)
    dv = (doubled[pl.ds(0, total), :] + doubled[pl.ds(total, total), :]).astype(BF)
    d_value[...] = dv
    rows = kept.shape[3]

    def store(kind, term):
        for z in range(frames // 2):
            for t in (0, 1):
                start = (4 * z + t) * rows
                first = term[start : start + rows]
                second = term[start + 2 * rows : start + 3 * rows]
                kept[x ^ kind, tile ^ t, plane ^ z] = jnp.where(core == 0, first, second)
                sent[x ^ kind, tile ^ t, plane ^ z] = jnp.where(core == 0, second, first)

    store(1, dot_rows(mixed_s[...].astype(BF), cot).astype(BF))
    store(0, dot_rows(mid, dv).astype(BF))


def slope_kernel(
    d_raw, q_hat, k_hat, qgain, kgain,
    d_qn, d_kn,
    doubled, doubled_acc,
    *, heads, padded,
):
    total, width = q_hat.shape
    depth = width // heads
    frames = total // padded
    lanes = d_raw.shape[-1]
    k_norm = k_hat[...] * kgain[...]
    doubled[pl.ds(0, total), :] = k_norm
    doubled[pl.ds(total, total), :] = k_norm
    q_norm = q_hat[...] * qgain[...]
    doubled_acc[...] = jnp.zeros_like(doubled_acc)
    d_qn[...] = jnp.zeros_like(d_qn)
    high, low = halves(d_raw[...])
    pair = jnp.concatenate([high, low], axis=1)

    def shift(s):
        one = spreader(lanes, width, depth, SLOT * s)
        weight = dot(pair, jnp.concatenate([one, one], axis=0))
        d_qn[...] += weight * doubled[pl.ds(s * padded, total), :]
        doubled_acc[pl.ds(s * padded, total), :] += weight * q_norm

    each(frames, shift)
    d_kn[...] = doubled_acc[pl.ds(0, total), :] + doubled_acc[pl.ds(total, total), :]


def back_kernel(
    d_qn, d_kn, q_hat, k_hat, q_rstd, k_rstd, d_value, weights, qgain, kgain, scale_sums,
    d_mid,
    *, heads, count, padded,
):
    total, width = q_hat.shape
    depth = width // heads
    frames = total // padded
    lanes = scale_sums.shape[-1]
    pick = picker(width, lanes, depth, 0)
    both = jnp.concatenate([spreader(lanes, width, depth, 0)] * 2, axis=0)

    def back(dhat, hat, rstd):
        first = spread(head_sums(dhat, pick) / depth, both)
        second = spread(head_sums(dhat * hat, pick) / depth, both)
        return (spread(rstd, both) * (dhat - first - hat * second)).astype(BF)

    d_query = back(d_qn[...] * qgain[...], q_hat[...], q_rstd[...])
    d_key = back(d_kn[...] * kgain[...], k_hat[...], k_rstd[...])
    out = dot_t(d_query, weights[0])
    out += dot_t(d_key, weights[1])
    out += dot_t(d_value[...], weights[2])

    row = lax.broadcasted_iota(jnp.int32, (width, 128), 0)
    col = lax.broadcasted_iota(jnp.int32, (width, 128), 1)
    fold = (row % depth == col).astype(F32)

    def folded(d_norm, hat):
        sums = jnp.sum(d_norm * hat, axis=0, keepdims=True)
        sums = jnp.broadcast_to(sums, (8, width))
        return jnp.dot(sums, fold, precision=lax.Precision.HIGHEST, preferred_element_type=F32)[0:1]

    by_head = over_slots(jnp.broadcast_to(scale_sums[...], (8, lanes)))[0:1, :128]
    small = [folded(d_qn[...], q_hat[...]), folded(d_kn[...], k_hat[...]), by_head]
    small.append(jnp.zeros((1, width - 384), F32))
    small = jnp.concatenate(small, axis=1)
    high, low = halves(small)
    lowest = (small - high.astype(F32) - low.astype(F32)).astype(BF)
    spare = [high.astype(F32), low.astype(F32), lowest.astype(F32)]
    if padded - count > 3:
        spare.append(jnp.zeros((padded - count - 3, width), F32))
    spare = jnp.concatenate(spare, axis=0)
    for f in range(frames):
        tokens = out[f * padded : f * padded + count]
        d_mid[f] = jnp.concatenate([tokens, spare], axis=0).astype(BF)


def call(kernel, mebibytes, outs, scratch, *args):
    smem = pl.BlockSpec(memory_space=pltpu.SMEM)
    vmem = pl.BlockSpec(memory_space=pltpu.VMEM)
    return pl.pallas_call(
        kernel,
        out_shape=[jax.ShapeDtypeStruct(shape, dtype) for shape, dtype in outs],
        in_specs=[smem if arg.dtype == jnp.int32 else vmem for arg in args],
        out_specs=[vmem] * len(outs),
        scratch_shapes=[pltpu.VMEM(shape, dtype) for shape, dtype in scratch],
        compiler_params=pltpu.CompilerParams(vmem_limit_bytes=mebibytes << 20),
    )(*args)


def local(
    clip_input, cotangent, norm_gain, conv_weight, attn_weight, query_gain, key_gain, logit_scale
):
    source = clip_input[0, 0]
    cot = cotangent[0, 0]
    rows, cols, width = source.shape
    heads = logit_scale.shape[0]
    depth = width // heads
    tokens = rows * cols
    clips, frames, tiles = (lax.axis_size(name) for name in ("dp", "frame", "tile"))
    square = ("frame", "tile")
    ranks = frames * tiles
    share = conv_weight.shape[1]
    count = tokens // frames
    third = count // 3
    part = width // 8
    x = lax.axis_index("dp") % 2
    core = lax.axis_index("frame") % 2
    tile = lax.axis_index("tile")
    plane = lax.axis_index("frame") // 2
    place = jnp.stack([x, core, tile, 4 * x + 2 * core + tile, plane]).astype(jnp.int32)
    flat = source.reshape(tokens, width)

    kinds = lax.dynamic_slice_in_dim(attn_weight, x * 2 * width, 2 * width, axis=1)
    kinds = kinds.reshape(share, 2, width).transpose(1, 0, 2)
    kinds = jnp.broadcast_to(kinds[None], (frames // 2,) + kinds.shape).reshape(frames, share, width)
    own = lax.all_to_all(kinds, "frame", 0, 0, tiled=True)

    along_x = swap(flat, "dp")
    along_y = swap(flat, "tile")

    lines = 3 * share // 2
    mine = lax.dynamic_slice_in_dim(conv_weight, x * (width // 2), width // 2, axis=2)
    mine = mine.reshape(3, 3, share, 4, part).transpose(3, 0, 2, 1, 4)
    mine = mine.reshape(4, 2, lines, 3 * part).transpose(1, 0, 2, 3)
    mine = jnp.broadcast_to(mine[None], (frames // 4,) + mine.shape)
    mine = mine.reshape(ranks, lines, 3 * part)
    mine, own, along_x, along_y = lax.optimization_barrier((mine, own, along_x, along_y))
    conv_half = lax.all_to_all(mine, square, 0, 0, tiled=True)

    half = tokens // 2
    across = jnp.concatenate([swap(along_x[:half], "tile"), swap(along_y[half:], "dp")])
    pieces = [flat, along_y, along_x, across]
    pieces += [swap(piece, "frame") for piece in pieces]
    cot_blocks = cot.reshape(frames, count, width)
    cot_blocks, conv_half, pieces = lax.optimization_barrier((cot_blocks, conv_half, pieces))
    cot_blocks = lax.all_to_all(cot_blocks, "frame", 0, 0, tiled=True)
    conv_other = lax.ppermute(conv_half, "frame", [(i, i ^ 2) for i in range(frames)])
    acts, kept = call(
        functools.partial(act_kernel, cols=cols, part=part),
        20,
        [((4, tiles * tokens + 2 * cols, width), BF), ((4, tiles * tokens, part), BF)],
        [],
        place,
        norm_gain[None],
        *pieces,
    )
    by_tile = swap(own, "tile")
    by_clip = swap(own, "dp")
    (conv_full,) = call(
        taps_kernel, 12, [((3, ranks, share, 3 * part), BF)], [], place, conv_half, conv_other
    )
    conv_full = conv_full.reshape(3, width, 3 * part)
    blocked = (2 * ranks, 2 * third, 3 * part)
    plain = (2, 2, tiles * tokens, part)
    (mid,) = call(
        functools.partial(conv_kernel, cols=cols, part=part, blocks=frames, count=count),
        16,
        [(plain if frames > 8 else blocked, BF)],
        [],
        place,
        conv_full,
        acts,
        kept,
    )
    if frames > 8:
        mid = mid.reshape(2, 2, tiles, frames, 3, third, part).transpose(0, 3, 2, 1, 5, 4, 6)
        mid = mid.reshape(blocked)
    mid, cot_blocks, by_tile, by_clip = lax.optimization_barrier(
        (mid, cot_blocks, by_tile, by_clip)
    )
    groups = None
    if clips > 2:
        groups = [[2 * ranks * g + i for i in range(2 * ranks)] for g in range(clips // 2)]
    mid = lax.all_to_all(mid, ("dp",) + square, 0, 0, axis_index_groups=groups, tiled=True)

    middle = frames // 2
    parts = [own, by_tile, by_clip, swap(by_clip[:middle], "tile"), swap(by_tile[middle:], "dp")]
    parts += [swap(piece, "frame") for piece in parts]
    parts, mid = lax.optimization_barrier((parts, mid))
    (attn_full,) = call(
        join_kernel, 16, [((4, frames, tiles, share, width), BF)], [], place, *parts
    )
    attn_full = attn_full.reshape(4, width, width)

    lanes = frames * SLOT
    padded = round_up(count + 3, 8)
    total = frames * padded
    scale = jnp.tile(jnp.pad(logit_scale, (0, SLOT - heads)), frames)[None]
    qgain = jnp.tile(query_gain, heads)[None]
    kgain = jnp.tile(key_gain, heads)[None]
    full = (total, width)
    double = (2 * total, width)
    narrow = (total, lanes)
    kept, sent, scale_sums, d_raw, q_hat, k_hat, q_rstd, k_rstd, d_value = call(
        functools.partial(attend_kernel, heads=heads, count=count, padded=padded, part=part),
        20,
        [
            ((2, 2, frames // 2, share, width), BF),
            ((2, 2, frames // 2, share, width), BF),
            ((1, lanes), F32), (narrow, F32),
            (full, F32), (full, F32), (narrow, F32), (narrow, F32), (full, BF),
        ],
        [
            (full, F32), (full, F32), (double, F32), (double, F32), (full, F32),
            (narrow, F32), (narrow, F32),
        ],
        place, mid, cot_blocks, attn_full, qgain, kgain, scale,
    )
    d_qn, d_kn = call(
        functools.partial(slope_kernel, heads=heads, padded=padded),
        16,
        [(full, F32), (full, F32)],
        [(double, F32), (double, F32)],
        d_raw, q_hat, k_hat, qgain, kgain,
    )

    def add(mine, theirs):
        return (mine.astype(F32) + theirs.astype(F32)).astype(BF)

    shares = add(kept, swap(sent, "frame"))
    shares, d_qn = lax.optimization_barrier((shares, d_qn))
    (d_mid,) = call(
        functools.partial(back_kernel, heads=heads, count=count, padded=padded),
        16,
        [((frames, padded, width), BF)],
        [],
        d_qn, d_kn, q_hat, k_hat, q_rstd, k_rstd, d_value, attn_full, qgain, kgain, scale_sums,
    )
    d_back = lax.all_to_all(d_mid, "frame", 0, 0, tiled=True)
    shares = add(shares[0], swap(shares[1], "dp"))
    shares = add(shares[0], swap(shares[1], "tile"))
    step = frames // 4
    while step > 0:
        pairs = [(i, i ^ (2 * step)) for i in range(frames)]
        if step == 1:
            shares, d_back = lax.optimization_barrier((shares, d_back))
        shares = add(shares[:step], lax.ppermute(shares[step:], "frame", pairs))
        step //= 2
    shares = shares[0]
    small = jnp.sum(d_back[:, count : count + 3].astype(F32), axis=(0, 1))
    d_back = d_back[:, :count].reshape(rows, cols, width)
    mid_grad = (cot.astype(F32) + d_back.astype(F32)).astype(BF)

    small = small + swap(small, "tile")
    if clips == 2:
        small = small + swap(small, "dp")
    else:
        small = lax.psum(small, "dp")
        same_clip = [[i for i in range(clips) if i % 2 == c] for c in (0, 1)]
        shares = lax.psum(shares, "dp", axis_index_groups=same_clip)
    theirs = swap(shares, "dp").astype(F32)
    shares = shares.astype(F32)
    factor = 1.0 / math.sqrt(clips * frames * tiles * tokens)
    value_grad = jnp.where(x == 0, shares, theirs) * factor
    out_proj_grad = jnp.where(x == 0, theirs, shares) * factor
    scale_sum = small[256 : 256 + heads]
    return (
        mid_grad[None, None],
        value_grad,
        out_proj_grad,
        small[:depth] * factor,
        small[128 : 128 + depth] * factor,
        scale_sum * factor,
    )


def solution(mesh):
    in_specs = (
        P("dp", "frame", "tile", None, None),
        P("dp", "frame", "tile", None, None),
        P(),
        P(None, ("frame", "tile"), None),
        P(("frame", "tile"), None),
        P(),
        P(),
        P(),
    )
    out_specs = (
        P("dp", "frame", "tile", None, None),
        P(("frame", "tile"), None),
        P(("frame", "tile"), None),
        P(),
        P(),
        P(),
    )
    return jax.shard_map(local, mesh=mesh, in_specs=in_specs, out_specs=out_specs, check_vma=False)
```

```python
import functools
import math

import jax
import jax.numpy as jnp
from jax import lax
from jax.experimental import pallas as pl
from jax.experimental.pallas import tpu as pltpu
from jax.sharding import PartitionSpec as P

GROUPS = 32
EPS = 1e-05
SLOT = 16
BF = jnp.bfloat16
F32 = jnp.float32


def swap(x, axis):
    return lax.ppermute(x, axis, [(i, i ^ 1) for i in range(lax.axis_size(axis))])


def round_up(value, unit):
    return -(-value // unit) * unit


def dot(a, b):
    return lax.dot_general(a, b, (((1,), (0,)), ((), ())), preferred_element_type=F32)


def dot_t(a, b):
    return lax.dot_general(a, b, (((1,), (1,)), ((), ())), preferred_element_type=F32)


def dot_rows(a, b):
    return lax.dot_general(a, b, (((0,), (0,)), ((), ())), preferred_element_type=F32)


def halves(x):
    high = x.astype(BF)
    return high, (x - high.astype(F32)).astype(BF)


def picker(rows, cols, depth, offset):
    row = lax.broadcasted_iota(jnp.int32, (rows, cols), 0)
    col = lax.broadcasted_iota(jnp.int32, (rows, cols), 1)
    return (col - row // depth == offset).astype(F32).astype(BF)


def spreader(rows, cols, depth, offset):
    row = lax.broadcasted_iota(jnp.int32, (rows, cols), 0)
    col = lax.broadcasted_iota(jnp.int32, (rows, cols), 1)
    return (row - col // depth == offset).astype(F32).astype(BF)


def head_sums(x, pick):
    high, low = halves(x)
    return dot(high, pick) + dot(low, pick)


def spread(x, both):
    high, low = halves(x)
    return dot(jnp.concatenate([high, low], axis=1), both)


def over_slots(x):
    step = SLOT
    while step < x.shape[1]:
        x = x + pltpu.roll(x, step, 1)
        step *= 2
    return x


def each(number, body):
    if number > 8:
        lax.fori_loop(0, number, lambda i, _: body(i), None)
    else:
        for i in range(number):
            body(i)


def join_kernel(place, *refs):
    pieces, out = (refs[:-1], refs[-1])
    x, core, tile = (place[0], place[1], place[2])
    frames = out.shape[1]
    for dc in (0, 1):
        own, by_tile, by_clip, low, high = pieces[5 * dc : 5 * dc + 5]
        own_kind = 2 * x + (core ^ dc)
        other_kind = 2 * (x ^ 1) + (core ^ dc)
        for f in range(frames):
            out[own_kind, f, tile] = own[f]
            out[own_kind, f, tile ^ 1] = by_tile[f]
            out[other_kind, f, tile] = by_clip[f]
            part, index = (low, f) if f < frames // 2 else (high, f - frames // 2)
            out[other_kind, f, tile ^ 1] = part[index]


def act_kernel(place, gain, *refs, cols, part):
    blocks, (acts, kept) = (refs[:-2], refs[-2:])
    half, width = blocks[0].shape
    tile, chosen = (place[2], place[3])
    choice = picker(width, part, 1, -part * chosen)
    per_group = width // GROUPS
    pick = picker(width, 128, per_group, 0)
    back = spreader(128, width, per_group, 0)

    def thirds(x):
        high, low = halves(x)
        return high, low, (x - high.astype(F32) - low.astype(F32)).astype(BF)

    totals, squares = ([], [])
    for frame in range(4):
        total, square = (0.0, 0.0)
        for dy in (0, 1):
            x = blocks[2 * frame + dy][...]
            start = pl.multiple_of((tile ^ dy) * half, half)
            kept[frame, pl.ds(start, half), :] = dot(x, choice).astype(BF)
            x = x.astype(F32)
            total = total + jnp.sum(x, axis=0, keepdims=True)
            square = square + jnp.sum(x * x, axis=0, keepdims=True)
        totals.append(total)
        squares.append(square)
    high, low, lowest = thirds(jnp.concatenate(totals + squares, axis=0))
    both = (dot(high, pick) + dot(low, pick) + dot(lowest, pick)) / (2 * half * per_group)
    mean = both[0:4]
    rstd = lax.rsqrt(both[4:8] - mean * mean + EPS)
    high, low, lowest = thirds(jnp.concatenate([mean, rstd], axis=0))
    both = dot(high, back) + dot(low, back) + dot(lowest, back)
    scales = both[4:8] * gain[...]
    for frame in range(4):
        acts[frame, pl.ds(0, cols), :] = jnp.zeros((cols, width), BF)
        acts[frame, pl.ds(cols + 2 * half, cols), :] = jnp.zeros((cols, width), BF)
        for dy in (0, 1):
            x = blocks[2 * frame + dy][...].astype(F32)
            zed = (x - both[frame : frame + 1]) * scales[frame : frame + 1]
            start = pl.multiple_of(cols + (tile ^ dy) * half, cols)
            acts[frame, pl.ds(start, half), :] = (zed / (1.0 + jnp.exp(-zed))).astype(BF)


def conv_kernel(place, weights, acts, kept, out, *, cols, part, blocks, count):
    x, core = (place[0], place[1])
    whole = kept.shape[1]
    half = whole // 2
    third = count // 3
    col = lax.broadcasted_iota(jnp.int32, (whole, part), 0) % cols
    for dx in (0, 1):
        mids = []
        for dc in (0, 1):
            frame = 2 * dc + dx
            taps = dot(acts[frame, pl.ds(0, whole), :], weights[0])
            taps += dot(acts[frame, pl.ds(cols, whole), :], weights[1])
            taps += dot(acts[frame, pl.ds(2 * cols, whole), :], weights[2])
            left = pltpu.roll(taps[:, :part], 1, 0)
            right = pltpu.roll(taps[:, 2 * part :], whole - 1, 0)
            pre = taps[:, part : 2 * part] + jnp.where(col > 0, left, 0.0)
            pre = pre + jnp.where(col < cols - 1, right, 0.0)
            mids.append((kept[frame].astype(F32) + pre).astype(BF))
        if blocks > 8:
            for dc in (0, 1):
                out[x ^ dx, dc] = mids[dc]
            continue
        for f in range(blocks):
            for t in (0, 1):
                start = t * half + f * count
                rows = [
                    jnp.concatenate(
                        [mid[start + third * j : start + third * (j + 1)] for j in range(3)], axis=1
                    )
                    for mid in mids
                ]
                index = ((x ^ dx) * blocks + f) * 2 + t
                out[index] = jnp.concatenate(rows, axis=0)


def attend_kernel(
    place, mid_in, cot_in, weights, qgain, kgain, scale,
    kept, sent, sums, d_raw, q_hat, k_hat, q_rstd, k_rstd, d_value,
    mid_s, cot_s, doubled, doubled_v, mixed_s, raw_s, probs_s,
    *, heads, count, padded, part,
):
    total, width = mid_s.shape
    frames = total // padded
    depth = width // heads
    lanes = scale.shape[-1]
    third = count // 3
    x, core, tile, plane = (place[0], place[1], place[2], place[4])
    mid_s[...] = jnp.zeros_like(mid_s)
    cot_s[...] = jnp.zeros_like(cot_s)
    for z in range(frames // 2):
        for e in (0, 1):
            f = 2 * z + e
            blocks = [
                mid_in[(x * frames + 2 * z + c) * 2 + t, pl.ds((e ^ c) * third, third), :]
                for x in (0, 1)
                for c in (0, 1)
                for t in (0, 1)
            ]
            for j in range(3):
                piece = [b[:, j * part : (j + 1) * part] for b in blocks]
                start = f * padded + j * third
                mid_s[pl.ds(start, third), :] = jnp.concatenate(piece, axis=1).astype(F32)
            cot_s[pl.ds(f * padded, count), :] = cot_in[f].astype(F32)
    mid = mid_s[...].astype(BF)
    cot = cot_s[...].astype(BF)
    pick = picker(width, lanes, depth, 0)
    both = jnp.concatenate([spreader(lanes, width, depth, 0)] * 2, axis=0)

    def stats(vec):
        cent = vec - spread(head_sums(vec, pick) / depth, both)
        var = head_sums(cent * cent, pick) / depth
        rstd = lax.rsqrt(var + EPS)
        return cent * spread(rstd, both), rstd

    hat, rstd = stats(dot(mid, weights[0]))
    q_hat[...] = hat
    q_rstd[...] = rstd
    q_norm = hat * qgain[...]
    hat, rstd = stats(dot(mid, weights[1]))
    k_hat[...] = hat
    k_rstd[...] = rstd
    hat = hat * kgain[...]
    doubled[pl.ds(0, total), :] = hat
    doubled[pl.ds(total, total), :] = hat
    value = dot(mid, weights[2]).astype(BF).astype(F32)
    doubled_v[pl.ds(0, total), :] = value
    doubled_v[pl.ds(total, total), :] = value
    d_mixed = dot_t(cot, weights[3]).astype(BF).astype(F32)
    raw_s[...] = jnp.zeros_like(raw_s)
    probs_s[...] = jnp.zeros_like(probs_s)

    def logits(s):
        here = picker(width, lanes, depth, SLOT * s)
        raw_s[...] += head_sums(q_norm * doubled[pl.ds(s * padded, total), :], here)
        probs_s[...] += head_sums(d_mixed * doubled_v[pl.ds(s * padded, total), :], here)

    each(frames, logits)
    raw = raw_s[...] / math.sqrt(depth)
    expo = jnp.exp(raw * scale[...])
    probs = expo / over_slots(expo)
    probs_b = probs.astype(BF)
    d_probs = probs_s[...]
    d_logits = probs * (d_probs - over_slots(probs * d_probs))
    sums[...] = jnp.sum(d_logits * raw, axis=0, keepdims=True)
    d_raw[...] = d_logits * scale[...] / math.sqrt(depth)
    mixed_s[...] = jnp.zeros_like(mixed_s)
    doubled[...] = jnp.zeros_like(doubled)

    def mix(s):
        weight = dot(probs_b, spreader(lanes, width, depth, SLOT * s))
        mixed_s[...] += weight * doubled_v[pl.ds(s * padded, total), :]
        doubled[pl.ds(s * padded, total), :] += weight * d_mixed

    each(frames, mix)
    dv = (doubled[pl.ds(0, total), :] + doubled[pl.ds(total, total), :]).astype(BF)
    d_value[...] = dv
    rows = kept.shape[3]

    def store(kind, term):
        for z in range(frames // 2):
            for t in (0, 1):
                start = (4 * z + t) * rows
                first = term[start : start + rows]
                second = term[start + 2 * rows : start + 3 * rows]
                kept[x ^ kind, tile ^ t, plane ^ z] = jnp.where(core == 0, first, second)
                sent[x ^ kind, tile ^ t, plane ^ z] = jnp.where(core == 0, second, first)

    store(1, dot_rows(mixed_s[...].astype(BF), cot).astype(BF))
    store(0, dot_rows(mid, dv).astype(BF))


def slope_kernel(
    d_raw, q_hat, k_hat, qgain, kgain,
    d_qn, d_kn,
    doubled, doubled_acc,
    *, heads, padded,
):
    total, width = q_hat.shape
    depth = width // heads
    frames = total // padded
    lanes = d_raw.shape[-1]
    k_norm = k_hat[...] * kgain[...]
    doubled[pl.ds(0, total), :] = k_norm
    doubled[pl.ds(total, total), :] = k_norm
    q_norm = q_hat[...] * qgain[...]
    doubled_acc[...] = jnp.zeros_like(doubled_acc)
    d_qn[...] = jnp.zeros_like(d_qn)
    high, low = halves(d_raw[...])
    pair = jnp.concatenate([high, low], axis=1)

    def shift(s):
        one = spreader(lanes, width, depth, SLOT * s)
        weight = dot(pair, jnp.concatenate([one, one], axis=0))
        d_qn[...] += weight * doubled[pl.ds(s * padded, total), :]
        doubled_acc[pl.ds(s * padded, total), :] += weight * q_norm

    each(frames, shift)
    d_kn[...] = doubled_acc[pl.ds(0, total), :] + doubled_acc[pl.ds(total, total), :]


def back_kernel(
    d_qn, d_kn, q_hat, k_hat, q_rstd, k_rstd, d_value, weights, qgain, kgain, scale_sums,
    d_mid,
    *, heads, count, padded,
):
    total, width = q_hat.shape
    depth = width // heads
    frames = total // padded
    lanes = scale_sums.shape[-1]
    pick = picker(width, lanes, depth, 0)
    both = jnp.concatenate([spreader(lanes, width, depth, 0)] * 2, axis=0)

    def back(dhat, hat, rstd):
        first = spread(head_sums(dhat, pick) / depth, both)
        second = spread(head_sums(dhat * hat, pick) / depth, both)
        return (spread(rstd, both) * (dhat - first - hat * second)).astype(BF)

    d_query = back(d_qn[...] * qgain[...], q_hat[...], q_rstd[...])
    d_key = back(d_kn[...] * kgain[...], k_hat[...], k_rstd[...])
    out = dot_t(d_query, weights[0])
    out += dot_t(d_key, weights[1])
    out += dot_t(d_value[...], weights[2])

    row = lax.broadcasted_iota(jnp.int32, (width, 128), 0)
    col = lax.broadcasted_iota(jnp.int32, (width, 128), 1)
    fold = (row % depth == col).astype(F32)

    def folded(d_norm, hat):
        sums = jnp.sum(d_norm * hat, axis=0, keepdims=True)
        sums = jnp.broadcast_to(sums, (8, width))
        return jnp.dot(sums, fold, precision=lax.Precision.HIGHEST, preferred_element_type=F32)[0:1]

    by_head = over_slots(jnp.broadcast_to(scale_sums[...], (8, lanes)))[0:1, :128]
    small = [folded(d_qn[...], q_hat[...]), folded(d_kn[...], k_hat[...]), by_head]
    small.append(jnp.zeros((1, width - 384), F32))
    small = jnp.concatenate(small, axis=1)
    high, low = halves(small)
    lowest = (small - high.astype(F32) - low.astype(F32)).astype(BF)
    spare = [high.astype(F32), low.astype(F32), lowest.astype(F32)]
    if padded - count > 3:
        spare.append(jnp.zeros((padded - count - 3, width), F32))
    spare = jnp.concatenate(spare, axis=0)
    for f in range(frames):
        tokens = out[f * padded : f * padded + count]
        d_mid[f] = jnp.concatenate([tokens, spare], axis=0).astype(BF)


def call(kernel, mebibytes, outs, scratch, *args):
    smem = pl.BlockSpec(memory_space=pltpu.SMEM)
    vmem = pl.BlockSpec(memory_space=pltpu.VMEM)
    return pl.pallas_call(
        kernel,
        out_shape=[jax.ShapeDtypeStruct(shape, dtype) for shape, dtype in outs],
        in_specs=[smem if arg.dtype == jnp.int32 else vmem for arg in args],
        out_specs=[vmem] * len(outs),
        scratch_shapes=[pltpu.VMEM(shape, dtype) for shape, dtype in scratch],
        compiler_params=pltpu.CompilerParams(vmem_limit_bytes=mebibytes << 20),
    )(*args)


def local(
    clip_input, cotangent, norm_gain, conv_weight, attn_weight, query_gain, key_gain, logit_scale
):
    source = clip_input[0, 0]
    cot = cotangent[0, 0]
    rows, cols, width = source.shape
    heads = logit_scale.shape[0]
    depth = width // heads
    tokens = rows * cols
    clips, frames, tiles = (lax.axis_size(name) for name in ("dp", "frame", "tile"))
    square = ("frame", "tile")
    ranks = frames * tiles
    share = conv_weight.shape[1]
    count = tokens // frames
    third = count // 3
    part = width // 8
    x = lax.axis_index("dp") % 2
    core = lax.axis_index("frame") % 2
    tile = lax.axis_index("tile")
    plane = lax.axis_index("frame") // 2
    place = jnp.stack([x, core, tile, 4 * x + 2 * core + tile, plane]).astype(jnp.int32)
    flat = source.reshape(tokens, width)

    kinds = lax.dynamic_slice_in_dim(attn_weight, x * 2 * width, 2 * width, axis=1)
    kinds = kinds.reshape(share, 2, width).transpose(1, 0, 2)
    kinds = jnp.broadcast_to(kinds[None], (frames // 2,) + kinds.shape).reshape(frames, share, width)
    own = lax.all_to_all(kinds, "frame", 0, 0, tiled=True)

    along_x = swap(flat, "dp")
    along_y = swap(flat, "tile")

    mine = lax.dynamic_slice_in_dim(conv_weight, x * (width // 2), width // 2, axis=2)
    mine = mine.reshape(3, 3, share, 4, part).transpose(3, 0, 2, 1, 4)
    mine = mine.reshape(4, 3, share, 3 * part)
    mine = jnp.broadcast_to(mine[None], (frames // 2,) + mine.shape)
    mine = mine.reshape((ranks,) + mine.shape[2:])
    mine, own, along_x, along_y = lax.optimization_barrier((mine, own, along_x, along_y))
    conv_in = lax.all_to_all(mine, square, 0, 0, tiled=True)

    half = tokens // 2
    across = jnp.concatenate([swap(along_x[:half], "tile"), swap(along_y[half:], "dp")])
    pieces = [flat, along_y, along_x, across]
    pieces += [swap(piece, "frame") for piece in pieces]
    cot_blocks = cot.reshape(frames, count, width)
    cot_blocks, conv_in, pieces = lax.optimization_barrier((cot_blocks, conv_in, pieces))
    cot_blocks = lax.all_to_all(cot_blocks, "frame", 0, 0, tiled=True)
    acts, kept = call(
        functools.partial(act_kernel, cols=cols, part=part),
        20,
        [((4, tiles * tokens + 2 * cols, width), BF), ((4, tiles * tokens, part), BF)],
        [],
        place,
        norm_gain[None],
        *pieces,
    )
    by_tile = swap(own, "tile")
    by_clip = swap(own, "dp")
    conv_full = conv_in.transpose(1, 0, 2, 3).reshape(3, width, 3 * part)
    blocked = (2 * ranks, 2 * third, 3 * part)
    plain = (2, 2, tiles * tokens, part)
    (mid,) = call(
        functools.partial(conv_kernel, cols=cols, part=part, blocks=frames, count=count),
        16,
        [(plain if frames > 8 else blocked, BF)],
        [],
        place,
        conv_full,
        acts,
        kept,
    )
    if frames > 8:
        mid = mid.reshape(2, 2, tiles, frames, 3, third, part).transpose(0, 3, 2, 1, 5, 4, 6)
        mid = mid.reshape(blocked)
    mid, cot_blocks, by_tile, by_clip = lax.optimization_barrier(
        (mid, cot_blocks, by_tile, by_clip)
    )
    groups = None
    if clips > 2:
        groups = [[2 * ranks * g + i for i in range(2 * ranks)] for g in range(clips // 2)]
    mid = lax.all_to_all(mid, ("dp",) + square, 0, 0, axis_index_groups=groups, tiled=True)

    middle = frames // 2
    parts = [own, by_tile, by_clip, swap(by_clip[:middle], "tile"), swap(by_tile[middle:], "dp")]
    parts += [swap(piece, "frame") for piece in parts]
    parts, mid = lax.optimization_barrier((parts, mid))
    (attn_full,) = call(
        join_kernel, 16, [((4, frames, tiles, share, width), BF)], [], place, *parts
    )
    attn_full = attn_full.reshape(4, width, width)

    lanes = frames * SLOT
    padded = round_up(count + 3, 8)
    total = frames * padded
    scale = jnp.tile(jnp.pad(logit_scale, (0, SLOT - heads)), frames)[None]
    qgain = jnp.tile(query_gain, heads)[None]
    kgain = jnp.tile(key_gain, heads)[None]
    full = (total, width)
    double = (2 * total, width)
    narrow = (total, lanes)
    kept, sent, scale_sums, d_raw, q_hat, k_hat, q_rstd, k_rstd, d_value = call(
        functools.partial(attend_kernel, heads=heads, count=count, padded=padded, part=part),
        20,
        [
            ((2, 2, frames // 2, share, width), BF),
            ((2, 2, frames // 2, share, width), BF),
            ((1, lanes), F32), (narrow, F32),
            (full, F32), (full, F32), (narrow, F32), (narrow, F32), (full, BF),
        ],
        [
            (full, F32), (full, F32), (double, F32), (double, F32), (full, F32),
            (narrow, F32), (narrow, F32),
        ],
        place, mid, cot_blocks, attn_full, qgain, kgain, scale,
    )
    d_qn, d_kn = call(
        functools.partial(slope_kernel, heads=heads, padded=padded),
        16,
        [(full, F32), (full, F32)],
        [(double, F32), (double, F32)],
        d_raw, q_hat, k_hat, qgain, kgain,
    )

    def add(mine, theirs):
        return (mine.astype(F32) + theirs.astype(F32)).astype(BF)

    shares = add(kept, swap(sent, "frame"))
    shares, d_qn = lax.optimization_barrier((shares, d_qn))
    (d_mid,) = call(
        functools.partial(back_kernel, heads=heads, count=count, padded=padded),
        16,
        [((frames, padded, width), BF)],
        [],
        d_qn, d_kn, q_hat, k_hat, q_rstd, k_rstd, d_value, attn_full, qgain, kgain, scale_sums,
    )
    d_back = lax.all_to_all(d_mid, "frame", 0, 0, tiled=True)
    shares = add(shares[0], swap(shares[1], "dp"))
    shares = add(shares[0], swap(shares[1], "tile"))
    step = frames // 4
    while step > 0:
        pairs = [(i, i ^ (2 * step)) for i in range(frames)]
        if step == 1:
            _, d_back = lax.optimization_barrier((shares, d_back))
        shares = add(shares[:step], lax.ppermute(shares[step:], "frame", pairs))
        step //= 2
    shares = shares[0]
    small = jnp.sum(d_back[:, count : count + 3].astype(F32), axis=(0, 1))
    d_back = d_back[:, :count].reshape(rows, cols, width)
    mid_grad = (cot.astype(F32) + d_back.astype(F32)).astype(BF)

    small = small + swap(small, "tile")
    if clips == 2:
        small = small + swap(small, "dp")
    else:
        small = lax.psum(small, "dp")
        same_clip = [[i for i in range(clips) if i % 2 == c] for c in (0, 1)]
        shares = lax.psum(shares, "dp", axis_index_groups=same_clip)
    theirs = swap(shares, "dp").astype(F32)
    shares = shares.astype(F32)
    factor = 1.0 / math.sqrt(clips * frames * tiles * tokens)
    value_grad = jnp.where(x == 0, shares, theirs) * factor
    out_proj_grad = jnp.where(x == 0, theirs, shares) * factor
    scale_sum = small[256 : 256 + heads]
    return (
        mid_grad[None, None],
        value_grad,
        out_proj_grad,
        small[:depth] * factor,
        small[128 : 128 + depth] * factor,
        scale_sum * factor,
    )


def solution(mesh):
    in_specs = (
        P("dp", "frame", "tile", None, None),
        P("dp", "frame", "tile", None, None),
        P(),
        P(None, ("frame", "tile"), None),
        P(("frame", "tile"), None),
        P(),
        P(),
        P(),
    )
    out_specs = (
        P("dp", "frame", "tile", None, None),
        P(("frame", "tile"), None),
        P(("frame", "tile"), None),
        P(),
        P(),
        P(),
    )
    return jax.shard_map(local, mesh=mesh, in_specs=in_specs, out_specs=out_specs, check_vma=False)
```

```python
import functools
import math

import jax
import jax.numpy as jnp
from jax import lax
from jax.experimental import pallas as pl
from jax.experimental.pallas import tpu as pltpu
from jax.sharding import PartitionSpec as P

GROUPS = 32
EPS = 1e-05
SLOT = 16
BF = jnp.bfloat16
F32 = jnp.float32


def swap(x, axis):
    return lax.ppermute(x, axis, [(i, i ^ 1) for i in range(lax.axis_size(axis))])


def round_up(value, unit):
    return -(-value // unit) * unit


def dot(a, b):
    return lax.dot_general(a, b, (((1,), (0,)), ((), ())), preferred_element_type=F32)


def dot_t(a, b):
    return lax.dot_general(a, b, (((1,), (1,)), ((), ())), preferred_element_type=F32)


def dot_rows(a, b):
    return lax.dot_general(a, b, (((0,), (0,)), ((), ())), preferred_element_type=F32)


def halves(x):
    high = x.astype(BF)
    return high, (x - high.astype(F32)).astype(BF)


def picker(rows, cols, depth, offset):
    row = lax.broadcasted_iota(jnp.int32, (rows, cols), 0)
    col = lax.broadcasted_iota(jnp.int32, (rows, cols), 1)
    return (col - row // depth == offset).astype(F32).astype(BF)


def spreader(rows, cols, depth, offset):
    row = lax.broadcasted_iota(jnp.int32, (rows, cols), 0)
    col = lax.broadcasted_iota(jnp.int32, (rows, cols), 1)
    return (row - col // depth == offset).astype(F32).astype(BF)


def head_sums(x, pick):
    high, low = halves(x)
    return dot(high, pick) + dot(low, pick)


def spread(x, both):
    high, low = halves(x)
    return dot(jnp.concatenate([high, low], axis=1), both)


def over_slots(x):
    step = SLOT
    while step < x.shape[1]:
        x = x + pltpu.roll(x, step, 1)
        step *= 2
    return x


def each(number, body):
    if number > 8:
        lax.fori_loop(0, number, lambda i, _: body(i), None)
    else:
        for i in range(number):
            body(i)


def join_kernel(place, *refs):
    pieces, out = (refs[:-1], refs[-1])
    x, core, tile = (place[0], place[1], place[2])
    frames = out.shape[1]
    for dc in (0, 1):
        own, by_tile, by_clip, low, high = pieces[5 * dc : 5 * dc + 5]
        own_kind = 2 * x + (core ^ dc)
        other_kind = 2 * (x ^ 1) + (core ^ dc)
        for f in range(frames):
            out[own_kind, f, tile] = own[f]
            out[own_kind, f, tile ^ 1] = by_tile[f]
            out[other_kind, f, tile] = by_clip[f]
            part, index = (low, f) if f < frames // 2 else (high, f - frames // 2)
            out[other_kind, f, tile ^ 1] = part[index]


def act_kernel(place, gain, *refs, cols, part):
    blocks, (acts, kept) = (refs[:-2], refs[-2:])
    half, width = blocks[0].shape
    tile, chosen = (place[2], place[3])
    choice = picker(width, part, 1, -part * chosen)
    per_group = width // GROUPS
    pick = picker(width, 128, per_group, 0)
    back = spreader(128, width, per_group, 0)

    def thirds(x):
        high, low = halves(x)
        return high, low, (x - high.astype(F32) - low.astype(F32)).astype(BF)

    totals, squares = ([], [])
    for frame in range(4):
        total, square = (0.0, 0.0)
        for dy in (0, 1):
            x = blocks[2 * frame + dy][...]
            start = pl.multiple_of((tile ^ dy) * half, half)
            kept[frame, pl.ds(start, half), :] = dot(x, choice).astype(BF)
            x = x.astype(F32)
            total = total + jnp.sum(x, axis=0, keepdims=True)
            square = square + jnp.sum(x * x, axis=0, keepdims=True)
        totals.append(total)
        squares.append(square)
    high, low, lowest = thirds(jnp.concatenate(totals + squares, axis=0))
    both = (dot(high, pick) + dot(low, pick) + dot(lowest, pick)) / (2 * half * per_group)
    mean = both[0:4]
    rstd = lax.rsqrt(both[4:8] - mean * mean + EPS)
    high, low, lowest = thirds(jnp.concatenate([mean, rstd], axis=0))
    both = dot(high, back) + dot(low, back) + dot(lowest, back)
    scales = both[4:8] * gain[...]
    for frame in range(4):
        acts[frame, pl.ds(0, cols), :] = jnp.zeros((cols, width), BF)
        acts[frame, pl.ds(cols + 2 * half, cols), :] = jnp.zeros((cols, width), BF)
        for dy in (0, 1):
            x = blocks[2 * frame + dy][...].astype(F32)
            zed = (x - both[frame : frame + 1]) * scales[frame : frame + 1]
            start = pl.multiple_of(cols + (tile ^ dy) * half, cols)
            acts[frame, pl.ds(start, half), :] = (zed / (1.0 + jnp.exp(-zed))).astype(BF)


def conv_kernel(place, weights, acts, kept, out, *, cols, part, blocks, count):
    x, core = (place[0], place[1])
    whole = kept.shape[1]
    half = whole // 2
    third = count // 3
    col = lax.broadcasted_iota(jnp.int32, (whole, part), 0) % cols
    for dx in (0, 1):
        mids = []
        for dc in (0, 1):
            frame = 2 * dc + dx
            taps = dot(acts[frame, pl.ds(0, whole), :], weights[0])
            taps += dot(acts[frame, pl.ds(cols, whole), :], weights[1])
            taps += dot(acts[frame, pl.ds(2 * cols, whole), :], weights[2])
            left = pltpu.roll(taps[:, :part], 1, 0)
            right = pltpu.roll(taps[:, 2 * part :], whole - 1, 0)
            pre = taps[:, part : 2 * part] + jnp.where(col > 0, left, 0.0)
            pre = pre + jnp.where(col < cols - 1, right, 0.0)
            mids.append((kept[frame].astype(F32) + pre).astype(BF))
        if blocks > 8:
            for dc in (0, 1):
                out[x ^ dx, dc] = mids[dc]
            continue
        for f in range(blocks):
            for t in (0, 1):
                start = t * half + f * count
                rows = [
                    jnp.concatenate(
                        [mid[start + third * j : start + third * (j + 1)] for j in range(3)], axis=1
                    )
                    for mid in mids
                ]
                index = ((x ^ dx) * blocks + f) * 2 + t
                out[index] = jnp.concatenate(rows, axis=0)


def attend_kernel(
    place, mid_in, cot_in, weights, qgain, kgain, scale,
    kept, sent, sums, d_raw, q_hat, k_hat, q_rstd, k_rstd, d_value,
    mid_s, cot_s, doubled, doubled_v, mixed_s, raw_s, probs_s,
    *, heads, count, padded, part,
):
    total, width = mid_s.shape
    frames = total // padded
    depth = width // heads
    lanes = scale.shape[-1]
    third = count // 3
    x, core, tile, plane = (place[0], place[1], place[2], place[4])
    mid_s[...] = jnp.zeros_like(mid_s)
    cot_s[...] = jnp.zeros_like(cot_s)
    for z in range(frames // 2):
        for e in (0, 1):
            f = 2 * z + e
            blocks = [
                mid_in[(x * frames + 2 * z + c) * 2 + t, pl.ds((e ^ c) * third, third), :]
                for x in (0, 1)
                for c in (0, 1)
                for t in (0, 1)
            ]
            for j in range(3):
                piece = [b[:, j * part : (j + 1) * part] for b in blocks]
                start = f * padded + j * third
                mid_s[pl.ds(start, third), :] = jnp.concatenate(piece, axis=1).astype(F32)
            cot_s[pl.ds(f * padded, count), :] = cot_in[f].astype(F32)
    mid = mid_s[...].astype(BF)
    cot = cot_s[...].astype(BF)
    pick = picker(width, lanes, depth, 0)
    both = jnp.concatenate([spreader(lanes, width, depth, 0)] * 2, axis=0)

    def stats(vec):
        cent = vec - spread(head_sums(vec, pick) / depth, both)
        var = head_sums(cent * cent, pick) / depth
        rstd = lax.rsqrt(var + EPS)
        return cent * spread(rstd, both), rstd

    hat, rstd = stats(dot(mid, weights[0]))
    q_hat[...] = hat
    q_rstd[...] = rstd
    q_norm = hat * qgain[...]
    hat, rstd = stats(dot(mid, weights[1]))
    k_hat[...] = hat
    k_rstd[...] = rstd
    hat = hat * kgain[...]
    doubled[pl.ds(0, total), :] = hat
    doubled[pl.ds(total, total), :] = hat
    value = dot(mid, weights[2]).astype(BF).astype(F32)
    doubled_v[pl.ds(0, total), :] = value
    doubled_v[pl.ds(total, total), :] = value
    d_mixed = dot_t(cot, weights[3]).astype(BF).astype(F32)
    raw_s[...] = jnp.zeros_like(raw_s)
    probs_s[...] = jnp.zeros_like(probs_s)

    def logits(s):
        here = picker(width, lanes, depth, SLOT * s)
        raw_s[...] += head_sums(q_norm * doubled[pl.ds(s * padded, total), :], here)
        probs_s[...] += head_sums(d_mixed * doubled_v[pl.ds(s * padded, total), :], here)

    each(frames, logits)
    raw = raw_s[...] / math.sqrt(depth)
    expo = jnp.exp(raw * scale[...])
    probs = expo / over_slots(expo)
    probs_b = probs.astype(BF)
    d_probs = probs_s[...]
    d_logits = probs * (d_probs - over_slots(probs * d_probs))
    sums[...] = jnp.sum(d_logits * raw, axis=0, keepdims=True)
    d_raw[...] = d_logits * scale[...] / math.sqrt(depth)
    mixed_s[...] = jnp.zeros_like(mixed_s)
    doubled[...] = jnp.zeros_like(doubled)

    def mix(s):
        weight = dot(probs_b, spreader(lanes, width, depth, SLOT * s))
        mixed_s[...] += weight * doubled_v[pl.ds(s * padded, total), :]
        doubled[pl.ds(s * padded, total), :] += weight * d_mixed

    each(frames, mix)
    dv = (doubled[pl.ds(0, total), :] + doubled[pl.ds(total, total), :]).astype(BF)
    d_value[...] = dv
    rows = kept.shape[3]

    def store(kind, term):
        for z in range(frames // 2):
            for t in (0, 1):
                start = (4 * z + t) * rows
                first = term[start : start + rows]
                second = term[start + 2 * rows : start + 3 * rows]
                kept[x ^ kind, tile ^ t, plane ^ z] = jnp.where(core == 0, first, second)
                sent[x ^ kind, tile ^ t, plane ^ z] = jnp.where(core == 0, second, first)

    store(1, dot_rows(mixed_s[...].astype(BF), cot).astype(BF))
    store(0, dot_rows(mid, dv).astype(BF))


def slope_kernel(
    d_raw, q_hat, k_hat, qgain, kgain,
    d_qn, d_kn,
    doubled, doubled_acc,
    *, heads, padded,
):
    total, width = q_hat.shape
    depth = width // heads
    frames = total // padded
    lanes = d_raw.shape[-1]
    k_norm = k_hat[...] * kgain[...]
    doubled[pl.ds(0, total), :] = k_norm
    doubled[pl.ds(total, total), :] = k_norm
    q_norm = q_hat[...] * qgain[...]
    doubled_acc[...] = jnp.zeros_like(doubled_acc)
    d_qn[...] = jnp.zeros_like(d_qn)
    high, low = halves(d_raw[...])
    pair = jnp.concatenate([high, low], axis=1)

    def shift(s):
        one = spreader(lanes, width, depth, SLOT * s)
        weight = dot(pair, jnp.concatenate([one, one], axis=0))
        d_qn[...] += weight * doubled[pl.ds(s * padded, total), :]
        doubled_acc[pl.ds(s * padded, total), :] += weight * q_norm

    each(frames, shift)
    d_kn[...] = doubled_acc[pl.ds(0, total), :] + doubled_acc[pl.ds(total, total), :]


def back_kernel(
    d_qn, d_kn, q_hat, k_hat, q_rstd, k_rstd, d_value, weights, qgain, kgain, scale_sums,
    d_mid,
    *, heads, count, padded,
):
    total, width = q_hat.shape
    depth = width // heads
    frames = total // padded
    lanes = scale_sums.shape[-1]
    pick = picker(width, lanes, depth, 0)
    both = jnp.concatenate([spreader(lanes, width, depth, 0)] * 2, axis=0)

    def back(dhat, hat, rstd):
        first = spread(head_sums(dhat, pick) / depth, both)
        second = spread(head_sums(dhat * hat, pick) / depth, both)
        return (spread(rstd, both) * (dhat - first - hat * second)).astype(BF)

    d_query = back(d_qn[...] * qgain[...], q_hat[...], q_rstd[...])
    d_key = back(d_kn[...] * kgain[...], k_hat[...], k_rstd[...])
    out = dot_t(d_query, weights[0])
    out += dot_t(d_key, weights[1])
    out += dot_t(d_value[...], weights[2])

    row = lax.broadcasted_iota(jnp.int32, (width, 128), 0)
    col = lax.broadcasted_iota(jnp.int32, (width, 128), 1)
    fold = (row % depth == col).astype(F32)

    def folded(d_norm, hat):
        sums = jnp.sum(d_norm * hat, axis=0, keepdims=True)
        sums = jnp.broadcast_to(sums, (8, width))
        return jnp.dot(sums, fold, precision=lax.Precision.HIGHEST, preferred_element_type=F32)[0:1]

    by_head = over_slots(jnp.broadcast_to(scale_sums[...], (8, lanes)))[0:1, :128]
    small = [folded(d_qn[...], q_hat[...]), folded(d_kn[...], k_hat[...]), by_head]
    small.append(jnp.zeros((1, width - 384), F32))
    small = jnp.concatenate(small, axis=1)
    high, low = halves(small)
    lowest = (small - high.astype(F32) - low.astype(F32)).astype(BF)
    spare = [high.astype(F32), low.astype(F32), lowest.astype(F32)]
    if padded - count > 3:
        spare.append(jnp.zeros((padded - count - 3, width), F32))
    spare = jnp.concatenate(spare, axis=0)
    for f in range(frames):
        tokens = out[f * padded : f * padded + count]
        d_mid[f] = jnp.concatenate([tokens, spare], axis=0).astype(BF)


def call(kernel, mebibytes, outs, scratch, *args):
    smem = pl.BlockSpec(memory_space=pltpu.SMEM)
    vmem = pl.BlockSpec(memory_space=pltpu.VMEM)
    return pl.pallas_call(
        kernel,
        out_shape=[jax.ShapeDtypeStruct(shape, dtype) for shape, dtype in outs],
        in_specs=[smem if arg.dtype == jnp.int32 else vmem for arg in args],
        out_specs=[vmem] * len(outs),
        scratch_shapes=[pltpu.VMEM(shape, dtype) for shape, dtype in scratch],
        compiler_params=pltpu.CompilerParams(vmem_limit_bytes=mebibytes << 20),
    )(*args)


def local(
    clip_input, cotangent, norm_gain, conv_weight, attn_weight, query_gain, key_gain, logit_scale
):
    source = clip_input[0, 0]
    cot = cotangent[0, 0]
    rows, cols, width = source.shape
    heads = logit_scale.shape[0]
    depth = width // heads
    tokens = rows * cols
    clips, frames, tiles = (lax.axis_size(name) for name in ("dp", "frame", "tile"))
    square = ("frame", "tile")
    ranks = frames * tiles
    share = conv_weight.shape[1]
    count = tokens // frames
    third = count // 3
    part = width // 8
    x = lax.axis_index("dp") % 2
    core = lax.axis_index("frame") % 2
    tile = lax.axis_index("tile")
    plane = lax.axis_index("frame") // 2
    place = jnp.stack([x, core, tile, 4 * x + 2 * core + tile, plane]).astype(jnp.int32)
    flat = source.reshape(tokens, width)

    kinds = lax.dynamic_slice_in_dim(attn_weight, x * 2 * width, 2 * width, axis=1)
    kinds = kinds.reshape(share, 2, width).transpose(1, 0, 2)
    kinds = jnp.broadcast_to(kinds[None], (frames // 2,) + kinds.shape).reshape(frames, share, width)
    own = lax.all_to_all(kinds, "frame", 0, 0, tiled=True)

    along_x = swap(flat, "dp")
    along_y = swap(flat, "tile")

    mine = lax.dynamic_slice_in_dim(conv_weight, x * (width // 2), width // 2, axis=2)
    mine = mine.reshape(3, 3, share, 4, part).transpose(3, 0, 2, 1, 4)
    mine = mine.reshape(4, 3, share, 3 * part)
    mine = jnp.broadcast_to(mine[None], (frames // 2,) + mine.shape)
    mine = mine.reshape((ranks,) + mine.shape[2:])
    mine, own, along_x, along_y = lax.optimization_barrier((mine, own, along_x, along_y))
    conv_in = lax.all_to_all(mine, square, 0, 0, tiled=True)

    half = tokens // 2
    across = jnp.concatenate([swap(along_x[:half], "tile"), swap(along_y[half:], "dp")])
    pieces = [flat, along_y, along_x, across]
    pieces += [swap(piece, "frame") for piece in pieces]
    cot_blocks = cot.reshape(frames, count, width)
    cot_blocks, conv_in, pieces = lax.optimization_barrier((cot_blocks, conv_in, pieces))
    cot_blocks = lax.all_to_all(cot_blocks, "frame", 0, 0, tiled=True)
    acts, kept = call(
        functools.partial(act_kernel, cols=cols, part=part),
        20,
        [((4, tiles * tokens + 2 * cols, width), BF), ((4, tiles * tokens, part), BF)],
        [],
        place,
        norm_gain[None],
        *pieces,
    )
    by_tile = swap(own, "tile")
    by_clip = swap(own, "dp")
    conv_full = conv_in.transpose(1, 0, 2, 3).reshape(3, width, 3 * part)
    blocked = (2 * ranks, 2 * third, 3 * part)
    plain = (2, 2, tiles * tokens, part)
    (mid,) = call(
        functools.partial(conv_kernel, cols=cols, part=part, blocks=frames, count=count),
        16,
        [(plain if frames > 8 else blocked, BF)],
        [],
        place,
        conv_full,
        acts,
        kept,
    )
    if frames > 8:
        mid = mid.reshape(2, 2, tiles, frames, 3, third, part).transpose(0, 3, 2, 1, 5, 4, 6)
        mid = mid.reshape(blocked)
    mid, cot_blocks, by_tile, by_clip = lax.optimization_barrier(
        (mid, cot_blocks, by_tile, by_clip)
    )
    groups = None
    if clips > 2:
        groups = [[2 * ranks * g + i for i in range(2 * ranks)] for g in range(clips // 2)]
    mid = lax.all_to_all(mid, ("dp",) + square, 0, 0, axis_index_groups=groups, tiled=True)

    middle = frames // 2
    parts = [own, by_tile, by_clip, swap(by_clip[:middle], "tile"), swap(by_tile[middle:], "dp")]
    parts += [swap(piece, "frame") for piece in parts]
    parts, mid = lax.optimization_barrier((parts, mid))
    (attn_full,) = call(
        join_kernel, 16, [((4, frames, tiles, share, width), BF)], [], place, *parts
    )
    attn_full = attn_full.reshape(4, width, width)

    lanes = frames * SLOT
    padded = round_up(count + 3, 8)
    total = frames * padded
    scale = jnp.tile(jnp.pad(logit_scale, (0, SLOT - heads)), frames)[None]
    qgain = jnp.tile(query_gain, heads)[None]
    kgain = jnp.tile(key_gain, heads)[None]
    full = (total, width)
    double = (2 * total, width)
    narrow = (total, lanes)
    kept, sent, scale_sums, d_raw, q_hat, k_hat, q_rstd, k_rstd, d_value = call(
        functools.partial(attend_kernel, heads=heads, count=count, padded=padded, part=part),
        20,
        [
            ((2, 2, frames // 2, share, width), BF),
            ((2, 2, frames // 2, share, width), BF),
            ((1, lanes), F32), (narrow, F32),
            (full, F32), (full, F32), (narrow, F32), (narrow, F32), (full, BF),
        ],
        [
            (full, F32), (full, F32), (double, F32), (double, F32), (full, F32),
            (narrow, F32), (narrow, F32),
        ],
        place, mid, cot_blocks, attn_full, qgain, kgain, scale,
    )
    d_qn, d_kn = call(
        functools.partial(slope_kernel, heads=heads, padded=padded),
        16,
        [(full, F32), (full, F32)],
        [(double, F32), (double, F32)],
        d_raw, q_hat, k_hat, qgain, kgain,
    )

    def add(mine, theirs):
        return (mine.astype(F32) + theirs.astype(F32)).astype(BF)

    shares = add(kept, swap(sent, "frame"))
    shares, d_qn = lax.optimization_barrier((shares, d_qn))
    (d_mid,) = call(
        functools.partial(back_kernel, heads=heads, count=count, padded=padded),
        16,
        [((frames, padded, width), BF)],
        [],
        d_qn, d_kn, q_hat, k_hat, q_rstd, k_rstd, d_value, attn_full, qgain, kgain, scale_sums,
    )
    d_back = lax.all_to_all(d_mid, "frame", 0, 0, tiled=True)
    theirs, _ = lax.optimization_barrier((swap(shares[1], "dp"), d_mid))
    shares = add(shares[0], theirs)
    shares = add(shares[0], swap(shares[1], "tile"))
    step = frames // 4
    while step > 0:
        pairs = [(i, i ^ (2 * step)) for i in range(frames)]
        if step == 1:
            _, d_back = lax.optimization_barrier((shares, d_back))
        shares = add(shares[:step], lax.ppermute(shares[step:], "frame", pairs))
        step //= 2
    shares = shares[0]
    small = jnp.sum(d_back[:, count : count + 3].astype(F32), axis=(0, 1))
    d_back = d_back[:, :count].reshape(rows, cols, width)
    mid_grad = (cot.astype(F32) + d_back.astype(F32)).astype(BF)

    small = small + swap(small, "tile")
    if clips == 2:
        small = small + swap(small, "dp")
    else:
        small = lax.psum(small, "dp")
        same_clip = [[i for i in range(clips) if i % 2 == c] for c in (0, 1)]
        shares = lax.psum(shares, "dp", axis_index_groups=same_clip)
    theirs = swap(shares, "dp").astype(F32)
    shares = shares.astype(F32)
    factor = 1.0 / math.sqrt(clips * frames * tiles * tokens)
    value_grad = jnp.where(x == 0, shares, theirs) * factor
    out_proj_grad = jnp.where(x == 0, theirs, shares) * factor
    scale_sum = small[256 : 256 + heads]
    return (
        mid_grad[None, None],
        value_grad,
        out_proj_grad,
        small[:depth] * factor,
        small[128 : 128 + depth] * factor,
        scale_sum * factor,
    )


def solution(mesh):
    in_specs = (
        P("dp", "frame", "tile", None, None),
        P("dp", "frame", "tile", None, None),
        P(),
        P(None, ("frame", "tile"), None),
        P(("frame", "tile"), None),
        P(),
        P(),
        P(),
    )
    out_specs = (
        P("dp", "frame", "tile", None, None),
        P(("frame", "tile"), None),
        P(("frame", "tile"), None),
        P(),
        P(),
        P(),
    )
    return jax.shard_map(local, mesh=mesh, in_specs=in_specs, out_specs=out_specs, check_vma=False)
```

```python
import functools
import math

import jax
import jax.numpy as jnp
from jax import lax
from jax.experimental import pallas as pl
from jax.experimental.pallas import tpu as pltpu
from jax.sharding import PartitionSpec as P

GROUPS = 32
EPS = 1e-05
SLOT = 16
BF = jnp.bfloat16
F32 = jnp.float32


def swap(x, axis):
    return lax.ppermute(x, axis, [(i, i ^ 1) for i in range(lax.axis_size(axis))])


def round_up(value, unit):
    return -(-value // unit) * unit


def dot(a, b):
    return lax.dot_general(a, b, (((1,), (0,)), ((), ())), preferred_element_type=F32)


def dot_t(a, b):
    return lax.dot_general(a, b, (((1,), (1,)), ((), ())), preferred_element_type=F32)


def dot_rows(a, b):
    return lax.dot_general(a, b, (((0,), (0,)), ((), ())), preferred_element_type=F32)


def halves(x):
    high = x.astype(BF)
    return high, (x - high.astype(F32)).astype(BF)


def picker(rows, cols, depth, offset):
    row = lax.broadcasted_iota(jnp.int32, (rows, cols), 0)
    col = lax.broadcasted_iota(jnp.int32, (rows, cols), 1)
    return (col - row // depth == offset).astype(F32).astype(BF)


def spreader(rows, cols, depth, offset):
    row = lax.broadcasted_iota(jnp.int32, (rows, cols), 0)
    col = lax.broadcasted_iota(jnp.int32, (rows, cols), 1)
    return (row - col // depth == offset).astype(F32).astype(BF)


def head_sums(x, pick):
    high, low = halves(x)
    return dot(high, pick) + dot(low, pick)


def spread(x, both):
    high, low = halves(x)
    return dot(jnp.concatenate([high, low], axis=1), both)


def over_slots(x):
    step = SLOT
    while step < x.shape[1]:
        x = x + pltpu.roll(x, step, 1)
        step *= 2
    return x


def each(number, body):
    if number > 8:
        lax.fori_loop(0, number, lambda i, _: body(i), None)
    else:
        for i in range(number):
            body(i)


def pack_kernel(place, weights, cot, out):
    share, width = (weights.shape[0], cot.shape[1])
    frames = out.shape[0]
    count = cot.shape[0] // frames
    half = share // 2
    x = place[0]
    chosen = [
        jnp.where(x == 0, weights[:, pl.ds(c * width, width)], weights[:, pl.ds((2 + c) * width, width)])
        for c in (0, 1)
    ]
    for f in range(frames):
        start = (f // 2 % 2) * half
        rows = [cot[pl.ds(f * count, count), :], chosen[f % 2][start : start + half]]
        out[f] = jnp.concatenate(rows, axis=0)


def merge_kernel(place, mine, theirs, out):
    odd = place[4] % 2
    half = mine.shape[1]
    for owner in range(mine.shape[0]):
        first = jnp.where(odd == 0, mine[owner], theirs[owner])
        second = jnp.where(odd == 0, theirs[owner], mine[owner])
        out[owner] = jnp.concatenate([first, second], axis=0)


def taps_kernel(place, mine, theirs, out):
    odd = place[4] % 2
    share = out.shape[2]
    for owner in range(mine.shape[0]):
        first = jnp.where(odd == 0, mine[owner], theirs[owner])
        second = jnp.where(odd == 0, theirs[owner], mine[owner])
        block = jnp.concatenate([first, second], axis=0)
        for row in range(3):
            out[row, owner] = block[row * share : (row + 1) * share]


def join_kernel(place, *refs):
    pieces, out = (refs[:-1], refs[-1])
    x, core, tile = (place[0], place[1], place[2])
    frames = out.shape[1]
    for dc in (0, 1):
        own, by_tile, by_clip, low, high = pieces[5 * dc : 5 * dc + 5]
        own_kind = 2 * x + (core ^ dc)
        other_kind = 2 * (x ^ 1) + (core ^ dc)
        for f in range(frames):
            out[own_kind, f, tile] = own[f]
            out[own_kind, f, tile ^ 1] = by_tile[f]
            out[other_kind, f, tile] = by_clip[f]
            part, index = (low, f) if f < frames // 2 else (high, f - frames // 2)
            out[other_kind, f, tile ^ 1] = part[index]


def act_kernel(place, gain, *refs, cols, part):
    blocks, (acts, kept) = (refs[:-2], refs[-2:])
    half, width = blocks[0].shape
    tile, chosen = (place[2], place[3])
    choice = picker(width, part, 1, -part * chosen)
    per_group = width // GROUPS
    pick = picker(width, 128, per_group, 0)
    back = spreader(128, width, per_group, 0)

    def thirds(x):
        high, low = halves(x)
        return high, low, (x - high.astype(F32) - low.astype(F32)).astype(BF)

    totals, squares = ([], [])
    for frame in range(4):
        total, square = (0.0, 0.0)
        for dy in (0, 1):
            x = blocks[2 * frame + dy][...]
            start = pl.multiple_of((tile ^ dy) * half, half)
            kept[frame, pl.ds(start, half), :] = dot(x, choice).astype(BF)
            x = x.astype(F32)
            total = total + jnp.sum(x, axis=0, keepdims=True)
            square = square + jnp.sum(x * x, axis=0, keepdims=True)
        totals.append(total)
        squares.append(square)
    high, low, lowest = thirds(jnp.concatenate(totals + squares, axis=0))
    both = (dot(high, pick) + dot(low, pick) + dot(lowest, pick)) / (2 * half * per_group)
    mean = both[0:4]
    rstd = lax.rsqrt(both[4:8] - mean * mean + EPS)
    high, low, lowest = thirds(jnp.concatenate([mean, rstd], axis=0))
    both = dot(high, back) + dot(low, back) + dot(lowest, back)
    scales = both[4:8] * gain[...]
    for frame in range(4):
        acts[frame, pl.ds(0, cols), :] = jnp.zeros((cols, width), BF)
        acts[frame, pl.ds(cols + 2 * half, cols), :] = jnp.zeros((cols, width), BF)
        for dy in (0, 1):
            x = blocks[2 * frame + dy][...].astype(F32)
            zed = (x - both[frame : frame + 1]) * scales[frame : frame + 1]
            start = pl.multiple_of(cols + (tile ^ dy) * half, cols)
            acts[frame, pl.ds(start, half), :] = (zed / (1.0 + jnp.exp(-zed))).astype(BF)


def conv_kernel(place, weights, acts, kept, out, *, cols, part, blocks, count):
    x, core = (place[0], place[1])
    whole = kept.shape[1]
    half = whole // 2
    third = count // 3
    col = lax.broadcasted_iota(jnp.int32, (whole, part), 0) % cols
    for dx in (0, 1):
        mids = []
        for dc in (0, 1):
            frame = 2 * dc + dx
            taps = dot(acts[frame, pl.ds(0, whole), :], weights[0])
            taps += dot(acts[frame, pl.ds(cols, whole), :], weights[1])
            taps += dot(acts[frame, pl.ds(2 * cols, whole), :], weights[2])
            left = pltpu.roll(taps[:, :part], 1, 0)
            right = pltpu.roll(taps[:, 2 * part :], whole - 1, 0)
            pre = taps[:, part : 2 * part] + jnp.where(col > 0, left, 0.0)
            pre = pre + jnp.where(col < cols - 1, right, 0.0)
            mids.append((kept[frame].astype(F32) + pre).astype(BF))
        if blocks > 8:
            for dc in (0, 1):
                out[x ^ dx, dc] = mids[dc]
            continue
        for f in range(blocks):
            for t in (0, 1):
                start = t * half + f * count
                rows = [
                    jnp.concatenate(
                        [mid[start + third * j : start + third * (j + 1)] for j in range(3)], axis=1
                    )
                    for mid in mids
                ]
                index = ((x ^ dx) * blocks + f) * 2 + t
                out[index] = jnp.concatenate(rows, axis=0)


def attend_kernel(
    place, mid_in, cot_in, weights, qgain, kgain, scale,
    kept, sent, sums, d_raw, q_hat, k_hat, q_rstd, k_rstd, d_value,
    mid_s, cot_s, doubled, doubled_v, mixed_s, raw_s, probs_s,
    *, heads, count, padded, part,
):
    total, width = mid_s.shape
    frames = total // padded
    depth = width // heads
    lanes = scale.shape[-1]
    third = count // 3
    x, core, tile, plane = (place[0], place[1], place[2], place[4])
    mid_s[...] = jnp.zeros_like(mid_s)
    cot_s[...] = jnp.zeros_like(cot_s)
    for z in range(frames // 2):
        for e in (0, 1):
            f = 2 * z + e
            blocks = [
                mid_in[(x * frames + 2 * z + c) * 2 + t, pl.ds((e ^ c) * third, third), :]
                for x in (0, 1)
                for c in (0, 1)
                for t in (0, 1)
            ]
            for j in range(3):
                piece = [b[:, j * part : (j + 1) * part] for b in blocks]
                start = f * padded + j * third
                mid_s[pl.ds(start, third), :] = jnp.concatenate(piece, axis=1).astype(F32)
            cot_s[pl.ds(f * padded, count), :] = cot_in[f, pl.ds(0, count), :].astype(F32)
    mid = mid_s[...].astype(BF)
    cot = cot_s[...].astype(BF)
    pick = picker(width, lanes, depth, 0)
    both = jnp.concatenate([spreader(lanes, width, depth, 0)] * 2, axis=0)

    def stats(vec):
        cent = vec - spread(head_sums(vec, pick) / depth, both)
        var = head_sums(cent * cent, pick) / depth
        rstd = lax.rsqrt(var + EPS)
        return cent * spread(rstd, both), rstd

    hat, rstd = stats(dot(mid, weights[0]))
    q_hat[...] = hat
    q_rstd[...] = rstd
    q_norm = hat * qgain[...]
    hat, rstd = stats(dot(mid, weights[1]))
    k_hat[...] = hat
    k_rstd[...] = rstd
    hat = hat * kgain[...]
    doubled[pl.ds(0, total), :] = hat
    doubled[pl.ds(total, total), :] = hat
    value = dot(mid, weights[2]).astype(BF).astype(F32)
    doubled_v[pl.ds(0, total), :] = value
    doubled_v[pl.ds(total, total), :] = value
    d_mixed = dot_t(cot, weights[3]).astype(BF).astype(F32)
    raw_s[...] = jnp.zeros_like(raw_s)
    probs_s[...] = jnp.zeros_like(probs_s)

    def logits(s):
        here = picker(width, lanes, depth, SLOT * s)
        raw_s[...] += head_sums(q_norm * doubled[pl.ds(s * padded, total), :], here)
        probs_s[...] += head_sums(d_mixed * doubled_v[pl.ds(s * padded, total), :], here)

    each(frames, logits)
    raw = raw_s[...] / math.sqrt(depth)
    expo = jnp.exp(raw * scale[...])
    probs = expo / over_slots(expo)
    probs_b = probs.astype(BF)
    d_probs = probs_s[...]
    d_logits = probs * (d_probs - over_slots(probs * d_probs))
    sums[...] = jnp.sum(d_logits * raw, axis=0, keepdims=True)
    d_raw[...] = d_logits * scale[...] / math.sqrt(depth)
    mixed_s[...] = jnp.zeros_like(mixed_s)
    doubled[...] = jnp.zeros_like(doubled)

    def mix(s):
        weight = dot(probs_b, spreader(lanes, width, depth, SLOT * s))
        mixed_s[...] += weight * doubled_v[pl.ds(s * padded, total), :]
        doubled[pl.ds(s * padded, total), :] += weight * d_mixed

    each(frames, mix)
    dv = (doubled[pl.ds(0, total), :] + doubled[pl.ds(total, total), :]).astype(BF)
    d_value[...] = dv
    rows = kept.shape[3]

    def store(kind, term):
        for z in range(frames // 2):
            for t in (0, 1):
                start = (4 * z + t) * rows
                first = term[start : start + rows]
                second = term[start + 2 * rows : start + 3 * rows]
                kept[x ^ kind, tile ^ t, plane ^ z] = jnp.where(core == 0, first, second)
                sent[x ^ kind, tile ^ t, plane ^ z] = jnp.where(core == 0, second, first)

    store(1, dot_rows(mixed_s[...].astype(BF), cot).astype(BF))
    store(0, dot_rows(mid, dv).astype(BF))


def slope_kernel(
    d_raw, q_hat, k_hat, qgain, kgain,
    d_qn, d_kn,
    doubled, doubled_acc,
    *, heads, padded,
):
    total, width = q_hat.shape
    depth = width // heads
    frames = total // padded
    lanes = d_raw.shape[-1]
    k_norm = k_hat[...] * kgain[...]
    doubled[pl.ds(0, total), :] = k_norm
    doubled[pl.ds(total, total), :] = k_norm
    q_norm = q_hat[...] * qgain[...]
    doubled_acc[...] = jnp.zeros_like(doubled_acc)
    d_qn[...] = jnp.zeros_like(d_qn)
    high, low = halves(d_raw[...])
    pair = jnp.concatenate([high, low], axis=1)

    def shift(s):
        one = spreader(lanes, width, depth, SLOT * s)
        weight = dot(pair, jnp.concatenate([one, one], axis=0))
        d_qn[...] += weight * doubled[pl.ds(s * padded, total), :]
        doubled_acc[pl.ds(s * padded, total), :] += weight * q_norm

    each(frames, shift)
    d_kn[...] = doubled_acc[pl.ds(0, total), :] + doubled_acc[pl.ds(total, total), :]


def back_kernel(
    d_qn, d_kn, q_hat, k_hat, q_rstd, k_rstd, d_value, weights, qgain, kgain, scale_sums,
    d_mid,
    *, heads, count, padded,
):
    total, width = q_hat.shape
    depth = width // heads
    frames = total // padded
    lanes = scale_sums.shape[-1]
    pick = picker(width, lanes, depth, 0)
    both = jnp.concatenate([spreader(lanes, width, depth, 0)] * 2, axis=0)

    def back(dhat, hat, rstd):
        first = spread(head_sums(dhat, pick) / depth, both)
        second = spread(head_sums(dhat * hat, pick) / depth, both)
        return (spread(rstd, both) * (dhat - first - hat * second)).astype(BF)

    d_query = back(d_qn[...] * qgain[...], q_hat[...], q_rstd[...])
    d_key = back(d_kn[...] * kgain[...], k_hat[...], k_rstd[...])
    out = dot_t(d_query, weights[0])
    out += dot_t(d_key, weights[1])
    out += dot_t(d_value[...], weights[2])

    row = lax.broadcasted_iota(jnp.int32, (width, 128), 0)
    col = lax.broadcasted_iota(jnp.int32, (width, 128), 1)
    fold = (row % depth == col).astype(F32)

    def folded(d_norm, hat):
        sums = jnp.sum(d_norm * hat, axis=0, keepdims=True)
        sums = jnp.broadcast_to(sums, (8, width))
        return jnp.dot(sums, fold, precision=lax.Precision.HIGHEST, preferred_element_type=F32)[0:1]

    by_head = over_slots(jnp.broadcast_to(scale_sums[...], (8, lanes)))[0:1, :128]
    small = [folded(d_qn[...], q_hat[...]), folded(d_kn[...], k_hat[...]), by_head]
    small.append(jnp.zeros((1, width - 384), F32))
    small = jnp.concatenate(small, axis=1)
    high, low = halves(small)
    lowest = (small - high.astype(F32) - low.astype(F32)).astype(BF)
    spare = [high.astype(F32), low.astype(F32), lowest.astype(F32)]
    if padded - count > 3:
        spare.append(jnp.zeros((padded - count - 3, width), F32))
    spare = jnp.concatenate(spare, axis=0)
    for f in range(frames):
        tokens = out[f * padded : f * padded + count]
        d_mid[f] = jnp.concatenate([tokens, spare], axis=0).astype(BF)


def call(kernel, mebibytes, outs, scratch, *args):
    smem = pl.BlockSpec(memory_space=pltpu.SMEM)
    vmem = pl.BlockSpec(memory_space=pltpu.VMEM)
    return pl.pallas_call(
        kernel,
        out_shape=[jax.ShapeDtypeStruct(shape, dtype) for shape, dtype in outs],
        in_specs=[smem if arg.dtype == jnp.int32 else vmem for arg in args],
        out_specs=[vmem] * len(outs),
        scratch_shapes=[pltpu.VMEM(shape, dtype) for shape, dtype in scratch],
        compiler_params=pltpu.CompilerParams(vmem_limit_bytes=mebibytes << 20),
    )(*args)


def local(
    clip_input, cotangent, norm_gain, conv_weight, attn_weight, query_gain, key_gain, logit_scale
):
    source = clip_input[0, 0]
    cot = cotangent[0, 0]
    rows, cols, width = source.shape
    heads = logit_scale.shape[0]
    depth = width // heads
    tokens = rows * cols
    clips, frames, tiles = (lax.axis_size(name) for name in ("dp", "frame", "tile"))
    square = ("frame", "tile")
    ranks = frames * tiles
    share = conv_weight.shape[1]
    count = tokens // frames
    third = count // 3
    part = width // 8
    x = lax.axis_index("dp") % 2
    core = lax.axis_index("frame") % 2
    tile = lax.axis_index("tile")
    plane = lax.axis_index("frame") // 2
    place = jnp.stack([x, core, tile, 4 * x + 2 * core + tile, plane]).astype(jnp.int32)
    flat = source.reshape(tokens, width)

    (packed,) = call(
        pack_kernel,
        12,
        [((frames, count + share // 2, width), BF)],
        [],
        place,
        attn_weight,
        cot.reshape(tokens, width),
    )
    packed = lax.all_to_all(packed, "frame", 0, 0, tiled=True)

    half = tokens // 2
    along_x = swap(flat, "dp")
    along_y = swap(flat, "tile")
    across = jnp.concatenate([swap(along_x[:half], "tile"), swap(along_y[half:], "dp")])
    pieces = [flat, along_y, along_x, across]
    pieces += [swap(piece, "frame") for piece in pieces]

    planes = [(i, i ^ 2) for i in range(frames)]
    lines = 3 * share // 2
    mine = lax.dynamic_slice_in_dim(conv_weight, x * (width // 2), width // 2, axis=2)
    mine = mine.reshape(3, 3, share, 4, part).transpose(3, 0, 2, 1, 4)
    mine = mine.reshape(4, 2, lines, 3 * part).transpose(1, 0, 2, 3)
    mine = jnp.broadcast_to(mine[None], (frames // 4,) + mine.shape)
    mine = mine.reshape(ranks, lines, 3 * part)
    mine, packed, pieces = lax.optimization_barrier((mine, packed, pieces))
    conv_half = lax.all_to_all(mine, square, 0, 0, tiled=True)
    own = packed[:, count:]
    own_other = lax.ppermute(own, "frame", planes)
    conv_other = lax.ppermute(conv_half, "frame", planes)
    acts, kept = call(
        functools.partial(act_kernel, cols=cols, part=part),
        20,
        [((4, tiles * tokens + 2 * cols, width), BF), ((4, tiles * tokens, part), BF)],
        [],
        place,
        norm_gain[None],
        *pieces,
    )
    (conv_full,) = call(
        taps_kernel, 12, [((3, ranks, share, 3 * part), BF)], [], place, conv_half, conv_other
    )
    conv_full = conv_full.reshape(3, width, 3 * part)
    (own,) = call(merge_kernel, 8, [((frames, share, width), BF)], [], place, own, own_other)
    by_tile = swap(own, "tile")
    by_clip = swap(own, "dp")
    blocked = (2 * ranks, 2 * third, 3 * part)
    plain = (2, 2, tiles * tokens, part)
    (mid,) = call(
        functools.partial(conv_kernel, cols=cols, part=part, blocks=frames, count=count),
        16,
        [(plain if frames > 8 else blocked, BF)],
        [],
        place,
        conv_full,
        acts,
        kept,
    )
    if frames > 8:
        mid = mid.reshape(2, 2, tiles, frames, 3, third, part).transpose(0, 3, 2, 1, 5, 4, 6)
        mid = mid.reshape(blocked)
    mid, by_tile, by_clip = lax.optimization_barrier((mid, by_tile, by_clip))
    groups = None
    if clips > 2:
        groups = [[2 * ranks * g + i for i in range(2 * ranks)] for g in range(clips // 2)]
    mid = lax.all_to_all(mid, ("dp",) + square, 0, 0, axis_index_groups=groups, tiled=True)

    middle = frames // 2
    parts = [own, by_tile, by_clip, swap(by_clip[:middle], "tile"), swap(by_tile[middle:], "dp")]
    parts += [swap(piece, "frame") for piece in parts]
    parts, mid = lax.optimization_barrier((parts, mid))
    (attn_full,) = call(
        join_kernel, 16, [((4, frames, tiles, share, width), BF)], [], place, *parts
    )
    attn_full = attn_full.reshape(4, width, width)

    lanes = frames * SLOT
    padded = round_up(count + 3, 8)
    total = frames * padded
    scale = jnp.tile(jnp.pad(logit_scale, (0, SLOT - heads)), frames)[None]
    qgain = jnp.tile(query_gain, heads)[None]
    kgain = jnp.tile(key_gain, heads)[None]
    full = (total, width)
    double = (2 * total, width)
    narrow = (total, lanes)
    kept, sent, scale_sums, d_raw, q_hat, k_hat, q_rstd, k_rstd, d_value = call(
        functools.partial(attend_kernel, heads=heads, count=count, padded=padded, part=part),
        20,
        [
            ((2, 2, frames // 2, share, width), BF),
            ((2, 2, frames // 2, share, width), BF),
            ((1, lanes), F32), (narrow, F32),
            (full, F32), (full, F32), (narrow, F32), (narrow, F32), (full, BF),
        ],
        [
            (full, F32), (full, F32), (double, F32), (double, F32), (full, F32),
            (narrow, F32), (narrow, F32),
        ],
        place, mid, packed, attn_full, qgain, kgain, scale,
    )
    d_qn, d_kn = call(
        functools.partial(slope_kernel, heads=heads, padded=padded),
        16,
        [(full, F32), (full, F32)],
        [(double, F32), (double, F32)],
        d_raw, q_hat, k_hat, qgain, kgain,
    )

    def add(mine, theirs):
        return (mine.astype(F32) + theirs.astype(F32)).astype(BF)

    shares = add(kept, swap(sent, "frame"))
    shares, d_qn = lax.optimization_barrier((shares, d_qn))
    (d_mid,) = call(
        functools.partial(back_kernel, heads=heads, count=count, padded=padded),
        16,
        [((frames, padded, width), BF)],
        [],
        d_qn, d_kn, q_hat, k_hat, q_rstd, k_rstd, d_value, attn_full, qgain, kgain, scale_sums,
    )
    d_back = lax.all_to_all(d_mid, "frame", 0, 0, tiled=True)
    theirs, _ = lax.optimization_barrier((swap(shares[1], "dp"), d_mid))
    shares = add(shares[0], theirs)
    shares = add(shares[0], swap(shares[1], "tile"))
    shares, d_back = lax.optimization_barrier((shares, d_back))
    step = frames // 4
    while step > 0:
        pairs = [(i, i ^ (2 * step)) for i in range(frames)]
        shares = add(shares[:step], lax.ppermute(shares[step:], "frame", pairs))
        step //= 2
    shares = shares[0]
    small = jnp.sum(d_back[:, count : count + 3].astype(F32), axis=(0, 1))
    d_back = d_back[:, :count].reshape(rows, cols, width)
    mid_grad = (cot.astype(F32) + d_back.astype(F32)).astype(BF)

    small = small + swap(small, "tile")
    if clips == 2:
        small = small + swap(small, "dp")
    else:
        small = lax.psum(small, "dp")
        same_clip = [[i for i in range(clips) if i % 2 == c] for c in (0, 1)]
        shares = lax.psum(shares, "dp", axis_index_groups=same_clip)
    theirs = swap(shares, "dp").astype(F32)
    shares = shares.astype(F32)
    factor = 1.0 / math.sqrt(clips * frames * tiles * tokens)
    value_grad = jnp.where(x == 0, shares, theirs) * factor
    out_proj_grad = jnp.where(x == 0, theirs, shares) * factor
    scale_sum = small[256 : 256 + heads]
    return (
        mid_grad[None, None],
        value_grad,
        out_proj_grad,
        small[:depth] * factor,
        small[128 : 128 + depth] * factor,
        scale_sum * factor,
    )


def solution(mesh):
    in_specs = (
        P("dp", "frame", "tile", None, None),
        P("dp", "frame", "tile", None, None),
        P(),
        P(None, ("frame", "tile"), None),
        P(("frame", "tile"), None),
        P(),
        P(),
        P(),
    )
    out_specs = (
        P("dp", "frame", "tile", None, None),
        P(("frame", "tile"), None),
        P(("frame", "tile"), None),
        P(),
        P(),
        P(),
    )
    return jax.shard_map(local, mesh=mesh, in_specs=in_specs, out_specs=out_specs, check_vma=False)
```

```python
import functools
import math

import jax
import jax.numpy as jnp
from jax import lax
from jax.experimental import pallas as pl
from jax.experimental.pallas import tpu as pltpu
from jax.sharding import PartitionSpec as P

GROUPS = 32
EPS = 1e-05
SLOT = 16
BF = jnp.bfloat16
F32 = jnp.float32


def swap(x, axis):
    return lax.ppermute(x, axis, [(i, i ^ 1) for i in range(lax.axis_size(axis))])


def swap_both(x, axis, bit):
    sizes = (lax.axis_size("dp"), lax.axis_size(axis))
    pairs = [
        (i * sizes[1] + j, (i ^ 1) * sizes[1] + (j ^ bit))
        for i in range(sizes[0])
        for j in range(sizes[1])
    ]
    return lax.ppermute(x, ("dp", axis), pairs)


def round_up(value, unit):
    return -(-value // unit) * unit


def dot(a, b):
    return lax.dot_general(a, b, (((1,), (0,)), ((), ())), preferred_element_type=F32)


def dot_t(a, b):
    return lax.dot_general(a, b, (((1,), (1,)), ((), ())), preferred_element_type=F32)


def dot_rows(a, b):
    return lax.dot_general(a, b, (((0,), (0,)), ((), ())), preferred_element_type=F32)


def halves(x):
    high = x.astype(BF)
    return high, (x - high.astype(F32)).astype(BF)


def picker(rows, cols, depth, offset):
    row = lax.broadcasted_iota(jnp.int32, (rows, cols), 0)
    col = lax.broadcasted_iota(jnp.int32, (rows, cols), 1)
    return (col - row // depth == offset).astype(F32).astype(BF)


def spreader(rows, cols, depth, offset):
    row = lax.broadcasted_iota(jnp.int32, (rows, cols), 0)
    col = lax.broadcasted_iota(jnp.int32, (rows, cols), 1)
    return (row - col // depth == offset).astype(F32).astype(BF)


def head_sums(x, pick):
    high, low = halves(x)
    return dot(high, pick) + dot(low, pick)


def spread(x, both):
    high, low = halves(x)
    return dot(jnp.concatenate([high, low], axis=1), both)


def over_slots(x):
    step = SLOT
    while step < x.shape[1]:
        x = x + pltpu.roll(x, step, 1)
        step *= 2
    return x


def each(number, body):
    if number > 8:
        lax.fori_loop(0, number, lambda i, _: body(i), None)
    else:
        for i in range(number):
            body(i)


def pack_kernel(place, weights, cot, out):
    share, width = (weights.shape[0], cot.shape[1])
    frames = out.shape[0]
    count = cot.shape[0] // frames
    half = share // 2
    x = place[0]
    chosen = [
        jnp.where(x == 0, weights[:, pl.ds(c * width, width)], weights[:, pl.ds((2 + c) * width, width)])
        for c in (0, 1)
    ]
    for f in range(frames):
        start = (f // 2 % 2) * half
        rows = [cot[pl.ds(f * count, count), :], chosen[f % 2][start : start + half]]
        out[f] = jnp.concatenate(rows, axis=0)


def merge_kernel(place, mine, theirs, out):
    odd = place[4] % 2
    half = mine.shape[1]
    for owner in range(mine.shape[0]):
        first = jnp.where(odd == 0, mine[owner], theirs[owner])
        second = jnp.where(odd == 0, theirs[owner], mine[owner])
        out[owner] = jnp.concatenate([first, second], axis=0)


def join_kernel(place, *refs):
    pieces, out = (refs[:-1], refs[-1])
    x, core, tile = (place[0], place[1], place[2])
    frames = out.shape[1]
    for dc in (0, 1):
        own, by_tile, by_clip, low, high = pieces[5 * dc : 5 * dc + 5]
        own_kind = 2 * x + (core ^ dc)
        other_kind = 2 * (x ^ 1) + (core ^ dc)
        for f in range(frames):
            out[own_kind, f, tile] = own[f]
            out[own_kind, f, tile ^ 1] = by_tile[f]
            out[other_kind, f, tile] = by_clip[f]
            part, index = (low, f) if f < frames // 2 else (high, f - frames // 2)
            out[other_kind, f, tile ^ 1] = part[index]


def act_kernel(place, gain, *refs, cols, part):
    blocks, (acts, kept) = (refs[:-2], refs[-2:])
    half, width = blocks[0].shape
    tile, chosen = (place[2], place[3])
    choice = picker(width, part, 1, -part * chosen)
    per_group = width // GROUPS
    pick = picker(width, 128, per_group, 0)
    back = spreader(128, width, per_group, 0)

    def thirds(x):
        high, low = halves(x)
        return high, low, (x - high.astype(F32) - low.astype(F32)).astype(BF)

    totals, squares = ([], [])
    for frame in range(4):
        total, square = (0.0, 0.0)
        for dy in (0, 1):
            x = blocks[2 * frame + dy][...]
            start = pl.multiple_of((tile ^ dy) * half, half)
            kept[frame, pl.ds(start, half), :] = dot(x, choice).astype(BF)
            x = x.astype(F32)
            total = total + jnp.sum(x, axis=0, keepdims=True)
            square = square + jnp.sum(x * x, axis=0, keepdims=True)
        totals.append(total)
        squares.append(square)
    high, low, lowest = thirds(jnp.concatenate(totals + squares, axis=0))
    both = (dot(high, pick) + dot(low, pick) + dot(lowest, pick)) / (2 * half * per_group)
    mean = both[0:4]
    rstd = lax.rsqrt(both[4:8] - mean * mean + EPS)
    high, low, lowest = thirds(jnp.concatenate([mean, rstd], axis=0))
    both = dot(high, back) + dot(low, back) + dot(lowest, back)
    scales = both[4:8] * gain[...]
    for frame in range(4):
        acts[frame, pl.ds(0, cols), :] = jnp.zeros((cols, width), BF)
        acts[frame, pl.ds(cols + 2 * half, cols), :] = jnp.zeros((cols, width), BF)
        for dy in (0, 1):
            x = blocks[2 * frame + dy][...].astype(F32)
            zed = (x - both[frame : frame + 1]) * scales[frame : frame + 1]
            start = pl.multiple_of(cols + (tile ^ dy) * half, cols)
            acts[frame, pl.ds(start, half), :] = (zed / (1.0 + jnp.exp(-zed))).astype(BF)


def conv_kernel(place, weights, acts, kept, out, *, cols, part, blocks, count):
    x, core = (place[0], place[1])
    whole = kept.shape[1]
    half = whole // 2
    third = count // 3
    col = lax.broadcasted_iota(jnp.int32, (whole, part), 0) % cols
    for dx in (0, 1):
        mids = []
        for dc in (0, 1):
            frame = 2 * dc + dx
            taps = dot(acts[frame, pl.ds(0, whole), :], weights[0])
            taps += dot(acts[frame, pl.ds(cols, whole), :], weights[1])
            taps += dot(acts[frame, pl.ds(2 * cols, whole), :], weights[2])
            left = pltpu.roll(taps[:, :part], 1, 0)
            right = pltpu.roll(taps[:, 2 * part :], whole - 1, 0)
            pre = taps[:, part : 2 * part] + jnp.where(col > 0, left, 0.0)
            pre = pre + jnp.where(col < cols - 1, right, 0.0)
            mids.append((kept[frame].astype(F32) + pre).astype(BF))
        if blocks > 8:
            for dc in (0, 1):
                out[x ^ dx, dc] = mids[dc]
            continue
        for f in range(blocks):
            for t in (0, 1):
                start = t * half + f * count
                rows = [
                    jnp.concatenate(
                        [mid[start + third * j : start + third * (j + 1)] for j in range(3)], axis=1
                    )
                    for mid in mids
                ]
                index = ((x ^ dx) * blocks + f) * 2 + t
                out[index] = jnp.concatenate(rows, axis=0)


def attend_kernel(
    place, mid_in, cot_in, weights, qgain, kgain, scale,
    kept, sent, sums, d_raw, q_hat, k_hat, q_rstd, k_rstd, d_value,
    mid_s, cot_s, doubled, doubled_v, mixed_s, raw_s, probs_s,
    *, heads, count, padded, part,
):
    total, width = mid_s.shape
    frames = total // padded
    depth = width // heads
    lanes = scale.shape[-1]
    third = count // 3
    x, core, tile, plane = (place[0], place[1], place[2], place[4])
    mid_s[...] = jnp.zeros_like(mid_s)
    cot_s[...] = jnp.zeros_like(cot_s)
    for z in range(frames // 2):
        for e in (0, 1):
            f = 2 * z + e
            blocks = [
                mid_in[(x * frames + 2 * z + c) * 2 + t, pl.ds((e ^ c) * third, third), :]
                for x in (0, 1)
                for c in (0, 1)
                for t in (0, 1)
            ]
            for j in range(3):
                piece = [b[:, j * part : (j + 1) * part] for b in blocks]
                start = f * padded + j * third
                mid_s[pl.ds(start, third), :] = jnp.concatenate(piece, axis=1).astype(F32)
            cot_s[pl.ds(f * padded, count), :] = cot_in[f, pl.ds(0, count), :].astype(F32)
    mid = mid_s[...].astype(BF)
    cot = cot_s[...].astype(BF)
    pick = picker(width, lanes, depth, 0)
    both = jnp.concatenate([spreader(lanes, width, depth, 0)] * 2, axis=0)

    def stats(vec):
        cent = vec - spread(head_sums(vec, pick) / depth, both)
        var = head_sums(cent * cent, pick) / depth
        rstd = lax.rsqrt(var + EPS)
        return cent * spread(rstd, both), rstd

    hat, rstd = stats(dot(mid, weights[0]))
    q_hat[...] = hat
    q_rstd[...] = rstd
    q_norm = hat * qgain[...]
    hat, rstd = stats(dot(mid, weights[1]))
    k_hat[...] = hat
    k_rstd[...] = rstd
    hat = hat * kgain[...]
    doubled[pl.ds(0, total), :] = hat
    doubled[pl.ds(total, total), :] = hat
    value = dot(mid, weights[2]).astype(BF).astype(F32)
    doubled_v[pl.ds(0, total), :] = value
    doubled_v[pl.ds(total, total), :] = value
    d_mixed = dot_t(cot, weights[3]).astype(BF).astype(F32)
    raw_s[...] = jnp.zeros_like(raw_s)
    probs_s[...] = jnp.zeros_like(probs_s)

    def logits(s):
        here = picker(width, lanes, depth, SLOT * s)
        raw_s[...] += head_sums(q_norm * doubled[pl.ds(s * padded, total), :], here)
        probs_s[...] += head_sums(d_mixed * doubled_v[pl.ds(s * padded, total), :], here)

    each(frames, logits)
    raw = raw_s[...] / math.sqrt(depth)
    expo = jnp.exp(raw * scale[...])
    probs = expo / over_slots(expo)
    probs_b = probs.astype(BF)
    d_probs = probs_s[...]
    d_logits = probs * (d_probs - over_slots(probs * d_probs))
    sums[...] = jnp.sum(d_logits * raw, axis=0, keepdims=True)
    d_raw[...] = d_logits * scale[...] / math.sqrt(depth)
    mixed_s[...] = jnp.zeros_like(mixed_s)
    doubled[...] = jnp.zeros_like(doubled)

    def mix(s):
        weight = dot(probs_b, spreader(lanes, width, depth, SLOT * s))
        mixed_s[...] += weight * doubled_v[pl.ds(s * padded, total), :]
        doubled[pl.ds(s * padded, total), :] += weight * d_mixed

    each(frames, mix)
    dv = (doubled[pl.ds(0, total), :] + doubled[pl.ds(total, total), :]).astype(BF)
    d_value[...] = dv
    rows = kept.shape[3]

    def store(kind, term):
        for z in range(frames // 2):
            for t in (0, 1):
                start = (4 * z + t) * rows
                first = term[start : start + rows]
                second = term[start + 2 * rows : start + 3 * rows]
                kept[x ^ kind, tile ^ t, plane ^ z] = jnp.where(core == 0, first, second)
                sent[x ^ kind, tile ^ t, plane ^ z] = jnp.where(core == 0, second, first)

    store(1, dot_rows(mixed_s[...].astype(BF), cot).astype(BF))
    store(0, dot_rows(mid, dv).astype(BF))


def slope_kernel(
    d_raw, q_hat, k_hat, qgain, kgain,
    d_qn, d_kn,
    doubled, doubled_acc,
    *, heads, padded,
):
    total, width = q_hat.shape
    depth = width // heads
    frames = total // padded
    lanes = d_raw.shape[-1]
    k_norm = k_hat[...] * kgain[...]
    doubled[pl.ds(0, total), :] = k_norm
    doubled[pl.ds(total, total), :] = k_norm
    q_norm = q_hat[...] * qgain[...]
    doubled_acc[...] = jnp.zeros_like(doubled_acc)
    d_qn[...] = jnp.zeros_like(d_qn)
    high, low = halves(d_raw[...])
    pair = jnp.concatenate([high, low], axis=1)

    def shift(s):
        one = spreader(lanes, width, depth, SLOT * s)
        weight = dot(pair, jnp.concatenate([one, one], axis=0))
        d_qn[...] += weight * doubled[pl.ds(s * padded, total), :]
        doubled_acc[pl.ds(s * padded, total), :] += weight * q_norm

    each(frames, shift)
    d_kn[...] = doubled_acc[pl.ds(0, total), :] + doubled_acc[pl.ds(total, total), :]


def back_kernel(
    d_qn, d_kn, q_hat, k_hat, q_rstd, k_rstd, d_value, weights, qgain, kgain, scale_sums,
    d_mid,
    *, heads, count, padded,
):
    total, width = q_hat.shape
    depth = width // heads
    frames = total // padded
    lanes = scale_sums.shape[-1]
    pick = picker(width, lanes, depth, 0)
    both = jnp.concatenate([spreader(lanes, width, depth, 0)] * 2, axis=0)

    def back(dhat, hat, rstd):
        first = spread(head_sums(dhat, pick) / depth, both)
        second = spread(head_sums(dhat * hat, pick) / depth, both)
        return (spread(rstd, both) * (dhat - first - hat * second)).astype(BF)

    d_query = back(d_qn[...] * qgain[...], q_hat[...], q_rstd[...])
    d_key = back(d_kn[...] * kgain[...], k_hat[...], k_rstd[...])
    out = dot_t(d_query, weights[0])
    out += dot_t(d_key, weights[1])
    out += dot_t(d_value[...], weights[2])

    row = lax.broadcasted_iota(jnp.int32, (width, 128), 0)
    col = lax.broadcasted_iota(jnp.int32, (width, 128), 1)
    fold = (row % depth == col).astype(F32)

    def folded(d_norm, hat):
        sums = jnp.sum(d_norm * hat, axis=0, keepdims=True)
        sums = jnp.broadcast_to(sums, (8, width))
        return jnp.dot(sums, fold, precision=lax.Precision.HIGHEST, preferred_element_type=F32)[0:1]

    by_head = over_slots(jnp.broadcast_to(scale_sums[...], (8, lanes)))[0:1, :128]
    small = [folded(d_qn[...], q_hat[...]), folded(d_kn[...], k_hat[...]), by_head]
    small.append(jnp.zeros((1, width - 384), F32))
    small = jnp.concatenate(small, axis=1)
    high, low = halves(small)
    lowest = (small - high.astype(F32) - low.astype(F32)).astype(BF)
    spare = [high.astype(F32), low.astype(F32), lowest.astype(F32)]
    if padded - count > 3:
        spare.append(jnp.zeros((padded - count - 3, width), F32))
    spare = jnp.concatenate(spare, axis=0)
    for f in range(frames):
        tokens = out[f * padded : f * padded + count]
        d_mid[f] = jnp.concatenate([tokens, spare], axis=0).astype(BF)


def call(kernel, mebibytes, outs, scratch, *args):
    smem = pl.BlockSpec(memory_space=pltpu.SMEM)
    vmem = pl.BlockSpec(memory_space=pltpu.VMEM)
    return pl.pallas_call(
        kernel,
        out_shape=[jax.ShapeDtypeStruct(shape, dtype) for shape, dtype in outs],
        in_specs=[smem if arg.dtype == jnp.int32 else vmem for arg in args],
        out_specs=[vmem] * len(outs),
        scratch_shapes=[pltpu.VMEM(shape, dtype) for shape, dtype in scratch],
        compiler_params=pltpu.CompilerParams(vmem_limit_bytes=mebibytes << 20),
    )(*args)


def local(
    clip_input, cotangent, norm_gain, conv_weight, attn_weight, query_gain, key_gain, logit_scale
):
    source = clip_input[0, 0]
    cot = cotangent[0, 0]
    rows, cols, width = source.shape
    heads = logit_scale.shape[0]
    depth = width // heads
    tokens = rows * cols
    clips, frames, tiles = (lax.axis_size(name) for name in ("dp", "frame", "tile"))
    square = ("frame", "tile")
    ranks = frames * tiles
    share = conv_weight.shape[1]
    count = tokens // frames
    third = count // 3
    part = width // 8
    x = lax.axis_index("dp") % 2
    core = lax.axis_index("frame") % 2
    tile = lax.axis_index("tile")
    plane = lax.axis_index("frame") // 2
    place = jnp.stack([x, core, tile, 4 * x + 2 * core + tile, plane]).astype(jnp.int32)
    flat = source.reshape(tokens, width)

    (packed,) = call(
        pack_kernel,
        12,
        [((frames, count + share // 2, width), BF)],
        [],
        place,
        attn_weight,
        cot.reshape(tokens, width),
    )
    flat, packed = lax.optimization_barrier((flat, packed))
    packed = lax.all_to_all(packed, "frame", 0, 0, tiled=True)

    half = tokens // 2
    along_x = swap(flat, "dp")
    along_y = swap(flat, "tile")
    across = jnp.concatenate([swap(along_x[:half], "tile"), swap(along_y[half:], "dp")])
    pieces = [flat, along_y, along_x, across]
    pieces += [swap(piece, "frame") for piece in pieces]

    mine = lax.dynamic_slice_in_dim(conv_weight, x * (width // 2), width // 2, axis=2)
    mine = mine.reshape(3, 3, share, 4, part).transpose(3, 0, 2, 1, 4)
    mine = mine.reshape(4, 3, share, 3 * part)
    mine = jnp.broadcast_to(mine[None], (frames // 2,) + mine.shape)
    mine = mine.reshape((ranks,) + mine.shape[2:])
    mine, packed, pieces = lax.optimization_barrier((mine, packed, pieces))
    conv_in = lax.all_to_all(mine, square, 0, 0, tiled=True)
    own = packed[:, count:]
    own_other = lax.ppermute(own, "frame", [(i, i ^ 2) for i in range(frames)])
    acts, kept = call(
        functools.partial(act_kernel, cols=cols, part=part),
        20,
        [((4, tiles * tokens + 2 * cols, width), BF), ((4, tiles * tokens, part), BF)],
        [],
        place,
        norm_gain[None],
        *pieces,
    )
    conv_in, acts, kept = lax.optimization_barrier((conv_in, acts, kept))
    conv_full = conv_in.transpose(1, 0, 2, 3).reshape(3, width, 3 * part)
    (own,) = call(merge_kernel, 8, [((frames, share, width), BF)], [], place, own, own_other)
    by_tile = swap(own, "tile")
    by_clip = swap(own, "dp")
    blocked = (2 * ranks, 2 * third, 3 * part)
    plain = (2, 2, tiles * tokens, part)
    (mid,) = call(
        functools.partial(conv_kernel, cols=cols, part=part, blocks=frames, count=count),
        16,
        [(plain if frames > 8 else blocked, BF)],
        [],
        place,
        conv_full,
        acts,
        kept,
    )
    if frames > 8:
        mid = mid.reshape(2, 2, tiles, frames, 3, third, part).transpose(0, 3, 2, 1, 5, 4, 6)
        mid = mid.reshape(blocked)
    mid, by_tile, by_clip = lax.optimization_barrier((mid, by_tile, by_clip))
    groups = None
    if clips > 2:
        groups = [[2 * ranks * g + i for i in range(2 * ranks)] for g in range(clips // 2)]
    mid = lax.all_to_all(mid, ("dp",) + square, 0, 0, axis_index_groups=groups, tiled=True)

    middle = frames // 2
    parts = [own, by_tile, by_clip, swap(by_clip[:middle], "tile"), swap(by_tile[middle:], "dp")]
    parts += [swap(piece, "frame") for piece in parts]
    parts, mid = lax.optimization_barrier((parts, mid))
    (attn_full,) = call(
        join_kernel, 16, [((4, frames, tiles, share, width), BF)], [], place, *parts
    )
    attn_full = attn_full.reshape(4, width, width)

    lanes = frames * SLOT
    padded = round_up(count + 3, 8)
    total = frames * padded
    scale = jnp.tile(jnp.pad(logit_scale, (0, SLOT - heads)), frames)[None]
    qgain = jnp.tile(query_gain, heads)[None]
    kgain = jnp.tile(key_gain, heads)[None]
    full = (total, width)
    double = (2 * total, width)
    narrow = (total, lanes)
    kept, sent, scale_sums, d_raw, q_hat, k_hat, q_rstd, k_rstd, d_value = call(
        functools.partial(attend_kernel, heads=heads, count=count, padded=padded, part=part),
        20,
        [
            ((2, 2, frames // 2, share, width), BF),
            ((2, 2, frames // 2, share, width), BF),
            ((1, lanes), F32), (narrow, F32),
            (full, F32), (full, F32), (narrow, F32), (narrow, F32), (full, BF),
        ],
        [
            (full, F32), (full, F32), (double, F32), (double, F32), (full, F32),
            (narrow, F32), (narrow, F32),
        ],
        place, mid, packed, attn_full, qgain, kgain, scale,
    )
    d_qn, d_kn = call(
        functools.partial(slope_kernel, heads=heads, padded=padded),
        16,
        [(full, F32), (full, F32)],
        [(double, F32), (double, F32)],
        d_raw, q_hat, k_hat, qgain, kgain,
    )

    def add(mine, theirs):
        return (mine.astype(F32) + theirs.astype(F32)).astype(BF)

    shares = add(kept, swap(sent, "frame"))
    shares, d_qn = lax.optimization_barrier((shares, d_qn))
    (d_mid,) = call(
        functools.partial(back_kernel, heads=heads, count=count, padded=padded),
        16,
        [((frames, padded, width), BF)],
        [],
        d_qn, d_kn, q_hat, k_hat, q_rstd, k_rstd, d_value, attn_full, qgain, kgain, scale_sums,
    )
    d_back = lax.all_to_all(d_mid, "frame", 0, 0, tiled=True)
    theirs, _ = lax.optimization_barrier((swap(shares[1], "dp"), d_mid))
    shares = add(shares[0], theirs)
    shares = add(shares[0], swap(shares[1], "tile"))
    shares, d_back = lax.optimization_barrier((shares, d_back))
    step = frames // 4
    while step > 1:
        pairs = [(i, i ^ (2 * step)) for i in range(frames)]
        shares = add(shares[:step], lax.ppermute(shares[step:], "frame", pairs))
        step //= 2
    by_plane = lax.ppermute(shares[1], "frame", [(i, i ^ 2) for i in range(frames)])
    by_clip = swap(shares[0], "dp")
    by_both = swap_both(shares[1], "frame", 2)
    shares = shares[0].astype(F32) + by_plane.astype(F32)
    theirs = by_clip.astype(F32) + by_both.astype(F32)
    small = jnp.sum(d_back[:, count : count + 3].astype(F32), axis=(0, 1))
    d_back = d_back[:, :count].reshape(rows, cols, width)
    mid_grad = (cot.astype(F32) + d_back.astype(F32)).astype(BF)

    by_tile = swap(small, "tile")
    small = (small + by_tile) + (swap(small, "dp") + swap_both(small, "tile", 1))
    if clips > 2:
        same_clip = [[i for i in range(clips) if i % 2 == c] for c in (0, 1)]
        small, shares, theirs = lax.psum(
            (small, shares, theirs), "dp", axis_index_groups=same_clip
        )
    factor = 1.0 / math.sqrt(clips * frames * tiles * tokens)
    value_grad = jnp.where(x == 0, shares, theirs) * factor
    out_proj_grad = jnp.where(x == 0, theirs, shares) * factor
    scale_sum = small[256 : 256 + heads]
    return (
        mid_grad[None, None],
        value_grad,
        out_proj_grad,
        small[:depth] * factor,
        small[128 : 128 + depth] * factor,
        scale_sum * factor,
    )


def solution(mesh):
    in_specs = (
        P("dp", "frame", "tile", None, None),
        P("dp", "frame", "tile", None, None),
        P(),
        P(None, ("frame", "tile"), None),
        P(("frame", "tile"), None),
        P(),
        P(),
        P(),
    )
    out_specs = (
        P("dp", "frame", "tile", None, None),
        P(("frame", "tile"), None),
        P(("frame", "tile"), None),
        P(),
        P(),
        P(),
    )
    return jax.shard_map(local, mesh=mesh, in_specs=in_specs, out_specs=out_specs, check_vma=False)
```

```python
import functools
import math

import jax
import jax.numpy as jnp
from jax import lax
from jax.experimental import pallas as pl
from jax.experimental.pallas import tpu as pltpu
from jax.sharding import PartitionSpec as P

GROUPS = 32
EPS = 1e-05
SLOT = 16
BF = jnp.bfloat16
F32 = jnp.float32


def swap(x, axis):
    return lax.ppermute(x, axis, [(i, i ^ 1) for i in range(lax.axis_size(axis))])


def swap_both(x, axis, bit):
    sizes = (lax.axis_size("dp"), lax.axis_size(axis))
    pairs = [
        (i * sizes[1] + j, (i ^ 1) * sizes[1] + (j ^ bit))
        for i in range(sizes[0])
        for j in range(sizes[1])
    ]
    return lax.ppermute(x, ("dp", axis), pairs)


def round_up(value, unit):
    return -(-value // unit) * unit


def dot(a, b):
    return lax.dot_general(a, b, (((1,), (0,)), ((), ())), preferred_element_type=F32)


def dot_t(a, b):
    return lax.dot_general(a, b, (((1,), (1,)), ((), ())), preferred_element_type=F32)


def dot_rows(a, b):
    return lax.dot_general(a, b, (((0,), (0,)), ((), ())), preferred_element_type=F32)


def halves(x):
    high = x.astype(BF)
    return high, (x - high.astype(F32)).astype(BF)


def picker(rows, cols, depth, offset):
    row = lax.broadcasted_iota(jnp.int32, (rows, cols), 0)
    col = lax.broadcasted_iota(jnp.int32, (rows, cols), 1)
    return (col - row // depth == offset).astype(F32).astype(BF)


def spreader(rows, cols, depth, offset):
    row = lax.broadcasted_iota(jnp.int32, (rows, cols), 0)
    col = lax.broadcasted_iota(jnp.int32, (rows, cols), 1)
    return (row - col // depth == offset).astype(F32).astype(BF)


def head_sums(x, pick):
    high, low = halves(x)
    return dot(high, pick) + dot(low, pick)


def spread(x, both):
    high, low = halves(x)
    return dot(jnp.concatenate([high, low], axis=1), both)


def over_slots(x):
    step = SLOT
    while step < x.shape[1]:
        x = x + pltpu.roll(x, step, 1)
        step *= 2
    return x


def each(number, body):
    if number > 8:
        lax.fori_loop(0, number, lambda i, _: body(i), None)
    else:
        for i in range(number):
            body(i)


def pack_kernel(place, weights, cot, out):
    share, width = (weights.shape[0], cot.shape[1])
    frames = out.shape[0]
    count = cot.shape[0] // frames
    half = share // 2
    x = place[0]
    chosen = [
        jnp.where(x == 0, weights[:, pl.ds(c * width, width)], weights[:, pl.ds((2 + c) * width, width)])
        for c in (0, 1)
    ]
    for f in range(frames):
        start = (f // 2 % 2) * half
        rows = [cot[pl.ds(f * count, count), :], chosen[f % 2][start : start + half]]
        out[f] = jnp.concatenate(rows, axis=0)


def merge_kernel(place, mine, theirs, out):
    odd = place[4] % 2
    half = mine.shape[1]
    for owner in range(mine.shape[0]):
        first = jnp.where(odd == 0, mine[owner], theirs[owner])
        second = jnp.where(odd == 0, theirs[owner], mine[owner])
        out[owner] = jnp.concatenate([first, second], axis=0)


def taps_kernel(place, mine, theirs, out):
    odd = place[4] % 2
    share = out.shape[2]
    for owner in range(mine.shape[0]):
        first = jnp.where(odd == 0, mine[owner], theirs[owner])
        second = jnp.where(odd == 0, theirs[owner], mine[owner])
        block = jnp.concatenate([first, second], axis=0)
        for row in range(3):
            out[row, owner] = block[row * share : (row + 1) * share]


def join_kernel(place, *refs):
    pieces, out = (refs[:-1], refs[-1])
    x, core, tile = (place[0], place[1], place[2])
    frames = out.shape[1]
    for dc in (0, 1):
        own, by_tile, by_clip, low, high = pieces[5 * dc : 5 * dc + 5]
        own_kind = 2 * x + (core ^ dc)
        other_kind = 2 * (x ^ 1) + (core ^ dc)
        for f in range(frames):
            out[own_kind, f, tile] = own[f]
            out[own_kind, f, tile ^ 1] = by_tile[f]
            out[other_kind, f, tile] = by_clip[f]
            part, index = (low, f) if f < frames // 2 else (high, f - frames // 2)
            out[other_kind, f, tile ^ 1] = part[index]


def act_kernel(place, gain, *refs, cols, part):
    blocks, (acts, kept) = (refs[:-2], refs[-2:])
    half, width = blocks[0].shape
    tile, chosen = (place[2], place[3])
    choice = picker(width, part, 1, -part * chosen)
    per_group = width // GROUPS
    pick = picker(width, 128, per_group, 0)
    back = spreader(128, width, per_group, 0)

    def thirds(x):
        high, low = halves(x)
        return high, low, (x - high.astype(F32) - low.astype(F32)).astype(BF)

    totals, squares = ([], [])
    for frame in range(4):
        total, square = (0.0, 0.0)
        for dy in (0, 1):
            x = blocks[2 * frame + dy][...]
            start = pl.multiple_of((tile ^ dy) * half, half)
            kept[frame, pl.ds(start, half), :] = dot(x, choice).astype(BF)
            x = x.astype(F32)
            total = total + jnp.sum(x, axis=0, keepdims=True)
            square = square + jnp.sum(x * x, axis=0, keepdims=True)
        totals.append(total)
        squares.append(square)
    high, low, lowest = thirds(jnp.concatenate(totals + squares, axis=0))
    both = (dot(high, pick) + dot(low, pick) + dot(lowest, pick)) / (2 * half * per_group)
    mean = both[0:4]
    rstd = lax.rsqrt(both[4:8] - mean * mean + EPS)
    high, low, lowest = thirds(jnp.concatenate([mean, rstd], axis=0))
    both = dot(high, back) + dot(low, back) + dot(lowest, back)
    scales = both[4:8] * gain[...]
    for frame in range(4):
        acts[frame, pl.ds(0, cols), :] = jnp.zeros((cols, width), BF)
        acts[frame, pl.ds(cols + 2 * half, cols), :] = jnp.zeros((cols, width), BF)
        for dy in (0, 1):
            x = blocks[2 * frame + dy][...].astype(F32)
            zed = (x - both[frame : frame + 1]) * scales[frame : frame + 1]
            start = pl.multiple_of(cols + (tile ^ dy) * half, cols)
            acts[frame, pl.ds(start, half), :] = (zed / (1.0 + jnp.exp(-zed))).astype(BF)


def conv_kernel(place, weights, acts, kept, out, *, cols, part, blocks, count):
    x, core = (place[0], place[1])
    whole = kept.shape[1]
    half = whole // 2
    third = count // 3
    col = lax.broadcasted_iota(jnp.int32, (whole, part), 0) % cols
    for dx in (0, 1):
        mids = []
        for dc in (0, 1):
            frame = 2 * dc + dx
            taps = dot(acts[frame, pl.ds(0, whole), :], weights[0])
            taps += dot(acts[frame, pl.ds(cols, whole), :], weights[1])
            taps += dot(acts[frame, pl.ds(2 * cols, whole), :], weights[2])
            left = pltpu.roll(taps[:, :part], 1, 0)
            right = pltpu.roll(taps[:, 2 * part :], whole - 1, 0)
            pre = taps[:, part : 2 * part] + jnp.where(col > 0, left, 0.0)
            pre = pre + jnp.where(col < cols - 1, right, 0.0)
            mids.append((kept[frame].astype(F32) + pre).astype(BF))
        if blocks > 8:
            for dc in (0, 1):
                out[x ^ dx, dc] = mids[dc]
            continue
        for f in range(blocks):
            for t in (0, 1):
                start = t * half + f * count
                rows = [
                    jnp.concatenate(
                        [mid[start + third * j : start + third * (j + 1)] for j in range(3)], axis=1
                    )
                    for mid in mids
                ]
                index = ((x ^ dx) * blocks + f) * 2 + t
                out[index] = jnp.concatenate(rows, axis=0)


def attend_kernel(
    place, mid_in, cot_in, weights, qgain, kgain, scale,
    kept, sent, sums, d_raw, q_hat, k_hat, q_rstd, k_rstd, d_value,
    mid_s, cot_s, doubled, doubled_v, mixed_s, raw_s, probs_s,
    *, heads, count, padded, part,
):
    total, width = mid_s.shape
    frames = total // padded
    depth = width // heads
    lanes = scale.shape[-1]
    third = count // 3
    x, core, tile, plane = (place[0], place[1], place[2], place[4])
    mid_s[...] = jnp.zeros_like(mid_s)
    cot_s[...] = jnp.zeros_like(cot_s)
    for z in range(frames // 2):
        for e in (0, 1):
            f = 2 * z + e
            blocks = [
                mid_in[(x * frames + 2 * z + c) * 2 + t, pl.ds((e ^ c) * third, third), :]
                for x in (0, 1)
                for c in (0, 1)
                for t in (0, 1)
            ]
            for j in range(3):
                piece = [b[:, j * part : (j + 1) * part] for b in blocks]
                start = f * padded + j * third
                mid_s[pl.ds(start, third), :] = jnp.concatenate(piece, axis=1).astype(F32)
            cot_s[pl.ds(f * padded, count), :] = cot_in[f, pl.ds(0, count), :].astype(F32)
    mid = mid_s[...].astype(BF)
    cot = cot_s[...].astype(BF)
    pick = picker(width, lanes, depth, 0)
    both = jnp.concatenate([spreader(lanes, width, depth, 0)] * 2, axis=0)

    def stats(vec):
        cent = vec - spread(head_sums(vec, pick) / depth, both)
        var = head_sums(cent * cent, pick) / depth
        rstd = lax.rsqrt(var + EPS)
        return cent * spread(rstd, both), rstd

    hat, rstd = stats(dot(mid, weights[0]))
    q_hat[...] = hat
    q_rstd[...] = rstd
    q_norm = hat * qgain[...]
    hat, rstd = stats(dot(mid, weights[1]))
    k_hat[...] = hat
    k_rstd[...] = rstd
    hat = hat * kgain[...]
    doubled[pl.ds(0, total), :] = hat
    doubled[pl.ds(total, total), :] = hat
    value = dot(mid, weights[2]).astype(BF).astype(F32)
    doubled_v[pl.ds(0, total), :] = value
    doubled_v[pl.ds(total, total), :] = value
    d_mixed = dot_t(cot, weights[3]).astype(BF).astype(F32)
    raw_s[...] = jnp.zeros_like(raw_s)
    probs_s[...] = jnp.zeros_like(probs_s)

    def logits(s):
        here = picker(width, lanes, depth, SLOT * s)
        raw_s[...] += head_sums(q_norm * doubled[pl.ds(s * padded, total), :], here)
        probs_s[...] += head_sums(d_mixed * doubled_v[pl.ds(s * padded, total), :], here)

    each(frames, logits)
    raw = raw_s[...] / math.sqrt(depth)
    expo = jnp.exp(raw * scale[...])
    probs = expo / over_slots(expo)
    probs_b = probs.astype(BF)
    d_probs = probs_s[...]
    d_logits = probs * (d_probs - over_slots(probs * d_probs))
    sums[...] = jnp.sum(d_logits * raw, axis=0, keepdims=True)
    d_raw[...] = d_logits * scale[...] / math.sqrt(depth)
    mixed_s[...] = jnp.zeros_like(mixed_s)
    doubled[...] = jnp.zeros_like(doubled)

    def mix(s):
        weight = dot(probs_b, spreader(lanes, width, depth, SLOT * s))
        mixed_s[...] += weight * doubled_v[pl.ds(s * padded, total), :]
        doubled[pl.ds(s * padded, total), :] += weight * d_mixed

    each(frames, mix)
    dv = (doubled[pl.ds(0, total), :] + doubled[pl.ds(total, total), :]).astype(BF)
    d_value[...] = dv
    rows = kept.shape[3]

    def store(kind, term):
        for z in range(frames // 2):
            for t in (0, 1):
                start = (4 * z + t) * rows
                first = term[start : start + rows]
                second = term[start + 2 * rows : start + 3 * rows]
                kept[x ^ kind, tile ^ t, plane ^ z] = jnp.where(core == 0, first, second)
                sent[x ^ kind, tile ^ t, plane ^ z] = jnp.where(core == 0, second, first)

    store(1, dot_rows(mixed_s[...].astype(BF), cot).astype(BF))
    store(0, dot_rows(mid, dv).astype(BF))


def slope_kernel(
    d_raw, q_hat, k_hat, qgain, kgain,
    d_qn, d_kn,
    doubled, doubled_acc,
    *, heads, padded,
):
    total, width = q_hat.shape
    depth = width // heads
    frames = total // padded
    lanes = d_raw.shape[-1]
    k_norm = k_hat[...] * kgain[...]
    doubled[pl.ds(0, total), :] = k_norm
    doubled[pl.ds(total, total), :] = k_norm
    q_norm = q_hat[...] * qgain[...]
    doubled_acc[...] = jnp.zeros_like(doubled_acc)
    d_qn[...] = jnp.zeros_like(d_qn)
    high, low = halves(d_raw[...])
    pair = jnp.concatenate([high, low], axis=1)

    def shift(s):
        one = spreader(lanes, width, depth, SLOT * s)
        weight = dot(pair, jnp.concatenate([one, one], axis=0))
        d_qn[...] += weight * doubled[pl.ds(s * padded, total), :]
        doubled_acc[pl.ds(s * padded, total), :] += weight * q_norm

    each(frames, shift)
    d_kn[...] = doubled_acc[pl.ds(0, total), :] + doubled_acc[pl.ds(total, total), :]


def back_kernel(
    d_qn, d_kn, q_hat, k_hat, q_rstd, k_rstd, d_value, weights, qgain, kgain, scale_sums,
    d_mid,
    *, heads, count, padded,
):
    total, width = q_hat.shape
    depth = width // heads
    frames = total // padded
    lanes = scale_sums.shape[-1]
    pick = picker(width, lanes, depth, 0)
    both = jnp.concatenate([spreader(lanes, width, depth, 0)] * 2, axis=0)

    def back(dhat, hat, rstd):
        first = spread(head_sums(dhat, pick) / depth, both)
        second = spread(head_sums(dhat * hat, pick) / depth, both)
        return (spread(rstd, both) * (dhat - first - hat * second)).astype(BF)

    d_query = back(d_qn[...] * qgain[...], q_hat[...], q_rstd[...])
    d_key = back(d_kn[...] * kgain[...], k_hat[...], k_rstd[...])
    out = dot_t(d_query, weights[0])
    out += dot_t(d_key, weights[1])
    out += dot_t(d_value[...], weights[2])

    row = lax.broadcasted_iota(jnp.int32, (width, 128), 0)
    col = lax.broadcasted_iota(jnp.int32, (width, 128), 1)
    fold = (row % depth == col).astype(F32)

    def folded(d_norm, hat):
        sums = jnp.sum(d_norm * hat, axis=0, keepdims=True)
        sums = jnp.broadcast_to(sums, (8, width))
        return jnp.dot(sums, fold, precision=lax.Precision.HIGHEST, preferred_element_type=F32)[0:1]

    by_head = over_slots(jnp.broadcast_to(scale_sums[...], (8, lanes)))[0:1, :128]
    small = [folded(d_qn[...], q_hat[...]), folded(d_kn[...], k_hat[...]), by_head]
    small.append(jnp.zeros((1, width - 384), F32))
    small = jnp.concatenate(small, axis=1)
    high, low = halves(small)
    lowest = (small - high.astype(F32) - low.astype(F32)).astype(BF)
    spare = [high.astype(F32), low.astype(F32), lowest.astype(F32)]
    if padded - count > 3:
        spare.append(jnp.zeros((padded - count - 3, width), F32))
    spare = jnp.concatenate(spare, axis=0)
    for f in range(frames):
        tokens = out[f * padded : f * padded + count]
        d_mid[f] = jnp.concatenate([tokens, spare], axis=0).astype(BF)


def call(kernel, mebibytes, outs, scratch, *args):
    smem = pl.BlockSpec(memory_space=pltpu.SMEM)
    vmem = pl.BlockSpec(memory_space=pltpu.VMEM)
    return pl.pallas_call(
        kernel,
        out_shape=[jax.ShapeDtypeStruct(shape, dtype) for shape, dtype in outs],
        in_specs=[smem if arg.dtype == jnp.int32 else vmem for arg in args],
        out_specs=[vmem] * len(outs),
        scratch_shapes=[pltpu.VMEM(shape, dtype) for shape, dtype in scratch],
        compiler_params=pltpu.CompilerParams(vmem_limit_bytes=mebibytes << 20),
    )(*args)


def local(
    clip_input, cotangent, norm_gain, conv_weight, attn_weight, query_gain, key_gain, logit_scale
):
    source = clip_input[0, 0]
    cot = cotangent[0, 0]
    rows, cols, width = source.shape
    heads = logit_scale.shape[0]
    depth = width // heads
    tokens = rows * cols
    clips, frames, tiles = (lax.axis_size(name) for name in ("dp", "frame", "tile"))
    square = ("frame", "tile")
    ranks = frames * tiles
    share = conv_weight.shape[1]
    count = tokens // frames
    third = count // 3
    part = width // 8
    x = lax.axis_index("dp") % 2
    core = lax.axis_index("frame") % 2
    tile = lax.axis_index("tile")
    plane = lax.axis_index("frame") // 2
    place = jnp.stack([x, core, tile, 4 * x + 2 * core + tile, plane]).astype(jnp.int32)
    flat = source.reshape(tokens, width)

    (packed,) = call(
        pack_kernel,
        12,
        [((frames, count + share // 2, width), BF)],
        [],
        place,
        attn_weight,
        cot.reshape(tokens, width),
    )
    packed = lax.all_to_all(packed, "frame", 0, 0, tiled=True)

    half = tokens // 2
    along_x = swap(flat, "dp")
    along_y = swap(flat, "tile")
    across = jnp.concatenate([swap(along_x[:half], "tile"), swap(along_y[half:], "dp")])
    pieces = [flat, along_y, along_x, across]
    pieces += [swap(piece, "frame") for piece in pieces]

    planes = [(i, i ^ 2) for i in range(frames)]
    lines = 3 * share // 2
    mine = lax.dynamic_slice_in_dim(conv_weight, x * (width // 2), width // 2, axis=2)
    mine = mine.reshape(3, 3, share, 4, part).transpose(3, 0, 2, 1, 4)
    mine = mine.reshape(4, 2, lines, 3 * part).transpose(1, 0, 2, 3)
    mine = jnp.broadcast_to(mine[None], (frames // 4,) + mine.shape)
    mine = mine.reshape(ranks, lines, 3 * part)
    mine, packed, pieces = lax.optimization_barrier((mine, packed, pieces))
    conv_half = lax.all_to_all(mine, square, 0, 0, tiled=True)
    own = packed[:, count:]
    own_other = lax.ppermute(own, "frame", planes)
    conv_other = lax.ppermute(conv_half, "frame", planes)
    acts, kept = call(
        functools.partial(act_kernel, cols=cols, part=part),
        20,
        [((4, tiles * tokens + 2 * cols, width), BF), ((4, tiles * tokens, part), BF)],
        [],
        place,
        norm_gain[None],
        *pieces,
    )
    (conv_full,) = call(
        taps_kernel, 12, [((3, ranks, share, 3 * part), BF)], [], place, conv_half, conv_other
    )
    conv_full = conv_full.reshape(3, width, 3 * part)
    (own,) = call(merge_kernel, 8, [((frames, share, width), BF)], [], place, own, own_other)
    by_tile = swap(own, "tile")
    by_clip = swap(own, "dp")
    blocked = (2 * ranks, 2 * third, 3 * part)
    plain = (2, 2, tiles * tokens, part)
    (mid,) = call(
        functools.partial(conv_kernel, cols=cols, part=part, blocks=frames, count=count),
        16,
        [(plain if frames > 8 else blocked, BF)],
        [],
        place,
        conv_full,
        acts,
        kept,
    )
    if frames > 8:
        mid = mid.reshape(2, 2, tiles, frames, 3, third, part).transpose(0, 3, 2, 1, 5, 4, 6)
        mid = mid.reshape(blocked)
    mid, by_tile, by_clip = lax.optimization_barrier((mid, by_tile, by_clip))
    groups = None
    if clips > 2:
        groups = [[2 * ranks * g + i for i in range(2 * ranks)] for g in range(clips // 2)]
    mid = lax.all_to_all(mid, ("dp",) + square, 0, 0, axis_index_groups=groups, tiled=True)

    middle = frames // 2
    parts = [own, by_tile, by_clip, swap(by_clip[:middle], "tile"), swap(by_tile[middle:], "dp")]
    parts += [swap(piece, "frame") for piece in parts]
    parts, mid = lax.optimization_barrier((parts, mid))
    (attn_full,) = call(
        join_kernel, 16, [((4, frames, tiles, share, width), BF)], [], place, *parts
    )
    attn_full = attn_full.reshape(4, width, width)

    lanes = frames * SLOT
    padded = round_up(count + 3, 8)
    total = frames * padded
    scale = jnp.tile(jnp.pad(logit_scale, (0, SLOT - heads)), frames)[None]
    qgain = jnp.tile(query_gain, heads)[None]
    kgain = jnp.tile(key_gain, heads)[None]
    full = (total, width)
    double = (2 * total, width)
    narrow = (total, lanes)
    kept, sent, scale_sums, d_raw, q_hat, k_hat, q_rstd, k_rstd, d_value = call(
        functools.partial(attend_kernel, heads=heads, count=count, padded=padded, part=part),
        20,
        [
            ((2, 2, frames // 2, share, width), BF),
            ((2, 2, frames // 2, share, width), BF),
            ((1, lanes), F32), (narrow, F32),
            (full, F32), (full, F32), (narrow, F32), (narrow, F32), (full, BF),
        ],
        [
            (full, F32), (full, F32), (double, F32), (double, F32), (full, F32),
            (narrow, F32), (narrow, F32),
        ],
        place, mid, packed, attn_full, qgain, kgain, scale,
    )
    d_qn, d_kn = call(
        functools.partial(slope_kernel, heads=heads, padded=padded),
        16,
        [(full, F32), (full, F32)],
        [(double, F32), (double, F32)],
        d_raw, q_hat, k_hat, qgain, kgain,
    )

    def add(mine, theirs):
        return (mine.astype(F32) + theirs.astype(F32)).astype(BF)

    shares = add(kept, swap(sent, "frame"))
    shares, d_qn = lax.optimization_barrier((shares, d_qn))
    (d_mid,) = call(
        functools.partial(back_kernel, heads=heads, count=count, padded=padded),
        16,
        [((frames, padded, width), BF)],
        [],
        d_qn, d_kn, q_hat, k_hat, q_rstd, k_rstd, d_value, attn_full, qgain, kgain, scale_sums,
    )
    d_back = lax.all_to_all(d_mid, "frame", 0, 0, tiled=True)
    theirs, _ = lax.optimization_barrier((swap(shares[1], "dp"), d_mid))
    shares = add(shares[0], theirs)
    shares = add(shares[0], swap(shares[1], "tile"))
    step = frames // 4
    while step > 1:
        pairs = [(i, i ^ (2 * step)) for i in range(frames)]
        shares = add(shares[:step], lax.ppermute(shares[step:], "frame", pairs))
        step //= 2
    by_plane = lax.ppermute(shares[1], "frame", planes)
    by_clip = swap(shares[0], "dp")
    by_both = swap_both(shares[1], "frame", 2)
    shares = shares[0].astype(F32) + by_plane.astype(F32)
    theirs = by_clip.astype(F32) + by_both.astype(F32)
    small = jnp.sum(d_back[:, count : count + 3].astype(F32), axis=(0, 1))
    d_back = d_back[:, :count].reshape(rows, cols, width)
    mid_grad = (cot.astype(F32) + d_back.astype(F32)).astype(BF)

    small = small + swap(small, "tile")
    small = small + swap(small, "dp")
    if clips > 2:
        same_clip = [[i for i in range(clips) if i % 2 == c] for c in (0, 1)]
        small, shares, theirs = lax.psum(
            (small, shares, theirs), "dp", axis_index_groups=same_clip
        )
    factor = 1.0 / math.sqrt(clips * frames * tiles * tokens)
    value_grad = jnp.where(x == 0, shares, theirs) * factor
    out_proj_grad = jnp.where(x == 0, theirs, shares) * factor
    scale_sum = small[256 : 256 + heads]
    return (
        mid_grad[None, None],
        value_grad,
        out_proj_grad,
        small[:depth] * factor,
        small[128 : 128 + depth] * factor,
        scale_sum * factor,
    )


def solution(mesh):
    in_specs = (
        P("dp", "frame", "tile", None, None),
        P("dp", "frame", "tile", None, None),
        P(),
        P(None, ("frame", "tile"), None),
        P(("frame", "tile"), None),
        P(),
        P(),
        P(),
    )
    out_specs = (
        P("dp", "frame", "tile", None, None),
        P(("frame", "tile"), None),
        P(("frame", "tile"), None),
        P(),
        P(),
        P(),
    )
    return jax.shard_map(local, mesh=mesh, in_specs=in_specs, out_specs=out_specs, check_vma=False)
```

```python
import functools
import math

import jax
import jax.numpy as jnp
from jax import lax
from jax.experimental import pallas as pl
from jax.experimental.pallas import tpu as pltpu
from jax.sharding import PartitionSpec as P

GROUPS = 32
EPS = 1e-05
SLOT = 16
BF = jnp.bfloat16
F32 = jnp.float32


def swap(x, axis):
    return lax.ppermute(x, axis, [(i, i ^ 1) for i in range(lax.axis_size(axis))])


def swap_both(x, axis, bit):
    sizes = (lax.axis_size("dp"), lax.axis_size(axis))
    pairs = [
        (i * sizes[1] + j, (i ^ 1) * sizes[1] + (j ^ bit))
        for i in range(sizes[0])
        for j in range(sizes[1])
    ]
    return lax.ppermute(x, ("dp", axis), pairs)


def round_up(value, unit):
    return -(-value // unit) * unit


def dot(a, b):
    return lax.dot_general(a, b, (((1,), (0,)), ((), ())), preferred_element_type=F32)


def dot_t(a, b):
    return lax.dot_general(a, b, (((1,), (1,)), ((), ())), preferred_element_type=F32)


def dot_rows(a, b):
    return lax.dot_general(a, b, (((0,), (0,)), ((), ())), preferred_element_type=F32)


def halves(x):
    high = x.astype(BF)
    return high, (x - high.astype(F32)).astype(BF)


def picker(rows, cols, depth, offset):
    row = lax.broadcasted_iota(jnp.int32, (rows, cols), 0)
    col = lax.broadcasted_iota(jnp.int32, (rows, cols), 1)
    return (col - row // depth == offset).astype(F32).astype(BF)


def spreader(rows, cols, depth, offset):
    row = lax.broadcasted_iota(jnp.int32, (rows, cols), 0)
    col = lax.broadcasted_iota(jnp.int32, (rows, cols), 1)
    return (row - col // depth == offset).astype(F32).astype(BF)


def head_sums(x, pick):
    high, low = halves(x)
    return dot(high, pick) + dot(low, pick)


def spread(x, both):
    high, low = halves(x)
    return dot(jnp.concatenate([high, low], axis=1), both)


def over_slots(x):
    step = SLOT
    while step < x.shape[1]:
        x = x + pltpu.roll(x, step, 1)
        step *= 2
    return x


def each(number, body):
    if number > 8:
        lax.fori_loop(0, number, lambda i, _: body(i), None)
    else:
        for i in range(number):
            body(i)


def pack_kernel(place, weights, cot, out):
    share, width = (weights.shape[0], cot.shape[1])
    frames = out.shape[0]
    count = cot.shape[0] // frames
    half = share // 2
    x = place[0]
    chosen = [
        jnp.where(x == 0, weights[:, pl.ds(c * width, width)], weights[:, pl.ds((2 + c) * width, width)])
        for c in (0, 1)
    ]
    for f in range(frames):
        start = (f // 2 % 2) * half
        rows = [cot[pl.ds(f * count, count), :], chosen[f % 2][start : start + half]]
        out[f] = jnp.concatenate(rows, axis=0)


def merge_kernel(place, mine, theirs, out):
    odd = place[4] % 2
    half = mine.shape[1]
    for owner in range(mine.shape[0]):
        first = jnp.where(odd == 0, mine[owner], theirs[owner])
        second = jnp.where(odd == 0, theirs[owner], mine[owner])
        out[owner] = jnp.concatenate([first, second], axis=0)


def taps_kernel(place, mine, theirs, out):
    odd = place[4] % 2
    share = out.shape[2]
    for owner in range(mine.shape[0]):
        first = jnp.where(odd == 0, mine[owner], theirs[owner])
        second = jnp.where(odd == 0, theirs[owner], mine[owner])
        block = jnp.concatenate([first, second], axis=0)
        for row in range(3):
            out[row, owner] = block[row * share : (row + 1) * share]


def join_kernel(place, *refs):
    pieces, out = (refs[:-1], refs[-1])
    x, core, tile = (place[0], place[1], place[2])
    frames = out.shape[1]
    for dc in (0, 1):
        own, by_tile, by_clip, low, high = pieces[5 * dc : 5 * dc + 5]
        own_kind = 2 * x + (core ^ dc)
        other_kind = 2 * (x ^ 1) + (core ^ dc)
        for f in range(frames):
            out[own_kind, f, tile] = own[f]
            out[own_kind, f, tile ^ 1] = by_tile[f]
            out[other_kind, f, tile] = by_clip[f]
            part, index = (low, f) if f < frames // 2 else (high, f - frames // 2)
            out[other_kind, f, tile ^ 1] = part[index]


def act_kernel(place, gain, *refs, cols, part):
    blocks, (acts, kept) = (refs[:-2], refs[-2:])
    half, width = blocks[0].shape
    tile, chosen = (place[2], place[3])
    choice = picker(width, part, 1, -part * chosen)
    per_group = width // GROUPS
    pick = picker(width, 128, per_group, 0)
    back = spreader(128, width, per_group, 0)

    def thirds(x):
        high, low = halves(x)
        return high, low, (x - high.astype(F32) - low.astype(F32)).astype(BF)

    totals, squares = ([], [])
    for frame in range(4):
        total, square = (0.0, 0.0)
        for dy in (0, 1):
            x = blocks[2 * frame + dy][...]
            start = pl.multiple_of((tile ^ dy) * half, half)
            kept[frame, pl.ds(start, half), :] = dot(x, choice).astype(BF)
            x = x.astype(F32)
            total = total + jnp.sum(x, axis=0, keepdims=True)
            square = square + jnp.sum(x * x, axis=0, keepdims=True)
        totals.append(total)
        squares.append(square)
    high, low, lowest = thirds(jnp.concatenate(totals + squares, axis=0))
    both = (dot(high, pick) + dot(low, pick) + dot(lowest, pick)) / (2 * half * per_group)
    mean = both[0:4]
    rstd = lax.rsqrt(both[4:8] - mean * mean + EPS)
    high, low, lowest = thirds(jnp.concatenate([mean, rstd], axis=0))
    both = dot(high, back) + dot(low, back) + dot(lowest, back)
    scales = both[4:8] * gain[...]
    for frame in range(4):
        acts[frame, pl.ds(0, cols), :] = jnp.zeros((cols, width), BF)
        acts[frame, pl.ds(cols + 2 * half, cols), :] = jnp.zeros((cols, width), BF)
        for dy in (0, 1):
            x = blocks[2 * frame + dy][...].astype(F32)
            zed = (x - both[frame : frame + 1]) * scales[frame : frame + 1]
            start = pl.multiple_of(cols + (tile ^ dy) * half, cols)
            acts[frame, pl.ds(start, half), :] = (zed / (1.0 + jnp.exp(-zed))).astype(BF)


def conv_kernel(place, weights, acts, kept, out, *, cols, part, blocks, count):
    x, core = (place[0], place[1])
    whole = kept.shape[1]
    half = whole // 2
    third = count // 3
    col = lax.broadcasted_iota(jnp.int32, (whole, part), 0) % cols
    for dx in (0, 1):
        mids = []
        for dc in (0, 1):
            frame = 2 * dc + dx
            taps = dot(acts[frame, pl.ds(0, whole), :], weights[0])
            taps += dot(acts[frame, pl.ds(cols, whole), :], weights[1])
            taps += dot(acts[frame, pl.ds(2 * cols, whole), :], weights[2])
            left = pltpu.roll(taps[:, :part], 1, 0)
            right = pltpu.roll(taps[:, 2 * part :], whole - 1, 0)
            pre = taps[:, part : 2 * part] + jnp.where(col > 0, left, 0.0)
            pre = pre + jnp.where(col < cols - 1, right, 0.0)
            mids.append((kept[frame].astype(F32) + pre).astype(BF))
        if blocks > 8:
            for dc in (0, 1):
                out[x ^ dx, dc] = mids[dc]
            continue
        for f in range(blocks):
            for t in (0, 1):
                start = t * half + f * count
                rows = [
                    jnp.concatenate(
                        [mid[start + third * j : start + third * (j + 1)] for j in range(3)], axis=1
                    )
                    for mid in mids
                ]
                index = ((x ^ dx) * blocks + f) * 2 + t
                out[index] = jnp.concatenate(rows, axis=0)


def attend_kernel(
    place, mid_in, cot_in, weights, qgain, kgain, scale,
    kept, sent, sums, d_raw, q_hat, k_hat, q_rstd, k_rstd, d_value,
    mid_s, cot_s, doubled, doubled_v, mixed_s, raw_s, probs_s,
    *, heads, count, padded, part,
):
    total, width = mid_s.shape
    frames = total // padded
    depth = width // heads
    lanes = scale.shape[-1]
    third = count // 3
    x, core, tile, plane = (place[0], place[1], place[2], place[4])
    mid_s[...] = jnp.zeros_like(mid_s)
    cot_s[...] = jnp.zeros_like(cot_s)
    for z in range(frames // 2):
        for e in (0, 1):
            f = 2 * z + e
            blocks = [
                mid_in[(x * frames + 2 * z + c) * 2 + t, pl.ds((e ^ c) * third, third), :]
                for x in (0, 1)
                for c in (0, 1)
                for t in (0, 1)
            ]
            for j in range(3):
                piece = [b[:, j * part : (j + 1) * part] for b in blocks]
                start = f * padded + j * third
                mid_s[pl.ds(start, third), :] = jnp.concatenate(piece, axis=1).astype(F32)
            cot_s[pl.ds(f * padded, count), :] = cot_in[f, pl.ds(0, count), :].astype(F32)
    mid = mid_s[...].astype(BF)
    cot = cot_s[...].astype(BF)
    pick = picker(width, lanes, depth, 0)
    both = jnp.concatenate([spreader(lanes, width, depth, 0)] * 2, axis=0)

    def stats(vec):
        cent = vec - spread(head_sums(vec, pick) / depth, both)
        var = head_sums(cent * cent, pick) / depth
        rstd = lax.rsqrt(var + EPS)
        return cent * spread(rstd, both), rstd

    hat, rstd = stats(dot(mid, weights[0]))
    q_hat[...] = hat
    q_rstd[...] = rstd
    q_norm = hat * qgain[...]
    hat, rstd = stats(dot(mid, weights[1]))
    k_hat[...] = hat
    k_rstd[...] = rstd
    hat = hat * kgain[...]
    doubled[pl.ds(0, total), :] = hat
    doubled[pl.ds(total, total), :] = hat
    value = dot(mid, weights[2]).astype(BF).astype(F32)
    doubled_v[pl.ds(0, total), :] = value
    doubled_v[pl.ds(total, total), :] = value
    d_mixed = dot_t(cot, weights[3]).astype(BF).astype(F32)
    raw_s[...] = jnp.zeros_like(raw_s)
    probs_s[...] = jnp.zeros_like(probs_s)

    def logits(s):
        here = picker(width, lanes, depth, SLOT * s)
        raw_s[...] += head_sums(q_norm * doubled[pl.ds(s * padded, total), :], here)
        probs_s[...] += head_sums(d_mixed * doubled_v[pl.ds(s * padded, total), :], here)

    each(frames, logits)
    raw = raw_s[...] / math.sqrt(depth)
    expo = jnp.exp(raw * scale[...])
    probs = expo / over_slots(expo)
    probs_b = probs.astype(BF)
    d_probs = probs_s[...]
    d_logits = probs * (d_probs - over_slots(probs * d_probs))
    sums[...] = jnp.sum(d_logits * raw, axis=0, keepdims=True)
    d_raw[...] = d_logits * scale[...] / math.sqrt(depth)
    mixed_s[...] = jnp.zeros_like(mixed_s)
    doubled[...] = jnp.zeros_like(doubled)

    def mix(s):
        weight = dot(probs_b, spreader(lanes, width, depth, SLOT * s))
        mixed_s[...] += weight * doubled_v[pl.ds(s * padded, total), :]
        doubled[pl.ds(s * padded, total), :] += weight * d_mixed

    each(frames, mix)
    dv = (doubled[pl.ds(0, total), :] + doubled[pl.ds(total, total), :]).astype(BF)
    d_value[...] = dv
    rows = kept.shape[3]

    def store(kind, term):
        for z in range(frames // 2):
            for t in (0, 1):
                start = (4 * z + t) * rows
                first = term[start : start + rows]
                second = term[start + 2 * rows : start + 3 * rows]
                kept[x ^ kind, tile ^ t, plane ^ z] = jnp.where(core == 0, first, second)
                sent[x ^ kind, tile ^ t, plane ^ z] = jnp.where(core == 0, second, first)

    store(1, dot_rows(mixed_s[...].astype(BF), cot).astype(BF))
    store(0, dot_rows(mid, dv).astype(BF))


def slope_kernel(
    d_raw, q_hat, k_hat, qgain, kgain,
    d_qn, d_kn,
    doubled, doubled_acc,
    *, heads, padded,
):
    total, width = q_hat.shape
    depth = width // heads
    frames = total // padded
    lanes = d_raw.shape[-1]
    k_norm = k_hat[...] * kgain[...]
    doubled[pl.ds(0, total), :] = k_norm
    doubled[pl.ds(total, total), :] = k_norm
    q_norm = q_hat[...] * qgain[...]
    doubled_acc[...] = jnp.zeros_like(doubled_acc)
    d_qn[...] = jnp.zeros_like(d_qn)
    high, low = halves(d_raw[...])
    pair = jnp.concatenate([high, low], axis=1)

    def shift(s):
        one = spreader(lanes, width, depth, SLOT * s)
        weight = dot(pair, jnp.concatenate([one, one], axis=0))
        d_qn[...] += weight * doubled[pl.ds(s * padded, total), :]
        doubled_acc[pl.ds(s * padded, total), :] += weight * q_norm

    each(frames, shift)
    d_kn[...] = doubled_acc[pl.ds(0, total), :] + doubled_acc[pl.ds(total, total), :]


def back_kernel(
    d_qn, d_kn, q_hat, k_hat, q_rstd, k_rstd, d_value, weights, qgain, kgain, scale_sums,
    d_mid,
    *, heads, count, padded,
):
    total, width = q_hat.shape
    depth = width // heads
    frames = total // padded
    lanes = scale_sums.shape[-1]
    pick = picker(width, lanes, depth, 0)
    both = jnp.concatenate([spreader(lanes, width, depth, 0)] * 2, axis=0)

    def back(dhat, hat, rstd):
        first = spread(head_sums(dhat, pick) / depth, both)
        second = spread(head_sums(dhat * hat, pick) / depth, both)
        return (spread(rstd, both) * (dhat - first - hat * second)).astype(BF)

    d_query = back(d_qn[...] * qgain[...], q_hat[...], q_rstd[...])
    d_key = back(d_kn[...] * kgain[...], k_hat[...], k_rstd[...])
    out = dot_t(d_query, weights[0])
    out += dot_t(d_key, weights[1])
    out += dot_t(d_value[...], weights[2])

    row = lax.broadcasted_iota(jnp.int32, (width, 128), 0)
    col = lax.broadcasted_iota(jnp.int32, (width, 128), 1)
    fold = (row % depth == col).astype(F32)

    def folded(d_norm, hat):
        sums = jnp.sum(d_norm * hat, axis=0, keepdims=True)
        sums = jnp.broadcast_to(sums, (8, width))
        return jnp.dot(sums, fold, precision=lax.Precision.HIGHEST, preferred_element_type=F32)[0:1]

    by_head = over_slots(jnp.broadcast_to(scale_sums[...], (8, lanes)))[0:1, :128]
    small = [folded(d_qn[...], q_hat[...]), folded(d_kn[...], k_hat[...]), by_head]
    small.append(jnp.zeros((1, width - 384), F32))
    small = jnp.concatenate(small, axis=1)
    high, low = halves(small)
    lowest = (small - high.astype(F32) - low.astype(F32)).astype(BF)
    spare = [high.astype(F32), low.astype(F32), lowest.astype(F32)]
    if padded - count > 3:
        spare.append(jnp.zeros((padded - count - 3, width), F32))
    spare = jnp.concatenate(spare, axis=0)
    for f in range(frames):
        tokens = out[f * padded : f * padded + count]
        d_mid[f] = jnp.concatenate([tokens, spare], axis=0).astype(BF)


def call(kernel, mebibytes, outs, scratch, *args):
    smem = pl.BlockSpec(memory_space=pltpu.SMEM)
    vmem = pl.BlockSpec(memory_space=pltpu.VMEM)
    return pl.pallas_call(
        kernel,
        out_shape=[jax.ShapeDtypeStruct(shape, dtype) for shape, dtype in outs],
        in_specs=[smem if arg.dtype == jnp.int32 else vmem for arg in args],
        out_specs=[vmem] * len(outs),
        scratch_shapes=[pltpu.VMEM(shape, dtype) for shape, dtype in scratch],
        compiler_params=pltpu.CompilerParams(vmem_limit_bytes=mebibytes << 20),
    )(*args)


def local(
    clip_input, cotangent, norm_gain, conv_weight, attn_weight, query_gain, key_gain, logit_scale
):
    source = clip_input[0, 0]
    cot = cotangent[0, 0]
    rows, cols, width = source.shape
    heads = logit_scale.shape[0]
    depth = width // heads
    tokens = rows * cols
    clips, frames, tiles = (lax.axis_size(name) for name in ("dp", "frame", "tile"))
    square = ("frame", "tile")
    ranks = frames * tiles
    share = conv_weight.shape[1]
    count = tokens // frames
    third = count // 3
    part = width // 8
    x = lax.axis_index("dp") % 2
    core = lax.axis_index("frame") % 2
    tile = lax.axis_index("tile")
    plane = lax.axis_index("frame") // 2
    place = jnp.stack([x, core, tile, 4 * x + 2 * core + tile, plane]).astype(jnp.int32)
    flat = source.reshape(tokens, width)

    (packed,) = call(
        pack_kernel,
        12,
        [((frames, count + share // 2, width), BF)],
        [],
        place,
        attn_weight,
        cot.reshape(tokens, width),
    )
    packed = lax.all_to_all(packed, "frame", 0, 0, tiled=True)

    half = tokens // 2
    along_x = swap(flat, "dp")
    along_y = swap(flat, "tile")
    across = jnp.concatenate([swap(along_x[:half], "tile"), swap(along_y[half:], "dp")])
    pieces = [flat, along_y, along_x, across]
    pieces += [swap(piece, "frame") for piece in pieces]

    planes = [(i, i ^ 2) for i in range(frames)]
    lines = 3 * share // 2
    mine = lax.dynamic_slice_in_dim(conv_weight, x * (width // 2), width // 2, axis=2)
    mine = mine.reshape(3, 3, share, 4, part).transpose(3, 0, 2, 1, 4)
    mine = mine.reshape(4, 2, lines, 3 * part).transpose(1, 0, 2, 3)
    mine = jnp.broadcast_to(mine[None], (frames // 4,) + mine.shape)
    mine = mine.reshape(ranks, lines, 3 * part)
    mine, packed, pieces = lax.optimization_barrier((mine, packed, pieces))
    conv_half = lax.all_to_all(mine, square, 0, 0, tiled=True)
    own = packed[:, count:]
    own_other = lax.ppermute(own, "frame", planes)
    conv_other = lax.ppermute(conv_half, "frame", planes)
    acts, kept = call(
        functools.partial(act_kernel, cols=cols, part=part),
        20,
        [((4, tiles * tokens + 2 * cols, width), BF), ((4, tiles * tokens, part), BF)],
        [],
        place,
        norm_gain[None],
        *pieces,
    )
    (conv_full,) = call(
        taps_kernel, 12, [((3, ranks, share, 3 * part), BF)], [], place, conv_half, conv_other
    )
    conv_full = conv_full.reshape(3, width, 3 * part)
    (own,) = call(merge_kernel, 8, [((frames, share, width), BF)], [], place, own, own_other)
    by_tile = swap(own, "tile")
    by_clip = swap(own, "dp")
    blocked = (2 * ranks, 2 * third, 3 * part)
    plain = (2, 2, tiles * tokens, part)
    (mid,) = call(
        functools.partial(conv_kernel, cols=cols, part=part, blocks=frames, count=count),
        16,
        [(plain if frames > 8 else blocked, BF)],
        [],
        place,
        conv_full,
        acts,
        kept,
    )
    if frames > 8:
        mid = mid.reshape(2, 2, tiles, frames, 3, third, part).transpose(0, 3, 2, 1, 5, 4, 6)
        mid = mid.reshape(blocked)
    mid, by_tile, by_clip = lax.optimization_barrier((mid, by_tile, by_clip))
    groups = None
    if clips > 2:
        groups = [[2 * ranks * g + i for i in range(2 * ranks)] for g in range(clips // 2)]
    mid = lax.all_to_all(mid, ("dp",) + square, 0, 0, axis_index_groups=groups, tiled=True)

    middle = frames // 2
    parts = [own, by_tile, by_clip, swap(by_clip[:middle], "tile"), swap(by_tile[middle:], "dp")]
    parts += [swap(piece, "frame") for piece in parts]
    parts, mid = lax.optimization_barrier((parts, mid))
    (attn_full,) = call(
        join_kernel, 16, [((4, frames, tiles, share, width), BF)], [], place, *parts
    )
    attn_full = attn_full.reshape(4, width, width)

    lanes = frames * SLOT
    padded = round_up(count + 3, 8)
    total = frames * padded
    scale = jnp.tile(jnp.pad(logit_scale, (0, SLOT - heads)), frames)[None]
    qgain = jnp.tile(query_gain, heads)[None]
    kgain = jnp.tile(key_gain, heads)[None]
    full = (total, width)
    double = (2 * total, width)
    narrow = (total, lanes)
    kept, sent, scale_sums, d_raw, q_hat, k_hat, q_rstd, k_rstd, d_value = call(
        functools.partial(attend_kernel, heads=heads, count=count, padded=padded, part=part),
        20,
        [
            ((2, 2, frames // 2, share, width), BF),
            ((2, 2, frames // 2, share, width), BF),
            ((1, lanes), F32), (narrow, F32),
            (full, F32), (full, F32), (narrow, F32), (narrow, F32), (full, BF),
        ],
        [
            (full, F32), (full, F32), (double, F32), (double, F32), (full, F32),
            (narrow, F32), (narrow, F32),
        ],
        place, mid, packed, attn_full, qgain, kgain, scale,
    )
    d_qn, d_kn = call(
        functools.partial(slope_kernel, heads=heads, padded=padded),
        16,
        [(full, F32), (full, F32)],
        [(double, F32), (double, F32)],
        d_raw, q_hat, k_hat, qgain, kgain,
    )

    def add(mine, theirs):
        return (mine.astype(F32) + theirs.astype(F32)).astype(BF)

    shares = add(kept, swap(sent, "frame"))
    shares, d_qn = lax.optimization_barrier((shares, d_qn))
    (d_mid,) = call(
        functools.partial(back_kernel, heads=heads, count=count, padded=padded),
        16,
        [((frames, padded, width), BF)],
        [],
        d_qn, d_kn, q_hat, k_hat, q_rstd, k_rstd, d_value, attn_full, qgain, kgain, scale_sums,
    )
    d_back = lax.all_to_all(d_mid, "frame", 0, 0, tiled=True)
    theirs, _ = lax.optimization_barrier((swap(shares[1], "dp"), d_mid))
    shares = add(shares[0], theirs)
    shares = add(shares[0], swap(shares[1], "tile"))
    shares, d_back = lax.optimization_barrier((shares, d_back))
    step = frames // 4
    while step > 1:
        pairs = [(i, i ^ (2 * step)) for i in range(frames)]
        shares = add(shares[:step], lax.ppermute(shares[step:], "frame", pairs))
        step //= 2
    by_plane = lax.ppermute(shares[1], "frame", planes)
    by_clip = swap(shares[0], "dp")
    by_both = swap_both(shares[1], "frame", 2)
    shares = shares[0].astype(F32) + by_plane.astype(F32)
    theirs = by_clip.astype(F32) + by_both.astype(F32)
    small = jnp.sum(d_back[:, count : count + 3].astype(F32), axis=(0, 1))
    d_back = d_back[:, :count].reshape(rows, cols, width)
    mid_grad = (cot.astype(F32) + d_back.astype(F32)).astype(BF)

    small = small + swap(small, "tile")
    small = small + swap(small, "dp")
    if clips > 2:
        same_clip = [[i for i in range(clips) if i % 2 == c] for c in (0, 1)]
        small, shares, theirs = lax.psum(
            (small, shares, theirs), "dp", axis_index_groups=same_clip
        )
    factor = 1.0 / math.sqrt(clips * frames * tiles * tokens)
    value_grad = jnp.where(x == 0, shares, theirs) * factor
    out_proj_grad = jnp.where(x == 0, theirs, shares) * factor
    scale_sum = small[256 : 256 + heads]
    return (
        mid_grad[None, None],
        value_grad,
        out_proj_grad,
        small[:depth] * factor,
        small[128 : 128 + depth] * factor,
        scale_sum * factor,
    )


def solution(mesh):
    in_specs = (
        P("dp", "frame", "tile", None, None),
        P("dp", "frame", "tile", None, None),
        P(),
        P(None, ("frame", "tile"), None),
        P(("frame", "tile"), None),
        P(),
        P(),
        P(),
    )
    out_specs = (
        P("dp", "frame", "tile", None, None),
        P(("frame", "tile"), None),
        P(("frame", "tile"), None),
        P(),
        P(),
        P(),
    )
    return jax.shard_map(local, mesh=mesh, in_specs=in_specs, out_specs=out_specs, check_vma=False)
```

```python
import functools
import math

import jax
import jax.numpy as jnp
from jax import lax
from jax.experimental import pallas as pl
from jax.experimental.pallas import tpu as pltpu
from jax.sharding import PartitionSpec as P

GROUPS = 32
EPS = 1e-05
SLOT = 16
BF = jnp.bfloat16
F32 = jnp.float32


def swap(x, axis):
    return lax.ppermute(x, axis, [(i, i ^ 1) for i in range(lax.axis_size(axis))])


def swap_both(x, axis, bit):
    sizes = (lax.axis_size("dp"), lax.axis_size(axis))
    pairs = [
        (i * sizes[1] + j, (i ^ 1) * sizes[1] + (j ^ bit))
        for i in range(sizes[0])
        for j in range(sizes[1])
    ]
    return lax.ppermute(x, ("dp", axis), pairs)


def round_up(value, unit):
    return -(-value // unit) * unit


def dot(a, b):
    return lax.dot_general(a, b, (((1,), (0,)), ((), ())), preferred_element_type=F32)


def dot_t(a, b):
    return lax.dot_general(a, b, (((1,), (1,)), ((), ())), preferred_element_type=F32)


def dot_rows(a, b):
    return lax.dot_general(a, b, (((0,), (0,)), ((), ())), preferred_element_type=F32)


def halves(x):
    high = x.astype(BF)
    return high, (x - high.astype(F32)).astype(BF)


def picker(rows, cols, depth, offset):
    row = lax.broadcasted_iota(jnp.int32, (rows, cols), 0)
    col = lax.broadcasted_iota(jnp.int32, (rows, cols), 1)
    return (col - row // depth == offset).astype(F32).astype(BF)


def spreader(rows, cols, depth, offset):
    row = lax.broadcasted_iota(jnp.int32, (rows, cols), 0)
    col = lax.broadcasted_iota(jnp.int32, (rows, cols), 1)
    return (row - col // depth == offset).astype(F32).astype(BF)


def head_sums(x, pick):
    high, low = halves(x)
    return dot(high, pick) + dot(low, pick)


def spread(x, both):
    high, low = halves(x)
    return dot(jnp.concatenate([high, low], axis=1), both)


def over_slots(x):
    step = SLOT
    while step < x.shape[1]:
        x = x + pltpu.roll(x, step, 1)
        step *= 2
    return x


def each(number, body):
    if number > 8:
        lax.fori_loop(0, number, lambda i, _: body(i), None)
    else:
        for i in range(number):
            body(i)


def pack_kernel(place, weights, cot, out):
    share, width = (weights.shape[0], cot.shape[1])
    frames = out.shape[0]
    count = cot.shape[0] // frames
    half = share // 2
    x = place[0]
    chosen = [
        jnp.where(x == 0, weights[:, pl.ds(c * width, width)], weights[:, pl.ds((2 + c) * width, width)])
        for c in (0, 1)
    ]
    for f in range(frames):
        start = (f // 2 % 2) * half
        rows = [cot[pl.ds(f * count, count), :], chosen[f % 2][start : start + half]]
        out[f] = jnp.concatenate(rows, axis=0)


def merge_kernel(place, mine, theirs, out):
    odd = place[4] % 2
    half = mine.shape[1]
    for owner in range(mine.shape[0]):
        first = jnp.where(odd == 0, mine[owner], theirs[owner])
        second = jnp.where(odd == 0, theirs[owner], mine[owner])
        out[owner] = jnp.concatenate([first, second], axis=0)


def taps_kernel(place, mine, theirs, out):
    odd = place[4] % 2
    share = out.shape[2]
    for owner in range(mine.shape[0]):
        first = jnp.where(odd == 0, mine[owner], theirs[owner])
        second = jnp.where(odd == 0, theirs[owner], mine[owner])
        block = jnp.concatenate([first, second], axis=0)
        for row in range(3):
            out[row, owner] = block[row * share : (row + 1) * share]


def join_kernel(place, *refs):
    pieces, out = (refs[:-1], refs[-1])
    x, core, tile = (place[0], place[1], place[2])
    frames = out.shape[1]
    for dc in (0, 1):
        own, by_tile, by_clip, low, high = pieces[5 * dc : 5 * dc + 5]
        own_kind = 2 * x + (core ^ dc)
        other_kind = 2 * (x ^ 1) + (core ^ dc)
        for f in range(frames):
            out[own_kind, f, tile] = own[f]
            out[own_kind, f, tile ^ 1] = by_tile[f]
            out[other_kind, f, tile] = by_clip[f]
            part, index = (low, f) if f < frames // 2 else (high, f - frames // 2)
            out[other_kind, f, tile ^ 1] = part[index]


def act_kernel(place, gain, *refs, cols, part):
    blocks, (acts, kept) = (refs[:-2], refs[-2:])
    half, width = blocks[0].shape
    tile, chosen = (place[2], place[3])
    choice = picker(width, part, 1, -part * chosen)
    per_group = width // GROUPS
    pick = picker(width, 128, per_group, 0)
    back = spreader(128, width, per_group, 0)

    def thirds(x):
        high, low = halves(x)
        return high, low, (x - high.astype(F32) - low.astype(F32)).astype(BF)

    totals, squares = ([], [])
    for frame in range(4):
        total, square = (0.0, 0.0)
        for dy in (0, 1):
            x = blocks[2 * frame + dy][...]
            start = pl.multiple_of((tile ^ dy) * half, half)
            kept[frame, pl.ds(start, half), :] = dot(x, choice).astype(BF)
            x = x.astype(F32)
            total = total + jnp.sum(x, axis=0, keepdims=True)
            square = square + jnp.sum(x * x, axis=0, keepdims=True)
        totals.append(total)
        squares.append(square)
    high, low, lowest = thirds(jnp.concatenate(totals + squares, axis=0))
    both = (dot(high, pick) + dot(low, pick) + dot(lowest, pick)) / (2 * half * per_group)
    mean = both[0:4]
    rstd = lax.rsqrt(both[4:8] - mean * mean + EPS)
    high, low, lowest = thirds(jnp.concatenate([mean, rstd], axis=0))
    both = dot(high, back) + dot(low, back) + dot(lowest, back)
    scales = both[4:8] * gain[...]
    for frame in range(4):
        acts[frame, pl.ds(0, cols), :] = jnp.zeros((cols, width), BF)
        acts[frame, pl.ds(cols + 2 * half, cols), :] = jnp.zeros((cols, width), BF)
        for dy in (0, 1):
            x = blocks[2 * frame + dy][...].astype(F32)
            zed = (x - both[frame : frame + 1]) * scales[frame : frame + 1]
            start = pl.multiple_of(cols + (tile ^ dy) * half, cols)
            acts[frame, pl.ds(start, half), :] = (zed / (1.0 + jnp.exp(-zed))).astype(BF)


def conv_kernel(place, weights, acts, kept, out, *, cols, part, blocks, count):
    x, core = (place[0], place[1])
    whole = kept.shape[1]
    half = whole // 2
    third = count // 3
    col = lax.broadcasted_iota(jnp.int32, (whole, part), 0) % cols
    for dx in (0, 1):
        mids = []
        for dc in (0, 1):
            frame = 2 * dc + dx
            taps = dot(acts[frame, pl.ds(0, whole), :], weights[0])
            taps += dot(acts[frame, pl.ds(cols, whole), :], weights[1])
            taps += dot(acts[frame, pl.ds(2 * cols, whole), :], weights[2])
            left = pltpu.roll(taps[:, :part], 1, 0)
            right = pltpu.roll(taps[:, 2 * part :], whole - 1, 0)
            pre = taps[:, part : 2 * part] + jnp.where(col > 0, left, 0.0)
            pre = pre + jnp.where(col < cols - 1, right, 0.0)
            mids.append((kept[frame].astype(F32) + pre).astype(BF))
        if blocks > 8:
            for dc in (0, 1):
                out[x ^ dx, dc] = mids[dc]
            continue
        for f in range(blocks):
            for t in (0, 1):
                start = t * half + f * count
                rows = [
                    jnp.concatenate(
                        [mid[start + third * j : start + third * (j + 1)] for j in range(3)], axis=1
                    )
                    for mid in mids
                ]
                index = ((x ^ dx) * blocks + f) * 2 + t
                out[index] = jnp.concatenate(rows, axis=0)


def attend_kernel(
    place, mid_in, cot_in, weights, qgain, kgain, scale,
    kept, sent, sums, d_raw, q_hat, k_hat, q_rstd, k_rstd, d_value,
    mid_s, cot_s, doubled, doubled_v, mixed_s, raw_s, probs_s,
    *, heads, count, padded, part,
):
    total, width = mid_s.shape
    frames = total // padded
    depth = width // heads
    lanes = scale.shape[-1]
    third = count // 3
    x, core, tile, plane = (place[0], place[1], place[2], place[4])
    mid_s[...] = jnp.zeros_like(mid_s)
    cot_s[...] = jnp.zeros_like(cot_s)
    for z in range(frames // 2):
        for e in (0, 1):
            f = 2 * z + e
            blocks = [
                mid_in[(x * frames + 2 * z + c) * 2 + t, pl.ds((e ^ c) * third, third), :]
                for x in (0, 1)
                for c in (0, 1)
                for t in (0, 1)
            ]
            for j in range(3):
                piece = [b[:, j * part : (j + 1) * part] for b in blocks]
                start = f * padded + j * third
                mid_s[pl.ds(start, third), :] = jnp.concatenate(piece, axis=1).astype(F32)
            cot_s[pl.ds(f * padded, count), :] = cot_in[f, pl.ds(0, count), :].astype(F32)
    mid = mid_s[...].astype(BF)
    cot = cot_s[...].astype(BF)
    pick = picker(width, lanes, depth, 0)
    both = jnp.concatenate([spreader(lanes, width, depth, 0)] * 2, axis=0)

    def stats(vec):
        cent = vec - spread(head_sums(vec, pick) / depth, both)
        var = head_sums(cent * cent, pick) / depth
        rstd = lax.rsqrt(var + EPS)
        return cent * spread(rstd, both), rstd

    hat, rstd = stats(dot(mid, weights[0]))
    q_hat[...] = hat
    q_rstd[...] = rstd
    q_norm = hat * qgain[...]
    hat, rstd = stats(dot(mid, weights[1]))
    k_hat[...] = hat
    k_rstd[...] = rstd
    hat = hat * kgain[...]
    doubled[pl.ds(0, total), :] = hat
    doubled[pl.ds(total, total), :] = hat
    value = dot(mid, weights[2]).astype(BF).astype(F32)
    doubled_v[pl.ds(0, total), :] = value
    doubled_v[pl.ds(total, total), :] = value
    d_mixed = dot_t(cot, weights[3]).astype(BF).astype(F32)
    raw_s[...] = jnp.zeros_like(raw_s)
    probs_s[...] = jnp.zeros_like(probs_s)

    def logits(s):
        here = picker(width, lanes, depth, SLOT * s)
        raw_s[...] += head_sums(q_norm * doubled[pl.ds(s * padded, total), :], here)
        probs_s[...] += head_sums(d_mixed * doubled_v[pl.ds(s * padded, total), :], here)

    each(frames, logits)
    raw = raw_s[...] / math.sqrt(depth)
    expo = jnp.exp(raw * scale[...])
    probs = expo / over_slots(expo)
    probs_b = probs.astype(BF)
    d_probs = probs_s[...]
    d_logits = probs * (d_probs - over_slots(probs * d_probs))
    sums[...] = jnp.sum(d_logits * raw, axis=0, keepdims=True)
    d_raw[...] = d_logits * scale[...] / math.sqrt(depth)
    mixed_s[...] = jnp.zeros_like(mixed_s)
    doubled[...] = jnp.zeros_like(doubled)

    def mix(s):
        weight = dot(probs_b, spreader(lanes, width, depth, SLOT * s))
        mixed_s[...] += weight * doubled_v[pl.ds(s * padded, total), :]
        doubled[pl.ds(s * padded, total), :] += weight * d_mixed

    each(frames, mix)
    dv = (doubled[pl.ds(0, total), :] + doubled[pl.ds(total, total), :]).astype(BF)
    d_value[...] = dv
    rows = kept.shape[3]

    def store(kind, term):
        for z in range(frames // 2):
            for t in (0, 1):
                start = (4 * z + t) * rows
                first = term[start : start + rows]
                second = term[start + 2 * rows : start + 3 * rows]
                kept[x ^ kind, tile ^ t, plane ^ z] = jnp.where(core == 0, first, second)
                sent[x ^ kind, tile ^ t, plane ^ z] = jnp.where(core == 0, second, first)

    store(1, dot_rows(mixed_s[...].astype(BF), cot).astype(BF))
    store(0, dot_rows(mid, dv).astype(BF))


def slope_kernel(
    d_raw, q_hat, k_hat, qgain, kgain,
    d_qn, d_kn,
    doubled, doubled_acc,
    *, heads, padded,
):
    total, width = q_hat.shape
    depth = width // heads
    frames = total // padded
    lanes = d_raw.shape[-1]
    k_norm = k_hat[...] * kgain[...]
    doubled[pl.ds(0, total), :] = k_norm
    doubled[pl.ds(total, total), :] = k_norm
    q_norm = q_hat[...] * qgain[...]
    doubled_acc[...] = jnp.zeros_like(doubled_acc)
    d_qn[...] = jnp.zeros_like(d_qn)
    high, low = halves(d_raw[...])
    pair = jnp.concatenate([high, low], axis=1)

    def shift(s):
        one = spreader(lanes, width, depth, SLOT * s)
        weight = dot(pair, jnp.concatenate([one, one], axis=0))
        d_qn[...] += weight * doubled[pl.ds(s * padded, total), :]
        doubled_acc[pl.ds(s * padded, total), :] += weight * q_norm

    each(frames, shift)
    d_kn[...] = doubled_acc[pl.ds(0, total), :] + doubled_acc[pl.ds(total, total), :]


def back_kernel(
    d_qn, d_kn, q_hat, k_hat, q_rstd, k_rstd, d_value, weights, qgain, kgain, scale_sums,
    d_mid,
    *, heads, count, padded,
):
    total, width = q_hat.shape
    depth = width // heads
    frames = total // padded
    lanes = scale_sums.shape[-1]
    pick = picker(width, lanes, depth, 0)
    both = jnp.concatenate([spreader(lanes, width, depth, 0)] * 2, axis=0)

    def back(dhat, hat, rstd):
        first = spread(head_sums(dhat, pick) / depth, both)
        second = spread(head_sums(dhat * hat, pick) / depth, both)
        return (spread(rstd, both) * (dhat - first - hat * second)).astype(BF)

    d_query = back(d_qn[...] * qgain[...], q_hat[...], q_rstd[...])
    d_key = back(d_kn[...] * kgain[...], k_hat[...], k_rstd[...])
    out = dot_t(d_query, weights[0])
    out += dot_t(d_key, weights[1])
    out += dot_t(d_value[...], weights[2])

    row = lax.broadcasted_iota(jnp.int32, (width, 128), 0)
    col = lax.broadcasted_iota(jnp.int32, (width, 128), 1)
    fold = (row % depth == col).astype(F32)

    def folded(d_norm, hat):
        sums = jnp.sum(d_norm * hat, axis=0, keepdims=True)
        sums = jnp.broadcast_to(sums, (8, width))
        return jnp.dot(sums, fold, precision=lax.Precision.HIGHEST, preferred_element_type=F32)[0:1]

    by_head = over_slots(jnp.broadcast_to(scale_sums[...], (8, lanes)))[0:1, :128]
    small = [folded(d_qn[...], q_hat[...]), folded(d_kn[...], k_hat[...]), by_head]
    small.append(jnp.zeros((1, width - 384), F32))
    small = jnp.concatenate(small, axis=1)
    high, low = halves(small)
    lowest = (small - high.astype(F32) - low.astype(F32)).astype(BF)
    spare = [high.astype(F32), low.astype(F32), lowest.astype(F32)]
    if padded - count > 3:
        spare.append(jnp.zeros((padded - count - 3, width), F32))
    spare = jnp.concatenate(spare, axis=0)
    for f in range(frames):
        tokens = out[f * padded : f * padded + count]
        d_mid[f] = jnp.concatenate([tokens, spare], axis=0).astype(BF)


def call(kernel, mebibytes, outs, scratch, *args):
    smem = pl.BlockSpec(memory_space=pltpu.SMEM)
    vmem = pl.BlockSpec(memory_space=pltpu.VMEM)
    return pl.pallas_call(
        kernel,
        out_shape=[jax.ShapeDtypeStruct(shape, dtype) for shape, dtype in outs],
        in_specs=[smem if arg.dtype == jnp.int32 else vmem for arg in args],
        out_specs=[vmem] * len(outs),
        scratch_shapes=[pltpu.VMEM(shape, dtype) for shape, dtype in scratch],
        compiler_params=pltpu.CompilerParams(vmem_limit_bytes=mebibytes << 20),
    )(*args)


def local(
    clip_input, cotangent, norm_gain, conv_weight, attn_weight, query_gain, key_gain, logit_scale
):
    source = clip_input[0, 0]
    cot = cotangent[0, 0]
    rows, cols, width = source.shape
    heads = logit_scale.shape[0]
    depth = width // heads
    tokens = rows * cols
    clips, frames, tiles = (lax.axis_size(name) for name in ("dp", "frame", "tile"))
    square = ("frame", "tile")
    ranks = frames * tiles
    share = conv_weight.shape[1]
    count = tokens // frames
    third = count // 3
    part = width // 8
    x = lax.axis_index("dp") % 2
    core = lax.axis_index("frame") % 2
    tile = lax.axis_index("tile")
    plane = lax.axis_index("frame") // 2
    place = jnp.stack([x, core, tile, 4 * x + 2 * core + tile, plane]).astype(jnp.int32)
    flat = source.reshape(tokens, width)

    (packed,) = call(
        pack_kernel,
        12,
        [((frames, count + share // 2, width), BF)],
        [],
        place,
        attn_weight,
        cot.reshape(tokens, width),
    )
    packed = lax.all_to_all(packed, "frame", 0, 0, tiled=True)

    half = tokens // 2
    along_x = swap(flat, "dp")
    along_y = swap(flat, "tile")
    across = jnp.concatenate([swap(along_x[:half], "tile"), swap(along_y[half:], "dp")])
    pieces = [flat, along_y, along_x, across]
    pieces += [swap(piece, "frame") for piece in pieces]

    planes = [(i, i ^ 2) for i in range(frames)]
    lines = 3 * share // 2
    mine = lax.dynamic_slice_in_dim(conv_weight, x * (width // 2), width // 2, axis=2)
    mine = mine.reshape(3, 3, share, 4, part).transpose(3, 0, 2, 1, 4)
    mine = mine.reshape(4, 2, lines, 3 * part).transpose(1, 0, 2, 3)
    mine = jnp.broadcast_to(mine[None], (frames // 4,) + mine.shape)
    mine = mine.reshape(ranks, lines, 3 * part)
    mine, packed, pieces = lax.optimization_barrier((mine, packed, pieces))
    conv_half = lax.all_to_all(mine, square, 0, 0, tiled=True)
    own = packed[:, count:]
    own_other = lax.ppermute(own, "frame", planes)
    conv_other = lax.ppermute(conv_half, "frame", planes)
    acts, kept = call(
        functools.partial(act_kernel, cols=cols, part=part),
        20,
        [((4, tiles * tokens + 2 * cols, width), BF), ((4, tiles * tokens, part), BF)],
        [],
        place,
        norm_gain[None],
        *pieces,
    )
    (conv_full,) = call(
        taps_kernel, 12, [((3, ranks, share, 3 * part), BF)], [], place, conv_half, conv_other
    )
    conv_full = conv_full.reshape(3, width, 3 * part)
    (own,) = call(merge_kernel, 8, [((frames, share, width), BF)], [], place, own, own_other)
    by_tile = swap(own, "tile")
    by_clip = swap(own, "dp")
    blocked = (2 * ranks, 2 * third, 3 * part)
    plain = (2, 2, tiles * tokens, part)
    (mid,) = call(
        functools.partial(conv_kernel, cols=cols, part=part, blocks=frames, count=count),
        16,
        [(plain if frames > 8 else blocked, BF)],
        [],
        place,
        conv_full,
        acts,
        kept,
    )
    if frames > 8:
        mid = mid.reshape(2, 2, tiles, frames, 3, third, part).transpose(0, 3, 2, 1, 5, 4, 6)
        mid = mid.reshape(blocked)
    mid, by_tile, by_clip = lax.optimization_barrier((mid, by_tile, by_clip))
    groups = None
    if clips > 2:
        groups = [[2 * ranks * g + i for i in range(2 * ranks)] for g in range(clips // 2)]
    mid = lax.all_to_all(mid, ("dp",) + square, 0, 0, axis_index_groups=groups, tiled=True)

    middle = frames // 2
    parts = [own, by_tile, by_clip, swap(by_clip[:middle], "tile"), swap(by_tile[middle:], "dp")]
    parts += [swap(piece, "frame") for piece in parts]
    parts, mid = lax.optimization_barrier((parts, mid))
    (attn_full,) = call(
        join_kernel, 16, [((4, frames, tiles, share, width), BF)], [], place, *parts
    )
    attn_full = attn_full.reshape(4, width, width)

    lanes = frames * SLOT
    padded = round_up(count + 3, 8)
    total = frames * padded
    scale = jnp.tile(jnp.pad(logit_scale, (0, SLOT - heads)), frames)[None]
    qgain = jnp.tile(query_gain, heads)[None]
    kgain = jnp.tile(key_gain, heads)[None]
    full = (total, width)
    double = (2 * total, width)
    narrow = (total, lanes)
    kept, sent, scale_sums, d_raw, q_hat, k_hat, q_rstd, k_rstd, d_value = call(
        functools.partial(attend_kernel, heads=heads, count=count, padded=padded, part=part),
        20,
        [
            ((2, 2, frames // 2, share, width), BF),
            ((2, 2, frames // 2, share, width), BF),
            ((1, lanes), F32), (narrow, F32),
            (full, F32), (full, F32), (narrow, F32), (narrow, F32), (full, BF),
        ],
        [
            (full, F32), (full, F32), (double, F32), (double, F32), (full, F32),
            (narrow, F32), (narrow, F32),
        ],
        place, mid, packed, attn_full, qgain, kgain, scale,
    )
    d_qn, d_kn = call(
        functools.partial(slope_kernel, heads=heads, padded=padded),
        16,
        [(full, F32), (full, F32)],
        [(double, F32), (double, F32)],
        d_raw, q_hat, k_hat, qgain, kgain,
    )

    def add(mine, theirs):
        return (mine.astype(F32) + theirs.astype(F32)).astype(BF)

    shares = add(kept, swap(sent, "frame"))
    shares, d_qn = lax.optimization_barrier((shares, d_qn))
    (d_mid,) = call(
        functools.partial(back_kernel, heads=heads, count=count, padded=padded),
        16,
        [((frames, padded, width), BF)],
        [],
        d_qn, d_kn, q_hat, k_hat, q_rstd, k_rstd, d_value, attn_full, qgain, kgain, scale_sums,
    )
    d_back = lax.all_to_all(d_mid, "frame", 0, 0, tiled=True)
    theirs, _ = lax.optimization_barrier((swap(shares[1], "dp"), d_mid))
    shares = add(shares[0], theirs)
    shares = add(shares[0], swap(shares[1], "tile"))
    shares, d_back = lax.optimization_barrier((shares, d_back))
    step = frames // 4
    while step > 1:
        pairs = [(i, i ^ (2 * step)) for i in range(frames)]
        shares = add(shares[:step], lax.ppermute(shares[step:], "frame", pairs))
        step //= 2
    small = jnp.sum(d_back[:, count : count + 3].astype(F32), axis=(0, 1))
    d_back = d_back[:, :count].reshape(rows, cols, width)
    mid_grad = (cot.astype(F32) + d_back.astype(F32)).astype(BF)

    small, _ = lax.optimization_barrier((small, shares))
    by_plane = lax.ppermute(shares[1], "frame", planes)
    by_clip = swap(shares[0], "dp")
    by_both = swap_both(shares[1], "frame", 2)
    shares = shares[0].astype(F32) + by_plane.astype(F32)
    theirs = by_clip.astype(F32) + by_both.astype(F32)
    small = small + swap(small, "tile")
    small = small + swap(small, "dp")
    if clips > 2:
        same_clip = [[i for i in range(clips) if i % 2 == c] for c in (0, 1)]
        small, shares, theirs = lax.psum(
            (small, shares, theirs), "dp", axis_index_groups=same_clip
        )
    factor = 1.0 / math.sqrt(clips * frames * tiles * tokens)
    value_grad = jnp.where(x == 0, shares, theirs) * factor
    out_proj_grad = jnp.where(x == 0, theirs, shares) * factor
    scale_sum = small[256 : 256 + heads]
    return (
        mid_grad[None, None],
        value_grad,
        out_proj_grad,
        small[:depth] * factor,
        small[128 : 128 + depth] * factor,
        scale_sum * factor,
    )


def solution(mesh):
    in_specs = (
        P("dp", "frame", "tile", None, None),
        P("dp", "frame", "tile", None, None),
        P(),
        P(None, ("frame", "tile"), None),
        P(("frame", "tile"), None),
        P(),
        P(),
        P(),
    )
    out_specs = (
        P("dp", "frame", "tile", None, None),
        P(("frame", "tile"), None),
        P(("frame", "tile"), None),
        P(),
        P(),
        P(),
    )
    return jax.shard_map(local, mesh=mesh, in_specs=in_specs, out_specs=out_specs, check_vma=False)
```

```python
import functools
import math

import jax
import jax.numpy as jnp
from jax import lax
from jax.experimental import pallas as pl
from jax.experimental.pallas import tpu as pltpu
from jax.sharding import PartitionSpec as P

GROUPS = 32
EPS = 1e-05
SLOT = 16
BF = jnp.bfloat16
F32 = jnp.float32


def swap(x, axis):
    return lax.ppermute(x, axis, [(i, i ^ 1) for i in range(lax.axis_size(axis))])


def swap_both(x, axis, bit):
    sizes = (lax.axis_size("dp"), lax.axis_size(axis))
    pairs = [
        (i * sizes[1] + j, (i ^ 1) * sizes[1] + (j ^ bit))
        for i in range(sizes[0])
        for j in range(sizes[1])
    ]
    return lax.ppermute(x, ("dp", axis), pairs)


def round_up(value, unit):
    return -(-value // unit) * unit


def dot(a, b):
    return lax.dot_general(a, b, (((1,), (0,)), ((), ())), preferred_element_type=F32)


def dot_t(a, b):
    return lax.dot_general(a, b, (((1,), (1,)), ((), ())), preferred_element_type=F32)


def dot_rows(a, b):
    return lax.dot_general(a, b, (((0,), (0,)), ((), ())), preferred_element_type=F32)


def halves(x):
    high = x.astype(BF)
    return high, (x - high.astype(F32)).astype(BF)


def picker(rows, cols, depth, offset):
    row = lax.broadcasted_iota(jnp.int32, (rows, cols), 0)
    col = lax.broadcasted_iota(jnp.int32, (rows, cols), 1)
    return (col - row // depth == offset).astype(F32).astype(BF)


def spreader(rows, cols, depth, offset):
    row = lax.broadcasted_iota(jnp.int32, (rows, cols), 0)
    col = lax.broadcasted_iota(jnp.int32, (rows, cols), 1)
    return (row - col // depth == offset).astype(F32).astype(BF)


def head_sums(x, pick):
    high, low = halves(x)
    return dot(high, pick) + dot(low, pick)


def spread(x, both):
    high, low = halves(x)
    return dot(jnp.concatenate([high, low], axis=1), both)


def over_slots(x):
    step = SLOT
    while step < x.shape[1]:
        x = x + pltpu.roll(x, step, 1)
        step *= 2
    return x


def each(number, body):
    if number > 8:
        lax.fori_loop(0, number, lambda i, _: body(i), None)
    else:
        for i in range(number):
            body(i)


def pack_kernel(place, weights, cot, out):
    share, width = (weights.shape[0], cot.shape[1])
    frames = out.shape[0]
    count = cot.shape[0] // frames
    half = share // 2
    x = place[0]
    chosen = [
        jnp.where(x == 0, weights[:, pl.ds(c * width, width)], weights[:, pl.ds((2 + c) * width, width)])
        for c in (0, 1)
    ]
    for f in range(frames):
        start = (f // 2 % 2) * half
        rows = [cot[pl.ds(f * count, count), :], chosen[f % 2][start : start + half]]
        out[f] = jnp.concatenate(rows, axis=0)


def merge_kernel(place, mine, theirs, out):
    odd = place[4] % 2
    half = mine.shape[1]
    for owner in range(mine.shape[0]):
        first = jnp.where(odd == 0, mine[owner], theirs[owner])
        second = jnp.where(odd == 0, theirs[owner], mine[owner])
        out[owner] = jnp.concatenate([first, second], axis=0)


def taps_kernel(place, mine, theirs, out):
    odd = place[4] % 2
    share = out.shape[2]
    for owner in range(mine.shape[0]):
        first = jnp.where(odd == 0, mine[owner], theirs[owner])
        second = jnp.where(odd == 0, theirs[owner], mine[owner])
        block = jnp.concatenate([first, second], axis=0)
        for row in range(3):
            out[row, owner] = block[row * share : (row + 1) * share]


def join_kernel(place, *refs):
    pieces, out = (refs[:-1], refs[-1])
    x, core, tile = (place[0], place[1], place[2])
    frames = out.shape[1]
    for dc in (0, 1):
        own, by_tile, by_clip, low, high = pieces[5 * dc : 5 * dc + 5]
        own_kind = 2 * x + (core ^ dc)
        other_kind = 2 * (x ^ 1) + (core ^ dc)
        for f in range(frames):
            out[own_kind, f, tile] = own[f]
            out[own_kind, f, tile ^ 1] = by_tile[f]
            out[other_kind, f, tile] = by_clip[f]
            part, index = (low, f) if f < frames // 2 else (high, f - frames // 2)
            out[other_kind, f, tile ^ 1] = part[index]


def act_kernel(place, gain, *refs, cols, part):
    blocks, (acts, kept) = (refs[:-2], refs[-2:])
    half, width = blocks[0].shape
    tile, chosen = (place[2], place[3])
    choice = picker(width, part, 1, -part * chosen)
    per_group = width // GROUPS
    pick = picker(width, 128, per_group, 0)
    back = spreader(128, width, per_group, 0)

    def thirds(x):
        high, low = halves(x)
        return high, low, (x - high.astype(F32) - low.astype(F32)).astype(BF)

    totals, squares = ([], [])
    for frame in range(4):
        total, square = (0.0, 0.0)
        for dy in (0, 1):
            x = blocks[2 * frame + dy][...]
            start = pl.multiple_of((tile ^ dy) * half, half)
            kept[frame, pl.ds(start, half), :] = dot(x, choice).astype(BF)
            x = x.astype(F32)
            total = total + jnp.sum(x, axis=0, keepdims=True)
            square = square + jnp.sum(x * x, axis=0, keepdims=True)
        totals.append(total)
        squares.append(square)
    high, low, lowest = thirds(jnp.concatenate(totals + squares, axis=0))
    both = (dot(high, pick) + dot(low, pick) + dot(lowest, pick)) / (2 * half * per_group)
    mean = both[0:4]
    rstd = lax.rsqrt(both[4:8] - mean * mean + EPS)
    high, low, lowest = thirds(jnp.concatenate([mean, rstd], axis=0))
    both = dot(high, back) + dot(low, back) + dot(lowest, back)
    scales = both[4:8] * gain[...]
    for frame in range(4):
        acts[frame, pl.ds(0, cols), :] = jnp.zeros((cols, width), BF)
        acts[frame, pl.ds(cols + 2 * half, cols), :] = jnp.zeros((cols, width), BF)
        for dy in (0, 1):
            x = blocks[2 * frame + dy][...].astype(F32)
            zed = (x - both[frame : frame + 1]) * scales[frame : frame + 1]
            start = pl.multiple_of(cols + (tile ^ dy) * half, cols)
            acts[frame, pl.ds(start, half), :] = (zed / (1.0 + jnp.exp(-zed))).astype(BF)


def conv_kernel(place, weights, acts, kept, out, *, cols, part, blocks, count):
    x, core = (place[0], place[1])
    whole = kept.shape[1]
    half = whole // 2
    third = count // 3
    col = lax.broadcasted_iota(jnp.int32, (whole, part), 0) % cols
    for dx in (0, 1):
        mids = []
        for dc in (0, 1):
            frame = 2 * dc + dx
            taps = dot(acts[frame, pl.ds(0, whole), :], weights[0])
            taps += dot(acts[frame, pl.ds(cols, whole), :], weights[1])
            taps += dot(acts[frame, pl.ds(2 * cols, whole), :], weights[2])
            left = pltpu.roll(taps[:, :part], 1, 0)
            right = pltpu.roll(taps[:, 2 * part :], whole - 1, 0)
            pre = taps[:, part : 2 * part] + jnp.where(col > 0, left, 0.0)
            pre = pre + jnp.where(col < cols - 1, right, 0.0)
            mids.append((kept[frame].astype(F32) + pre).astype(BF))
        if blocks > 8:
            for dc in (0, 1):
                out[x ^ dx, dc] = mids[dc]
            continue
        for f in range(blocks):
            for t in (0, 1):
                start = t * half + f * count
                rows = [
                    jnp.concatenate(
                        [mid[start + third * j : start + third * (j + 1)] for j in range(3)], axis=1
                    )
                    for mid in mids
                ]
                index = ((x ^ dx) * blocks + f) * 2 + t
                out[index] = jnp.concatenate(rows, axis=0)


def attend_kernel(
    place, mid_in, cot_in, weights, qgain, kgain, scale,
    kept, sent, sums, d_raw, q_hat, k_hat, q_rstd, k_rstd, d_value,
    mid_s, cot_s, doubled, doubled_v, mixed_s, raw_s, probs_s,
    *, heads, count, padded, part,
):
    total, width = mid_s.shape
    frames = total // padded
    depth = width // heads
    lanes = scale.shape[-1]
    third = count // 3
    x, core, tile, plane = (place[0], place[1], place[2], place[4])
    mid_s[...] = jnp.zeros_like(mid_s)
    cot_s[...] = jnp.zeros_like(cot_s)
    for z in range(frames // 2):
        for e in (0, 1):
            f = 2 * z + e
            blocks = [
                mid_in[(x * frames + 2 * z + c) * 2 + t, pl.ds((e ^ c) * third, third), :]
                for x in (0, 1)
                for c in (0, 1)
                for t in (0, 1)
            ]
            for j in range(3):
                piece = [b[:, j * part : (j + 1) * part] for b in blocks]
                start = f * padded + j * third
                mid_s[pl.ds(start, third), :] = jnp.concatenate(piece, axis=1).astype(F32)
            cot_s[pl.ds(f * padded, count), :] = cot_in[f, pl.ds(0, count), :].astype(F32)
    mid = mid_s[...].astype(BF)
    cot = cot_s[...].astype(BF)
    pick = picker(width, lanes, depth, 0)
    both = jnp.concatenate([spreader(lanes, width, depth, 0)] * 2, axis=0)

    def stats(vec):
        cent = vec - spread(head_sums(vec, pick) / depth, both)
        var = head_sums(cent * cent, pick) / depth
        rstd = lax.rsqrt(var + EPS)
        return cent * spread(rstd, both), rstd

    hat, rstd = stats(dot(mid, weights[0]))
    q_hat[...] = hat
    q_rstd[...] = rstd
    q_norm = hat * qgain[...]
    hat, rstd = stats(dot(mid, weights[1]))
    k_hat[...] = hat
    k_rstd[...] = rstd
    hat = hat * kgain[...]
    doubled[pl.ds(0, total), :] = hat
    doubled[pl.ds(total, total), :] = hat
    value = dot(mid, weights[2]).astype(BF).astype(F32)
    doubled_v[pl.ds(0, total), :] = value
    doubled_v[pl.ds(total, total), :] = value
    d_mixed = dot_t(cot, weights[3]).astype(BF).astype(F32)
    raw_s[...] = jnp.zeros_like(raw_s)
    probs_s[...] = jnp.zeros_like(probs_s)

    def logits(s):
        here = picker(width, lanes, depth, SLOT * s)
        raw_s[...] += head_sums(q_norm * doubled[pl.ds(s * padded, total), :], here)
        probs_s[...] += head_sums(d_mixed * doubled_v[pl.ds(s * padded, total), :], here)

    each(frames, logits)
    raw = raw_s[...] / math.sqrt(depth)
    expo = jnp.exp(raw * scale[...])
    probs = expo / over_slots(expo)
    probs_b = probs.astype(BF)
    d_probs = probs_s[...]
    d_logits = probs * (d_probs - over_slots(probs * d_probs))
    sums[...] = jnp.sum(d_logits * raw, axis=0, keepdims=True)
    d_raw[...] = d_logits * scale[...] / math.sqrt(depth)
    mixed_s[...] = jnp.zeros_like(mixed_s)
    doubled[...] = jnp.zeros_like(doubled)

    def mix(s):
        weight = dot(probs_b, spreader(lanes, width, depth, SLOT * s))
        mixed_s[...] += weight * doubled_v[pl.ds(s * padded, total), :]
        doubled[pl.ds(s * padded, total), :] += weight * d_mixed

    each(frames, mix)
    dv = (doubled[pl.ds(0, total), :] + doubled[pl.ds(total, total), :]).astype(BF)
    d_value[...] = dv
    rows = kept.shape[3]

    def store(kind, term):
        for z in range(frames // 2):
            for t in (0, 1):
                start = (4 * z + t) * rows
                first = term[start : start + rows]
                second = term[start + 2 * rows : start + 3 * rows]
                kept[x ^ kind, tile ^ t, plane ^ z] = jnp.where(core == 0, first, second)
                sent[x ^ kind, tile ^ t, plane ^ z] = jnp.where(core == 0, second, first)

    store(1, dot_rows(mixed_s[...].astype(BF), cot).astype(BF))
    store(0, dot_rows(mid, dv).astype(BF))


def slope_kernel(
    d_raw, q_hat, k_hat, qgain, kgain,
    d_qn, d_kn,
    doubled, doubled_acc,
    *, heads, padded,
):
    total, width = q_hat.shape
    depth = width // heads
    frames = total // padded
    lanes = d_raw.shape[-1]
    k_norm = k_hat[...] * kgain[...]
    doubled[pl.ds(0, total), :] = k_norm
    doubled[pl.ds(total, total), :] = k_norm
    q_norm = q_hat[...] * qgain[...]
    doubled_acc[...] = jnp.zeros_like(doubled_acc)
    d_qn[...] = jnp.zeros_like(d_qn)
    high, low = halves(d_raw[...])
    pair = jnp.concatenate([high, low], axis=1)

    def shift(s):
        one = spreader(lanes, width, depth, SLOT * s)
        weight = dot(pair, jnp.concatenate([one, one], axis=0))
        d_qn[...] += weight * doubled[pl.ds(s * padded, total), :]
        doubled_acc[pl.ds(s * padded, total), :] += weight * q_norm

    each(frames, shift)
    d_kn[...] = doubled_acc[pl.ds(0, total), :] + doubled_acc[pl.ds(total, total), :]


def back_kernel(
    d_qn, d_kn, q_hat, k_hat, q_rstd, k_rstd, d_value, weights, qgain, kgain, scale_sums,
    d_mid,
    *, heads, count, padded,
):
    total, width = q_hat.shape
    depth = width // heads
    frames = total // padded
    lanes = scale_sums.shape[-1]
    pick = picker(width, lanes, depth, 0)
    both = jnp.concatenate([spreader(lanes, width, depth, 0)] * 2, axis=0)

    def back(dhat, hat, rstd):
        first = spread(head_sums(dhat, pick) / depth, both)
        second = spread(head_sums(dhat * hat, pick) / depth, both)
        return (spread(rstd, both) * (dhat - first - hat * second)).astype(BF)

    d_query = back(d_qn[...] * qgain[...], q_hat[...], q_rstd[...])
    d_key = back(d_kn[...] * kgain[...], k_hat[...], k_rstd[...])
    out = dot_t(d_query, weights[0])
    out += dot_t(d_key, weights[1])
    out += dot_t(d_value[...], weights[2])

    row = lax.broadcasted_iota(jnp.int32, (width, 128), 0)
    col = lax.broadcasted_iota(jnp.int32, (width, 128), 1)
    fold = (row % depth == col).astype(F32)

    def folded(d_norm, hat):
        sums = jnp.sum(d_norm * hat, axis=0, keepdims=True)
        sums = jnp.broadcast_to(sums, (8, width))
        return jnp.dot(sums, fold, precision=lax.Precision.HIGHEST, preferred_element_type=F32)[0:1]

    by_head = over_slots(jnp.broadcast_to(scale_sums[...], (8, lanes)))[0:1, :128]
    small = [folded(d_qn[...], q_hat[...]), folded(d_kn[...], k_hat[...]), by_head]
    small.append(jnp.zeros((1, width - 384), F32))
    small = jnp.concatenate(small, axis=1)
    high, low = halves(small)
    lowest = (small - high.astype(F32) - low.astype(F32)).astype(BF)
    spare = [high.astype(F32), low.astype(F32), lowest.astype(F32)]
    if padded - count > 3:
        spare.append(jnp.zeros((padded - count - 3, width), F32))
    spare = jnp.concatenate(spare, axis=0)
    for f in range(frames):
        tokens = out[f * padded : f * padded + count]
        d_mid[f] = jnp.concatenate([tokens, spare], axis=0).astype(BF)


def call(kernel, mebibytes, outs, scratch, *args):
    smem = pl.BlockSpec(memory_space=pltpu.SMEM)
    vmem = pl.BlockSpec(memory_space=pltpu.VMEM)
    return pl.pallas_call(
        kernel,
        out_shape=[jax.ShapeDtypeStruct(shape, dtype) for shape, dtype in outs],
        in_specs=[smem if arg.dtype == jnp.int32 else vmem for arg in args],
        out_specs=[vmem] * len(outs),
        scratch_shapes=[pltpu.VMEM(shape, dtype) for shape, dtype in scratch],
        compiler_params=pltpu.CompilerParams(vmem_limit_bytes=mebibytes << 20),
    )(*args)


def local(
    clip_input, cotangent, norm_gain, conv_weight, attn_weight, query_gain, key_gain, logit_scale
):
    source = clip_input[0, 0]
    cot = cotangent[0, 0]
    rows, cols, width = source.shape
    heads = logit_scale.shape[0]
    depth = width // heads
    tokens = rows * cols
    clips, frames, tiles = (lax.axis_size(name) for name in ("dp", "frame", "tile"))
    square = ("frame", "tile")
    ranks = frames * tiles
    share = conv_weight.shape[1]
    count = tokens // frames
    third = count // 3
    part = width // 8
    x = lax.axis_index("dp") % 2
    core = lax.axis_index("frame") % 2
    tile = lax.axis_index("tile")
    plane = lax.axis_index("frame") // 2
    place = jnp.stack([x, core, tile, 4 * x + 2 * core + tile, plane]).astype(jnp.int32)
    flat = source.reshape(tokens, width)

    (packed,) = call(
        pack_kernel,
        12,
        [((frames, count + share // 2, width), BF)],
        [],
        place,
        attn_weight,
        cot.reshape(tokens, width),
    )
    packed = lax.all_to_all(packed, "frame", 0, 0, tiled=True)

    half = tokens // 2
    along_x = swap(flat, "dp")
    along_y = swap(flat, "tile")
    across = jnp.concatenate([swap(along_x[:half], "tile"), swap(along_y[half:], "dp")])
    pieces = [flat, along_y, along_x, across]
    pieces += [swap(piece, "frame") for piece in pieces]

    planes = [(i, i ^ 2) for i in range(frames)]
    lines = 3 * share // 2
    mine = lax.dynamic_slice_in_dim(conv_weight, x * (width // 2), width // 2, axis=2)
    mine = mine.reshape(3, 3, share, 4, part).transpose(3, 0, 2, 1, 4)
    mine = mine.reshape(4, 2, lines, 3 * part).transpose(1, 0, 2, 3)
    mine = jnp.broadcast_to(mine[None], (frames // 4,) + mine.shape)
    mine = mine.reshape(ranks, lines, 3 * part)
    mine, packed, pieces = lax.optimization_barrier((mine, packed, pieces))
    conv_half = lax.all_to_all(mine, square, 0, 0, tiled=True)
    own = packed[:, count:]
    own_other = lax.ppermute(own, "frame", planes)
    conv_other = lax.ppermute(conv_half, "frame", planes)
    acts, kept = call(
        functools.partial(act_kernel, cols=cols, part=part),
        20,
        [((4, tiles * tokens + 2 * cols, width), BF), ((4, tiles * tokens, part), BF)],
        [],
        place,
        norm_gain[None],
        *pieces,
    )
    (conv_full,) = call(
        taps_kernel, 12, [((3, ranks, share, 3 * part), BF)], [], place, conv_half, conv_other
    )
    conv_full = conv_full.reshape(3, width, 3 * part)
    (own,) = call(merge_kernel, 8, [((frames, share, width), BF)], [], place, own, own_other)
    by_tile = swap(own, "tile")
    by_clip = swap(own, "dp")
    blocked = (2 * ranks, 2 * third, 3 * part)
    plain = (2, 2, tiles * tokens, part)
    (mid,) = call(
        functools.partial(conv_kernel, cols=cols, part=part, blocks=frames, count=count),
        16,
        [(plain if frames > 8 else blocked, BF)],
        [],
        place,
        conv_full,
        acts,
        kept,
    )
    if frames > 8:
        mid = mid.reshape(2, 2, tiles, frames, 3, third, part).transpose(0, 3, 2, 1, 5, 4, 6)
        mid = mid.reshape(blocked)
    mid, by_tile, by_clip = lax.optimization_barrier((mid, by_tile, by_clip))
    groups = None
    if clips > 2:
        groups = [[2 * ranks * g + i for i in range(2 * ranks)] for g in range(clips // 2)]
    mid = lax.all_to_all(mid, ("dp",) + square, 0, 0, axis_index_groups=groups, tiled=True)

    middle = frames // 2
    parts = [own, by_tile, by_clip, swap(by_clip[:middle], "tile"), swap(by_tile[middle:], "dp")]
    parts += [swap(piece, "frame") for piece in parts]
    parts, mid = lax.optimization_barrier((parts, mid))
    (attn_full,) = call(
        join_kernel, 16, [((4, frames, tiles, share, width), BF)], [], place, *parts
    )
    attn_full = attn_full.reshape(4, width, width)

    lanes = frames * SLOT
    padded = round_up(count + 3, 8)
    total = frames * padded
    scale = jnp.tile(jnp.pad(logit_scale, (0, SLOT - heads)), frames)[None]
    qgain = jnp.tile(query_gain, heads)[None]
    kgain = jnp.tile(key_gain, heads)[None]
    full = (total, width)
    double = (2 * total, width)
    narrow = (total, lanes)
    kept, sent, scale_sums, d_raw, q_hat, k_hat, q_rstd, k_rstd, d_value = call(
        functools.partial(attend_kernel, heads=heads, count=count, padded=padded, part=part),
        20,
        [
            ((2, 2, frames // 2, share, width), BF),
            ((2, 2, frames // 2, share, width), BF),
            ((1, lanes), F32), (narrow, F32),
            (full, F32), (full, F32), (narrow, F32), (narrow, F32), (full, BF),
        ],
        [
            (full, F32), (full, F32), (double, F32), (double, F32), (full, F32),
            (narrow, F32), (narrow, F32),
        ],
        place, mid, packed, attn_full, qgain, kgain, scale,
    )
    d_qn, d_kn = call(
        functools.partial(slope_kernel, heads=heads, padded=padded),
        16,
        [(full, F32), (full, F32)],
        [(double, F32), (double, F32)],
        d_raw, q_hat, k_hat, qgain, kgain,
    )

    def add(mine, theirs):
        return (mine.astype(F32) + theirs.astype(F32)).astype(BF)

    shares = add(kept, swap(sent, "frame"))
    shares, d_qn = lax.optimization_barrier((shares, d_qn))
    (d_mid,) = call(
        functools.partial(back_kernel, heads=heads, count=count, padded=padded),
        16,
        [((frames, padded, width), BF)],
        [],
        d_qn, d_kn, q_hat, k_hat, q_rstd, k_rstd, d_value, attn_full, qgain, kgain, scale_sums,
    )
    d_back = lax.all_to_all(d_mid, "frame", 0, 0, tiled=True)
    theirs, _ = lax.optimization_barrier((swap(shares[1], "dp"), d_mid))
    shares = add(shares[0], theirs)
    shares = add(shares[0], swap(shares[1], "tile"))
    shares, d_back = lax.optimization_barrier((shares, d_back))
    step = frames // 4
    while step > 1:
        pairs = [(i, i ^ (2 * step)) for i in range(frames)]
        shares = add(shares[:step], lax.ppermute(shares[step:], "frame", pairs))
        step //= 2
    small = jnp.sum(d_back[:, count : count + 3].astype(F32), axis=(0, 1))
    d_back = d_back[:, :count].reshape(rows, cols, width)
    mid_grad = (cot.astype(F32) + d_back.astype(F32)).astype(BF)

    small = small + swap(small, "tile")
    small, _ = lax.optimization_barrier((small, shares))
    by_plane = lax.ppermute(shares[1], "frame", planes)
    by_clip = swap(shares[0], "dp")
    by_both = swap_both(shares[1], "frame", 2)
    shares = shares[0].astype(F32) + by_plane.astype(F32)
    theirs = by_clip.astype(F32) + by_both.astype(F32)
    small = small + swap(small, "dp")
    if clips > 2:
        same_clip = [[i for i in range(clips) if i % 2 == c] for c in (0, 1)]
        small, shares, theirs = lax.psum(
            (small, shares, theirs), "dp", axis_index_groups=same_clip
        )
    factor = 1.0 / math.sqrt(clips * frames * tiles * tokens)
    value_grad = jnp.where(x == 0, shares, theirs) * factor
    out_proj_grad = jnp.where(x == 0, theirs, shares) * factor
    scale_sum = small[256 : 256 + heads]
    return (
        mid_grad[None, None],
        value_grad,
        out_proj_grad,
        small[:depth] * factor,
        small[128 : 128 + depth] * factor,
        scale_sum * factor,
    )


def solution(mesh):
    in_specs = (
        P("dp", "frame", "tile", None, None),
        P("dp", "frame", "tile", None, None),
        P(),
        P(None, ("frame", "tile"), None),
        P(("frame", "tile"), None),
        P(),
        P(),
        P(),
    )
    out_specs = (
        P("dp", "frame", "tile", None, None),
        P(("frame", "tile"), None),
        P(("frame", "tile"), None),
        P(),
        P(),
        P(),
    )
    return jax.shard_map(local, mesh=mesh, in_specs=in_specs, out_specs=out_specs, check_vma=False)
```

```python
import functools
import math

import jax
import jax.numpy as jnp
from jax import lax
from jax.experimental import pallas as pl
from jax.experimental.pallas import tpu as pltpu
from jax.sharding import PartitionSpec as P

GROUPS = 32
EPS = 1e-05
SLOT = 16
BF = jnp.bfloat16
F32 = jnp.float32


def swap(x, axis):
    return lax.ppermute(x, axis, [(i, i ^ 1) for i in range(lax.axis_size(axis))])


def swap_both(x, axis, bit):
    sizes = (lax.axis_size("dp"), lax.axis_size(axis))
    pairs = [
        (i * sizes[1] + j, (i ^ 1) * sizes[1] + (j ^ bit))
        for i in range(sizes[0])
        for j in range(sizes[1])
    ]
    return lax.ppermute(x, ("dp", axis), pairs)


def round_up(value, unit):
    return -(-value // unit) * unit


def dot(a, b):
    return lax.dot_general(a, b, (((1,), (0,)), ((), ())), preferred_element_type=F32)


def dot_t(a, b):
    return lax.dot_general(a, b, (((1,), (1,)), ((), ())), preferred_element_type=F32)


def dot_rows(a, b):
    return lax.dot_general(a, b, (((0,), (0,)), ((), ())), preferred_element_type=F32)


def halves(x):
    high = x.astype(BF)
    return high, (x - high.astype(F32)).astype(BF)


def picker(rows, cols, depth, offset):
    row = lax.broadcasted_iota(jnp.int32, (rows, cols), 0)
    col = lax.broadcasted_iota(jnp.int32, (rows, cols), 1)
    return (col - row // depth == offset).astype(F32).astype(BF)


def spreader(rows, cols, depth, offset):
    row = lax.broadcasted_iota(jnp.int32, (rows, cols), 0)
    col = lax.broadcasted_iota(jnp.int32, (rows, cols), 1)
    return (row - col // depth == offset).astype(F32).astype(BF)


def head_sums(x, pick):
    high, low = halves(x)
    return dot(high, pick) + dot(low, pick)


def spread(x, both):
    high, low = halves(x)
    return dot(jnp.concatenate([high, low], axis=1), both)


def over_slots(x):
    step = SLOT
    while step < x.shape[1]:
        x = x + pltpu.roll(x, step, 1)
        step *= 2
    return x


def each(number, body):
    if number > 8:
        lax.fori_loop(0, number, lambda i, _: body(i), None)
    else:
        for i in range(number):
            body(i)


def pack_kernel(place, weights, cot, out):
    share, width = (weights.shape[0], cot.shape[1])
    frames = out.shape[0]
    count = cot.shape[0] // frames
    half = share // 2
    x = place[0]
    chosen = [
        jnp.where(x == 0, weights[:, pl.ds(c * width, width)], weights[:, pl.ds((2 + c) * width, width)])
        for c in (0, 1)
    ]
    for f in range(frames):
        start = (f // 2 % 2) * half
        rows = [cot[pl.ds(f * count, count), :], chosen[f % 2][start : start + half]]
        out[f] = jnp.concatenate(rows, axis=0)


def merge_kernel(place, mine, theirs, out):
    odd = place[4] % 2
    half = mine.shape[1]
    for owner in range(mine.shape[0]):
        first = jnp.where(odd == 0, mine[owner], theirs[owner])
        second = jnp.where(odd == 0, theirs[owner], mine[owner])
        out[owner] = jnp.concatenate([first, second], axis=0)


def taps_kernel(place, mine, theirs, out):
    odd = place[4] % 2
    share = out.shape[2]
    for owner in range(mine.shape[0]):
        first = jnp.where(odd == 0, mine[owner], theirs[owner])
        second = jnp.where(odd == 0, theirs[owner], mine[owner])
        block = jnp.concatenate([first, second], axis=0)
        for row in range(3):
            out[row, owner] = block[row * share : (row + 1) * share]


def join_kernel(place, *refs):
    pieces, out, sems = (refs[:-2], refs[-2], refs[-1])
    x, core, tile = (place[0], place[1], place[2])
    frames = out.shape[1]
    middle = frames // 2
    copies = []
    for dc in (0, 1):
        own_kind = 2 * x + (core ^ dc)
        other_kind = 2 * (x ^ 1) + (core ^ dc)
        targets = [
            out.at[own_kind, :, tile],
            out.at[own_kind, :, tile ^ 1],
            out.at[other_kind, :, tile],
            out.at[other_kind, pl.ds(0, middle), tile ^ 1],
            out.at[other_kind, pl.ds(middle, middle), tile ^ 1],
        ]
        for n, target in enumerate(targets):
            index = 5 * dc + n
            copies.append(pltpu.make_async_copy(pieces[index], target, sems.at[index]))
    for copy in copies:
        copy.start()
    for copy in copies:
        copy.wait()


def act_kernel(place, gain, *refs, cols, part):
    blocks, (acts, kept) = (refs[:-2], refs[-2:])
    half, width = blocks[0].shape
    tile, chosen = (place[2], place[3])
    choice = picker(width, part, 1, -part * chosen)
    per_group = width // GROUPS
    pick = picker(width, 128, per_group, 0)
    back = spreader(128, width, per_group, 0)

    def thirds(x):
        high, low = halves(x)
        return high, low, (x - high.astype(F32) - low.astype(F32)).astype(BF)

    totals, squares = ([], [])
    for frame in range(4):
        total, square = (0.0, 0.0)
        for dy in (0, 1):
            x = blocks[2 * frame + dy][...]
            start = pl.multiple_of((tile ^ dy) * half, half)
            kept[frame, pl.ds(start, half), :] = dot(x, choice).astype(BF)
            x = x.astype(F32)
            total = total + jnp.sum(x, axis=0, keepdims=True)
            square = square + jnp.sum(x * x, axis=0, keepdims=True)
        totals.append(total)
        squares.append(square)
    high, low, lowest = thirds(jnp.concatenate(totals + squares, axis=0))
    both = (dot(high, pick) + dot(low, pick) + dot(lowest, pick)) / (2 * half * per_group)
    mean = both[0:4]
    rstd = lax.rsqrt(both[4:8] - mean * mean + EPS)
    high, low, lowest = thirds(jnp.concatenate([mean, rstd], axis=0))
    both = dot(high, back) + dot(low, back) + dot(lowest, back)
    scales = both[4:8] * gain[...]
    for frame in range(4):
        acts[frame, pl.ds(0, cols), :] = jnp.zeros((cols, width), BF)
        acts[frame, pl.ds(cols + 2 * half, cols), :] = jnp.zeros((cols, width), BF)
        for dy in (0, 1):
            x = blocks[2 * frame + dy][...].astype(F32)
            zed = (x - both[frame : frame + 1]) * scales[frame : frame + 1]
            start = pl.multiple_of(cols + (tile ^ dy) * half, cols)
            acts[frame, pl.ds(start, half), :] = (zed / (1.0 + jnp.exp(-zed))).astype(BF)


def conv_kernel(place, weights, acts, kept, out, *, cols, part, blocks, count):
    x, core = (place[0], place[1])
    whole = kept.shape[1]
    half = whole // 2
    third = count // 3
    col = lax.broadcasted_iota(jnp.int32, (whole, part), 0) % cols
    for dx in (0, 1):
        mids = []
        for dc in (0, 1):
            frame = 2 * dc + dx
            taps = dot(acts[frame, pl.ds(0, whole), :], weights[0])
            taps += dot(acts[frame, pl.ds(cols, whole), :], weights[1])
            taps += dot(acts[frame, pl.ds(2 * cols, whole), :], weights[2])
            left = pltpu.roll(taps[:, :part], 1, 0)
            right = pltpu.roll(taps[:, 2 * part :], whole - 1, 0)
            pre = taps[:, part : 2 * part] + jnp.where(col > 0, left, 0.0)
            pre = pre + jnp.where(col < cols - 1, right, 0.0)
            mids.append((kept[frame].astype(F32) + pre).astype(BF))
        if blocks > 8:
            for dc in (0, 1):
                out[x ^ dx, dc] = mids[dc]
            continue
        for f in range(blocks):
            for t in (0, 1):
                start = t * half + f * count
                rows = [
                    jnp.concatenate(
                        [mid[start + third * j : start + third * (j + 1)] for j in range(3)], axis=1
                    )
                    for mid in mids
                ]
                index = ((x ^ dx) * blocks + f) * 2 + t
                out[index] = jnp.concatenate(rows, axis=0)


def attend_kernel(
    place, mid_in, cot_in, weights_in, qgain, kgain, scale,
    kept, sent, sums, d_raw, q_hat, k_hat, q_rstd, k_rstd, d_value,
    mid_s, cot_s, doubled, doubled_v, mixed_s, raw_s, probs_s, weights, sems,
    *, heads, count, padded, part,
):
    total, width = mid_s.shape
    frames = total // padded
    depth = width // heads
    lanes = scale.shape[-1]
    third = count // 3
    x, core, tile, plane = (place[0], place[1], place[2], place[4])
    copies = [
        pltpu.make_async_copy(weights_in.at[n], weights.at[n], sems.at[n]) for n in range(4)
    ]
    for copy in copies:
        copy.start()
    mid_s[...] = jnp.zeros_like(mid_s)
    cot_s[...] = jnp.zeros_like(cot_s)
    for z in range(frames // 2):
        for e in (0, 1):
            f = 2 * z + e
            blocks = [
                mid_in[(x * frames + 2 * z + c) * 2 + t, pl.ds((e ^ c) * third, third), :]
                for x in (0, 1)
                for c in (0, 1)
                for t in (0, 1)
            ]
            for j in range(3):
                piece = [b[:, j * part : (j + 1) * part] for b in blocks]
                start = f * padded + j * third
                mid_s[pl.ds(start, third), :] = jnp.concatenate(piece, axis=1).astype(F32)
            cot_s[pl.ds(f * padded, count), :] = cot_in[f, pl.ds(0, count), :].astype(F32)
    mid = mid_s[...].astype(BF)
    cot = cot_s[...].astype(BF)
    pick = picker(width, lanes, depth, 0)
    both = jnp.concatenate([spreader(lanes, width, depth, 0)] * 2, axis=0)

    def stats(vec):
        cent = vec - spread(head_sums(vec, pick) / depth, both)
        var = head_sums(cent * cent, pick) / depth
        rstd = lax.rsqrt(var + EPS)
        return cent * spread(rstd, both), rstd

    copies[0].wait()
    hat, rstd = stats(dot(mid, weights[0]))
    q_hat[...] = hat
    q_rstd[...] = rstd
    q_norm = hat * qgain[...]
    copies[1].wait()
    hat, rstd = stats(dot(mid, weights[1]))
    k_hat[...] = hat
    k_rstd[...] = rstd
    hat = hat * kgain[...]
    doubled[pl.ds(0, total), :] = hat
    doubled[pl.ds(total, total), :] = hat
    copies[2].wait()
    copies[3].wait()
    value = dot(mid, weights[2]).astype(BF).astype(F32)
    doubled_v[pl.ds(0, total), :] = value
    doubled_v[pl.ds(total, total), :] = value
    d_mixed = dot_t(cot, weights[3]).astype(BF).astype(F32)
    raw_s[...] = jnp.zeros_like(raw_s)
    probs_s[...] = jnp.zeros_like(probs_s)

    def logits(s):
        here = picker(width, lanes, depth, SLOT * s)
        raw_s[...] += head_sums(q_norm * doubled[pl.ds(s * padded, total), :], here)
        probs_s[...] += head_sums(d_mixed * doubled_v[pl.ds(s * padded, total), :], here)

    each(frames, logits)
    raw = raw_s[...] / math.sqrt(depth)
    expo = jnp.exp(raw * scale[...])
    probs = expo / over_slots(expo)
    probs_b = probs.astype(BF)
    d_probs = probs_s[...]
    d_logits = probs * (d_probs - over_slots(probs * d_probs))
    sums[...] = jnp.sum(d_logits * raw, axis=0, keepdims=True)
    d_raw[...] = d_logits * scale[...] / math.sqrt(depth)
    mixed_s[...] = jnp.zeros_like(mixed_s)
    doubled[...] = jnp.zeros_like(doubled)

    def mix(s):
        weight = dot(probs_b, spreader(lanes, width, depth, SLOT * s))
        mixed_s[...] += weight * doubled_v[pl.ds(s * padded, total), :]
        doubled[pl.ds(s * padded, total), :] += weight * d_mixed

    each(frames, mix)
    dv = (doubled[pl.ds(0, total), :] + doubled[pl.ds(total, total), :]).astype(BF)
    d_value[...] = dv
    rows = kept.shape[3]

    def store(kind, term):
        for z in range(frames // 2):
            for t in (0, 1):
                start = (4 * z + t) * rows
                first = term[start : start + rows]
                second = term[start + 2 * rows : start + 3 * rows]
                kept[x ^ kind, tile ^ t, plane ^ z] = jnp.where(core == 0, first, second)
                sent[x ^ kind, tile ^ t, plane ^ z] = jnp.where(core == 0, second, first)

    store(1, dot_rows(mixed_s[...].astype(BF), cot).astype(BF))
    store(0, dot_rows(mid, dv).astype(BF))


def slope_kernel(
    d_raw, q_hat, k_hat, qgain, kgain,
    d_qn, d_kn,
    doubled, doubled_acc,
    *, heads, padded,
):
    total, width = q_hat.shape
    depth = width // heads
    frames = total // padded
    lanes = d_raw.shape[-1]
    k_norm = k_hat[...] * kgain[...]
    doubled[pl.ds(0, total), :] = k_norm
    doubled[pl.ds(total, total), :] = k_norm
    q_norm = q_hat[...] * qgain[...]
    doubled_acc[...] = jnp.zeros_like(doubled_acc)
    d_qn[...] = jnp.zeros_like(d_qn)
    high, low = halves(d_raw[...])
    pair = jnp.concatenate([high, low], axis=1)

    def shift(s):
        one = spreader(lanes, width, depth, SLOT * s)
        weight = dot(pair, jnp.concatenate([one, one], axis=0))
        d_qn[...] += weight * doubled[pl.ds(s * padded, total), :]
        doubled_acc[pl.ds(s * padded, total), :] += weight * q_norm

    each(frames, shift)
    d_kn[...] = doubled_acc[pl.ds(0, total), :] + doubled_acc[pl.ds(total, total), :]


def back_kernel(
    d_qn, d_kn, q_hat, k_hat, q_rstd, k_rstd, d_value, weights_in, qgain, kgain, scale_sums,
    d_mid,
    weights, sems,
    *, heads, count, padded,
):
    total, width = q_hat.shape
    depth = width // heads
    frames = total // padded
    lanes = scale_sums.shape[-1]
    copies = [
        pltpu.make_async_copy(weights_in.at[n], weights.at[n], sems.at[n]) for n in range(3)
    ]
    for copy in copies:
        copy.start()
    pick = picker(width, lanes, depth, 0)
    both = jnp.concatenate([spreader(lanes, width, depth, 0)] * 2, axis=0)

    def back(dhat, hat, rstd):
        first = spread(head_sums(dhat, pick) / depth, both)
        second = spread(head_sums(dhat * hat, pick) / depth, both)
        return (spread(rstd, both) * (dhat - first - hat * second)).astype(BF)

    d_query = back(d_qn[...] * qgain[...], q_hat[...], q_rstd[...])
    d_key = back(d_kn[...] * kgain[...], k_hat[...], k_rstd[...])
    for copy in copies:
        copy.wait()
    out = dot_t(d_query, weights[0])
    out += dot_t(d_key, weights[1])
    out += dot_t(d_value[...], weights[2])

    row = lax.broadcasted_iota(jnp.int32, (width, 128), 0)
    col = lax.broadcasted_iota(jnp.int32, (width, 128), 1)
    fold = (row % depth == col).astype(F32)

    def folded(d_norm, hat):
        sums = jnp.sum(d_norm * hat, axis=0, keepdims=True)
        sums = jnp.broadcast_to(sums, (8, width))
        return jnp.dot(sums, fold, precision=lax.Precision.HIGHEST, preferred_element_type=F32)[0:1]

    by_head = over_slots(jnp.broadcast_to(scale_sums[...], (8, lanes)))[0:1, :128]
    small = [folded(d_qn[...], q_hat[...]), folded(d_kn[...], k_hat[...]), by_head]
    small.append(jnp.zeros((1, width - 384), F32))
    small = jnp.concatenate(small, axis=1)
    high, low = halves(small)
    lowest = (small - high.astype(F32) - low.astype(F32)).astype(BF)
    spare = [high.astype(F32), low.astype(F32), lowest.astype(F32)]
    if padded - count > 3:
        spare.append(jnp.zeros((padded - count - 3, width), F32))
    spare = jnp.concatenate(spare, axis=0)
    for f in range(frames):
        tokens = out[f * padded : f * padded + count]
        d_mid[f] = jnp.concatenate([tokens, spare], axis=0).astype(BF)


def call(kernel, mebibytes, outs, scratch, *args, apart=(), outs_apart=False, sems=0):
    smem = pl.BlockSpec(memory_space=pltpu.SMEM)
    vmem = pl.BlockSpec(memory_space=pltpu.VMEM)
    apart_spec = pl.BlockSpec(memory_space=pl.ANY)
    in_specs = [smem if arg.dtype == jnp.int32 else vmem for arg in args]
    for index in apart:
        in_specs[index] = apart_spec
    shapes = [pltpu.VMEM(shape, dtype) for shape, dtype in scratch]
    if sems > 0:
        shapes.append(pltpu.SemaphoreType.DMA((sems,)))
    return pl.pallas_call(
        kernel,
        out_shape=[jax.ShapeDtypeStruct(shape, dtype) for shape, dtype in outs],
        in_specs=in_specs,
        out_specs=[apart_spec if outs_apart else vmem] * len(outs),
        scratch_shapes=shapes,
        compiler_params=pltpu.CompilerParams(vmem_limit_bytes=mebibytes << 20),
    )(*args)


def local(
    clip_input, cotangent, norm_gain, conv_weight, attn_weight, query_gain, key_gain, logit_scale
):
    source = clip_input[0, 0]
    cot = cotangent[0, 0]
    rows, cols, width = source.shape
    heads = logit_scale.shape[0]
    depth = width // heads
    tokens = rows * cols
    clips, frames, tiles = (lax.axis_size(name) for name in ("dp", "frame", "tile"))
    square = ("frame", "tile")
    ranks = frames * tiles
    share = conv_weight.shape[1]
    count = tokens // frames
    third = count // 3
    part = width // 8
    x = lax.axis_index("dp") % 2
    core = lax.axis_index("frame") % 2
    tile = lax.axis_index("tile")
    plane = lax.axis_index("frame") // 2
    place = jnp.stack([x, core, tile, 4 * x + 2 * core + tile, plane]).astype(jnp.int32)
    flat = source.reshape(tokens, width)

    (packed,) = call(
        pack_kernel,
        12,
        [((frames, count + share // 2, width), BF)],
        [],
        place,
        attn_weight,
        cot.reshape(tokens, width),
    )
    packed = lax.all_to_all(packed, "frame", 0, 0, tiled=True)

    half = tokens // 2
    along_x = swap(flat, "dp")
    along_y = swap(flat, "tile")
    across = jnp.concatenate([swap(along_x[:half], "tile"), swap(along_y[half:], "dp")])
    pieces = [flat, along_y, along_x, across]
    pieces += [swap(piece, "frame") for piece in pieces]

    planes = [(i, i ^ 2) for i in range(frames)]
    lines = 3 * share // 2
    mine = lax.dynamic_slice_in_dim(conv_weight, x * (width // 2), width // 2, axis=2)
    mine = mine.reshape(3, 3, share, 4, part).transpose(3, 0, 2, 1, 4)
    mine = mine.reshape(4, 2, lines, 3 * part).transpose(1, 0, 2, 3)
    mine = jnp.broadcast_to(mine[None], (frames // 4,) + mine.shape)
    mine = mine.reshape(ranks, lines, 3 * part)
    mine, packed, pieces = lax.optimization_barrier((mine, packed, pieces))
    conv_half = lax.all_to_all(mine, square, 0, 0, tiled=True)
    own = packed[:, count:]
    own_other = lax.ppermute(own, "frame", planes)
    conv_other = lax.ppermute(conv_half, "frame", planes)
    acts, kept = call(
        functools.partial(act_kernel, cols=cols, part=part),
        20,
        [((4, tiles * tokens + 2 * cols, width), BF), ((4, tiles * tokens, part), BF)],
        [],
        place,
        norm_gain[None],
        *pieces,
    )
    (conv_full,) = call(
        taps_kernel, 12, [((3, ranks, share, 3 * part), BF)], [], place, conv_half, conv_other
    )
    conv_full = conv_full.reshape(3, width, 3 * part)
    (own,) = call(merge_kernel, 8, [((frames, share, width), BF)], [], place, own, own_other)
    by_tile = swap(own, "tile")
    by_clip = swap(own, "dp")
    blocked = (2 * ranks, 2 * third, 3 * part)
    plain = (2, 2, tiles * tokens, part)
    (mid,) = call(
        functools.partial(conv_kernel, cols=cols, part=part, blocks=frames, count=count),
        16,
        [(plain if frames > 8 else blocked, BF)],
        [],
        place,
        conv_full,
        acts,
        kept,
    )
    if frames > 8:
        mid = mid.reshape(2, 2, tiles, frames, 3, third, part).transpose(0, 3, 2, 1, 5, 4, 6)
        mid = mid.reshape(blocked)
    mid, by_tile, by_clip = lax.optimization_barrier((mid, by_tile, by_clip))
    groups = None
    if clips > 2:
        groups = [[2 * ranks * g + i for i in range(2 * ranks)] for g in range(clips // 2)]
    mid = lax.all_to_all(mid, ("dp",) + square, 0, 0, axis_index_groups=groups, tiled=True)

    middle = frames // 2
    parts = [own, by_tile, by_clip, swap(by_clip[:middle], "tile"), swap(by_tile[middle:], "dp")]
    parts += [swap(piece, "frame") for piece in parts]
    (attn_full,) = call(
        join_kernel,
        8,
        [((4, frames, tiles, share, width), BF)],
        [],
        place,
        *parts,
        apart=range(1, 11),
        outs_apart=True,
        sems=10,
    )
    attn_full = attn_full.reshape(4, width, width)

    lanes = frames * SLOT
    padded = round_up(count + 3, 8)
    total = frames * padded
    scale = jnp.tile(jnp.pad(logit_scale, (0, SLOT - heads)), frames)[None]
    qgain = jnp.tile(query_gain, heads)[None]
    kgain = jnp.tile(key_gain, heads)[None]
    full = (total, width)
    double = (2 * total, width)
    narrow = (total, lanes)
    kept, sent, scale_sums, d_raw, q_hat, k_hat, q_rstd, k_rstd, d_value = call(
        functools.partial(attend_kernel, heads=heads, count=count, padded=padded, part=part),
        32,
        [
            ((2, 2, frames // 2, share, width), BF),
            ((2, 2, frames // 2, share, width), BF),
            ((1, lanes), F32), (narrow, F32),
            (full, F32), (full, F32), (narrow, F32), (narrow, F32), (full, BF),
        ],
        [
            (full, F32), (full, F32), (double, F32), (double, F32), (full, F32),
            (narrow, F32), (narrow, F32), ((4, width, width), BF),
        ],
        place, mid, packed, attn_full, qgain, kgain, scale,
        apart=(3,), sems=4,
    )
    d_qn, d_kn = call(
        functools.partial(slope_kernel, heads=heads, padded=padded),
        16,
        [(full, F32), (full, F32)],
        [(double, F32), (double, F32)],
        d_raw, q_hat, k_hat, qgain, kgain,
    )

    def add(mine, theirs):
        return (mine.astype(F32) + theirs.astype(F32)).astype(BF)

    shares = add(kept, swap(sent, "frame"))
    shares, d_qn = lax.optimization_barrier((shares, d_qn))
    (d_mid,) = call(
        functools.partial(back_kernel, heads=heads, count=count, padded=padded),
        16,
        [((frames, padded, width), BF)],
        [((3, width, width), BF)],
        d_qn, d_kn, q_hat, k_hat, q_rstd, k_rstd, d_value, attn_full, qgain, kgain, scale_sums,
        apart=(7,), sems=3,
    )
    d_back = lax.all_to_all(d_mid, "frame", 0, 0, tiled=True)
    theirs, _ = lax.optimization_barrier((swap(shares[1], "dp"), d_mid))
    shares = add(shares[0], theirs)
    shares = add(shares[0], swap(shares[1], "tile"))
    shares, d_back = lax.optimization_barrier((shares, d_back))
    step = frames // 4
    while step > 1:
        pairs = [(i, i ^ (2 * step)) for i in range(frames)]
        shares = add(shares[:step], lax.ppermute(shares[step:], "frame", pairs))
        step //= 2
    small = jnp.sum(d_back[:, count : count + 3].astype(F32), axis=(0, 1))
    d_back = d_back[:, :count].reshape(rows, cols, width)
    mid_grad = (cot.astype(F32) + d_back.astype(F32)).astype(BF)

    small = small + swap(small, "tile")
    small, _ = lax.optimization_barrier((small, shares))
    by_plane = lax.ppermute(shares[1], "frame", planes)
    by_clip = swap(shares[0], "dp")
    by_both = swap_both(shares[1], "frame", 2)
    shares = shares[0].astype(F32) + by_plane.astype(F32)
    theirs = by_clip.astype(F32) + by_both.astype(F32)
    small = small + swap(small, "dp")
    if clips > 2:
        same_clip = [[i for i in range(clips) if i % 2 == c] for c in (0, 1)]
        small, shares, theirs = lax.psum(
            (small, shares, theirs), "dp", axis_index_groups=same_clip
        )
    factor = 1.0 / math.sqrt(clips * frames * tiles * tokens)
    value_grad = jnp.where(x == 0, shares, theirs) * factor
    out_proj_grad = jnp.where(x == 0, theirs, shares) * factor
    scale_sum = small[256 : 256 + heads]
    return (
        mid_grad[None, None],
        value_grad,
        out_proj_grad,
        small[:depth] * factor,
        small[128 : 128 + depth] * factor,
        scale_sum * factor,
    )


def solution(mesh):
    in_specs = (
        P("dp", "frame", "tile", None, None),
        P("dp", "frame", "tile", None, None),
        P(),
        P(None, ("frame", "tile"), None),
        P(("frame", "tile"), None),
        P(),
        P(),
        P(),
    )
    out_specs = (
        P("dp", "frame", "tile", None, None),
        P(("frame", "tile"), None),
        P(("frame", "tile"), None),
        P(),
        P(),
        P(),
    )
    return jax.shard_map(local, mesh=mesh, in_specs=in_specs, out_specs=out_specs, check_vma=False)
```
